128 devices in a mesh: gx: 16 (over z, x), gy: 8 (over y, core).
Axes of the slice: x: 4, y: 4, z: 4, core: 2. Of those that a mesh axis runs over, the one named last changes fastest.
Arguments:
- theta: float32 [80, 1024, 1024], P(None, 'gx', 'gy'), may hold values from -6 to 6
- wind_u: float32 [80, 1024, 1024], P(None, 'gx', 'gy'), may hold values from -1 to 1
- wind_v: float32 [80, 1024, 1024], P(None, 'gx', 'gy'), may hold values from -1 to 1
- level_set: float32 [16, 8, 16, 128, 128], P('gx', 'gy'), may hold values from -6 to 6
- fuel_load: float32 [16, 8, 16, 128, 128], P('gx', 'gy'), may hold values from 0.5 to 1.5
- spread_base: float32 [16, 8, 16, 128, 128], P('gx', 'gy'), may hold values from 0.3 to 3
- tile_owner: int32 [16, 8, 16], P('gx', 'gy'), may hold values from 0 to 15, as said below
- tile_place: int32 [16, 8, 16], P('gx', 'gy'), may hold values from 0 to 511, as said below
Outputs:
- theta_next: float32 [80, 1024, 1024], P(None, 'gx', 'gy')
- level_next: float32 [16, 8, 16, 128, 128], P('gx', 'gy')
- fuel_next: float32 [16, 8, 16, 128, 128], P('gx', 'gy')
The draws below stay inside these ranges and needn't reach their ends.
Inputs may be any that keep to these rules, and one draw needn't show every extreme that they name: Every tile of device (i, j) lies in the block of a device (tile_owner, j) of the same gy index; at most 2 tiles of one device lie in one owner's block, and in every draw some owner of each gy index holds exactly 2 tiles from every device of that index. `tile_place`: no two computed tiles have the same owner and place.
All inputs are finite; a program needn't handle non-finite values.
Results may differ from the reference program's by a relative error of at most 0.0003.
Values sent between devices are 32-bit elements; how exact they have to be, the bound alone decides.
No kernel may reach another device: no remote copies, remote signals or barrier semaphores. Data moves between devices by JAX's collectives and lax.ppermute only.
A program may use at most 128 MiB of HBM per device.

```python
import math
import jax
import jax.numpy as jnp
from jax import lax

CX = 64
CY = 128
LZ = 80
TA = 4
R = 32
KSUB = 6
CAP = 2
TPD = 16
S = 128
FIRE_X = 16
FIRE_Y = 8
NXA = 1024
NYA = 1024


def tile_lists(key):
    cycle = NXA // CX
    rows = NYA // CY
    places_count = CX // TA * (CY // TA)
    owner_key = jax.random.fold_in(key, 101)
    hot_key = jax.random.fold_in(key, 102)
    place_key = jax.random.fold_in(key, 103)
    pool = jnp.repeat(jnp.arange(1, cycle, dtype=jnp.int32), CAP)
    owner_keys = jax.random.split(owner_key, cycle * rows)

    def pick(single):
        return jax.random.permutation(single, pool)[:TPD - CAP]
    others = jax.vmap(pick)(owner_keys).reshape(cycle, rows, TPD - CAP)
    first = jnp.zeros((cycle, rows, CAP), jnp.int32)
    shifted = jnp.concatenate([first, others], axis=2)
    hottest = jax.random.randint(hot_key, (rows,), 0, cycle)
    owners = ((shifted + hottest[None, :, None]) % cycle).astype(jnp.int32)
    same_owner = owners[:, :, :, None] == owners[:, :, None, :]
    earlier = jnp.arange(TPD)[None, :] < jnp.arange(TPD)[:, None]
    slot_rank = jnp.sum(jnp.logical_and(same_owner, earlier[None, None]), axis=3).astype(jnp.int32)
    place_keys = jax.random.split(place_key, cycle * rows)
    orders = jax.vmap(lambda single: jax.random.permutation(single, places_count))(place_keys).reshape(cycle, rows, places_count)
    source = jnp.arange(cycle, dtype=jnp.int32)[:, None, None]
    row_index = jnp.arange(rows, dtype=jnp.int32)[None, :, None]
    places = orders[owners, row_index, source * CAP + slot_rank].astype(jnp.int32)
    return (owners, places)


def draw_tile_owner(key, part):
    return tile_lists(key)[0]


def draw_tile_place(key, part):
    return tile_lists(key)[1]


def level_of(own_key, shape, cuts, low, top_value):
    def one(position, shards_of):
        heights = jax.random.uniform(jax.random.fold_in(jax.random.fold_in(own_key, 6), position), (shards_of,), jnp.float32, low / len(cuts), top_value / len(cuts))
        return jnp.repeat(jnp.exp(heights), shape[position] // shards_of).reshape((-1,) + (1,) * (len(shape) - position - 1))

    loudness = one(*cuts[0])
    for cut in cuts[1:]:
        loudness = loudness * one(*cut)
    return loudness


def centred(key, dims, deviation, most, cuts=(), kind=jnp.bfloat16):
    values = deviation * jax.random.normal(key, dims, jnp.float32)
    if cuts:
        values = values * level_of(key, dims, cuts, -0.22, 0.18)
    return jnp.clip(values, -most, most).astype(kind)


def setup_inputs(seed: int = 0) -> dict:
    key_of = jax.random.split(jax.random.key(seed), 9)
    theta = centred(key_of[0], (LZ, NXA, NYA), 1.0, 6.0, ((1, 16), (2, 8)), jnp.float32)
    wind_u = jnp.clip(jax.random.uniform(key_of[1], (LZ, NXA, NYA), jnp.float32, -1.0, 1.0) * level_of(key_of[1], (LZ, NXA, NYA), ((1, 16), (2, 8)), -0.4, 0.0), -1.0, 1.0)
    wind_v = jnp.clip(jax.random.uniform(key_of[2], (LZ, NXA, NYA), jnp.float32, -1.0, 1.0) * level_of(key_of[2], (LZ, NXA, NYA), ((1, 16), (2, 8)), -0.4, 0.0), -1.0, 1.0)
    level_set = centred(key_of[3], (FIRE_X, FIRE_Y, TPD, S, S), 1.0, 6.0, ((0, 16), (1, 8)), jnp.float32)
    fuel_load = jnp.clip(0.5 + 1.0 * jax.random.uniform(key_of[4], (FIRE_X, FIRE_Y, TPD, S, S), jnp.float32) ** level_of(key_of[4], (FIRE_X, FIRE_Y, TPD, S, S), ((0, 16), (1, 8)), -0.2, 0.2), 0.5, 1.5)
    spread_base = jnp.clip(jnp.exp(math.log(3.0) - 2.3025851 * jax.random.uniform(key_of[5], (FIRE_X, FIRE_Y, TPD, S, S), jnp.float32) ** level_of(key_of[5], (FIRE_X, FIRE_Y, TPD, S, S), ((0, 16), (1, 8)), -0.2, 0.2)), 0.3, 3.0)
    tile_owner = draw_tile_owner(jax.random.fold_in(key_of[8], 71), 0)
    tile_place = draw_tile_place(jax.random.fold_in(key_of[8], 71), 0)
    return {"theta": theta, "wind_u": wind_u, "wind_v": wind_v, "level_set": level_set, "fuel_load": fuel_load, "spread_base": spread_base, "tile_owner": tile_owner, "tile_place": tile_place}


time_step = 0.03
diffusion = 0.15
burn_rate = 0.15
sharpness = 2.0
regular = 0.01
courant = 0.4
heat_gain = 2.0

def interp_table():
    where_fine = (jnp.arange(S, dtype=jnp.float32) + 0.5) / R + 0.5
    columns = jnp.arange(TA + 2, dtype=jnp.float32)
    return jnp.maximum(0.0, 1.0 - jnp.abs(where_fine[:, None] - columns[None, :]))

def average_table():
    block_of = jnp.arange(S, dtype=jnp.int32) // R
    coarse = jnp.arange(TA, dtype=jnp.int32)
    return jnp.where(coarse[:, None] == block_of[None, :], 1.0 / R, 0.0).astype(jnp.float32)

def fire_tile(level, fuel, base, wind, average):
    heat = jnp.zeros_like(fuel)
    for substep in range(KSUB):
        padded = jnp.pad(level, 1, mode='edge')
        grad_x = 0.5 * (padded[2:, 1:-1] - padded[:-2, 1:-1])
        grad_y = 0.5 * (padded[1:-1, 2:] - padded[1:-1, :-2])
        laplace = padded[2:, 1:-1] + padded[:-2, 1:-1] + padded[1:-1, 2:] + padded[1:-1, :-2] - 4.0 * level
        length = jnp.sqrt(grad_x * grad_x + grad_y * grad_y + regular)
        along = (wind[0] * grad_x + wind[1] * grad_y) / length
        speed = base * jnp.maximum(1.0 + along, 0.0)
        level = level - time_step * speed * length + diffusion * laplace
        used = burn_rate * fuel * jax.nn.sigmoid(-sharpness * level)
        fuel = fuel - used
        heat = heat + used
    flux = jnp.dot(jnp.dot(average, heat, precision=lax.Precision.HIGHEST), average.T, precision=lax.Precision.HIGHEST)
    return (level, fuel, flux)

def reference(theta, wind_u, wind_v, level_set, fuel_load, spread_base, tile_owner, tile_place):
    cycle = NXA // CX
    rows = NYA // CY
    tiles_y = CY // TA
    interp = interp_table()
    average = average_table()
    surface = jnp.pad(jnp.stack([wind_u[0], wind_v[0]]), ((0, 0), (1, 1), (1, 1)))
    row_index = jnp.arange(rows, dtype=jnp.int32)[None, :, None]
    start_x = (tile_owner * CX + tile_place // tiles_y * TA).astype(jnp.int32)
    start_y = (row_index * CY + tile_place % tiles_y * TA).astype(jnp.int32)
    start_x = start_x.reshape(cycle * rows, TPD)
    start_y = start_y.reshape(cycle * rows, TPD)

    def one_device(items):
        level, fuel, base, first_x, first_y = items

        def cut(left, bottom):
            return lax.dynamic_slice(surface, (jnp.int32(0), left.astype(jnp.int32), bottom.astype(jnp.int32)), (2, TA + 2, TA + 2))
        patches = jax.vmap(cut)(first_x, first_y)
        winds = jnp.einsum('ak,tckl,bl->tcab', interp, patches, interp, precision=lax.Precision.HIGHEST)
        return jax.vmap(lambda a, b, c, d: fire_tile(a, b, c, d, average))(level, fuel, base, winds)
    shaped = (level_set.reshape(cycle * rows, TPD, S, S), fuel_load.reshape(cycle * rows, TPD, S, S), spread_base.reshape(cycle * rows, TPD, S, S), start_x, start_y)
    level_out, fuel_out, fluxes = lax.map(one_device, shaped)
    offsets = jnp.arange(TA, dtype=jnp.int32)
    index_x = start_x.reshape(-1)[:, None, None] + offsets[None, :, None]
    index_y = start_y.reshape(-1)[:, None, None] + offsets[None, None, :]
    index_x = jnp.broadcast_to(index_x, (cycle * rows * TPD, TA, TA))
    index_y = jnp.broadcast_to(index_y, (cycle * rows * TPD, TA, TA))
    field = jnp.zeros((NXA, NYA), jnp.float32).at[index_x, index_y].add(fluxes.reshape(-1, TA, TA))
    padded = jnp.pad(theta, ((0, 0), (1, 1), (1, 1)))
    centre = theta
    advect = courant * (jnp.maximum(wind_u, 0.0) * (centre - padded[:, :-2, 1:-1]) + jnp.minimum(wind_u, 0.0) * (padded[:, 2:, 1:-1] - centre) + jnp.maximum(wind_v, 0.0) * (centre - padded[:, 1:-1, :-2]) + jnp.minimum(wind_v, 0.0) * (padded[:, 1:-1, 2:] - centre))
    profile = jnp.exp(-(jnp.arange(LZ, dtype=jnp.float32) + 0.5) / (LZ / 4.0))
    theta_next = theta - advect + heat_gain * field[None, :, :] * profile[:, None, None]
    shape_out = (cycle, rows, TPD, S, S)
    return (theta_next, level_out.reshape(shape_out), fuel_out.reshape(shape_out))
```

```python
import functools

import jax
import jax.numpy as jnp
from jax import lax
from jax.experimental import pallas as pl
from jax.experimental.pallas import tpu as pltpu
from jax.sharding import PartitionSpec as P

LZ = 80
TA = 4
R = 32
KSUB = 6
CAP = 2
TPD = 16
S = 128
CX = 64
CY = 128
ROWS = S // 8
BLOCK = 2 * CX + 8
RIM = 8

time_step = 0.03
diffusion = 0.15
burn_rate = 0.15
regular = 0.01
courant = 0.4
heat_gain = 2.0

F32 = jnp.float32


def iota(dim, shape=(8, 128)):
    return lax.broadcasted_iota(jnp.int32, shape, dim)


def wind_edge_kernel(u_ref, v_ref, up_ref, down_ref):
    columns = jnp.transpose(jnp.concatenate([u_ref[0], v_ref[0]], axis=0))
    row = iota(0)
    last = jnp.broadcast_to(columns[CY - 1 : CY], (8, 128))
    first = jnp.broadcast_to(columns[0:1], (8, 128))
    up_ref[...] = jnp.where(row == 0, last, 0.0)
    down_ref[...] = jnp.where(row == TA + 1, first, 0.0)


def wind_edges(wind_u, wind_v):
    surface = pl.BlockSpec((1, CX, CY), lambda i: (0, 0, 0))
    edge = pl.BlockSpec((8, 128), lambda i: (0, 0))
    return pl.pallas_call(
        wind_edge_kernel,
        grid=(1,),
        in_specs=[surface, surface],
        out_specs=[edge, edge],
        out_shape=[jax.ShapeDtypeStruct((8, 128), F32)] * 2,
        name="wind_edges",
    )(wind_u, wind_v)


def pack_kernel(u_ref, v_ref, low_ref, high_ref, out_ref):
    block = jnp.concatenate([u_ref[0], v_ref[0], low_ref[...] + high_ref[...]], axis=0)
    for peer in range(out_ref.shape[0]):
        out_ref[peer] = block


def pack_winds(wind_u, wind_v, low, high, peers):
    surface = pl.BlockSpec((1, CX, CY), lambda i: (0, 0, 0))
    edge = pl.BlockSpec((8, 128), lambda i: (0, 0))
    return pl.pallas_call(
        pack_kernel,
        grid=(1,),
        in_specs=[surface, surface, edge, edge],
        out_specs=pl.BlockSpec((peers, BLOCK, 128), lambda i: (0, 0, 0)),
        out_shape=jax.ShapeDtypeStruct((peers, BLOCK, 128), F32),
        name="pack_winds",
    )(wind_u, wind_v, low, high)


def theta_edge_kernel(levels, theta_ref, west_ref, east_ref, south_ref, north_ref):
    step = pl.program_id(0)

    @pl.when(step == 0)
    def _():
        south_ref[...] = jnp.zeros_like(south_ref)
        north_ref[...] = jnp.zeros_like(north_ref)

    lane = iota(1, (CX, 128))
    south, north = south_ref[...], north_ref[...]
    for k in range(levels):
        z = step * levels + k
        cells = theta_ref[k]
        west_ref[k : k + 1] = cells[0:1]
        east_ref[k : k + 1] = cells[CX - 1 : CX]
        south = jnp.where(lane == z, pltpu.roll(cells, z, 1), south)
        north = jnp.where(lane == z, pltpu.roll(cells, z + 1, 1), north)
    south_ref[...] = south
    north_ref[...] = north


def theta_edges(theta):
    levels = 16
    row = pl.BlockSpec((levels, 128), lambda i: (i, 0))
    column = pl.BlockSpec((CX, 128), lambda i: (0, 0))
    rows = jax.ShapeDtypeStruct((LZ, 128), F32)
    columns = jax.ShapeDtypeStruct((CX, 128), F32)
    return pl.pallas_call(
        functools.partial(theta_edge_kernel, levels),
        grid=(LZ // levels,),
        in_specs=[pl.BlockSpec((levels, CX, CY), lambda i: (i, 0, 0))],
        out_specs=[row, row, column, column],
        out_shape=[rows, rows, columns, columns],
        name="theta_edges",
        cost_estimate=pl.CostEstimate(flops=4_000_000, bytes_accessed=2_800_000, transcendentals=0),
    )(theta)


def advect_kernel(levels, theta_ref, u_ref, v_ref, west_ref, east_ref, south_ref, north_ref, out_ref):
    step = pl.program_id(0)
    lane = iota(1, (CX, 128))
    row = iota(0, (CX, 128))
    for k in range(levels):
        z = step * levels + k
        t = theta_ref[k]
        u = u_ref[k]
        v = v_ref[k]
        west = jnp.where(row == 0, west_ref[k : k + 1], pltpu.roll(t, 1, 0))
        east = jnp.where(row == CX - 1, east_ref[k : k + 1], pltpu.roll(t, CX - 1, 0))
        back = lax.rem(128 - z, 128)
        south = jnp.where(lane == 0, pltpu.roll(south_ref[...], back, 1), pltpu.roll(t, 1, 1))
        north = jnp.where(lane == CY - 1, pltpu.roll(north_ref[...], 127 - z, 1), pltpu.roll(t, CY - 1, 1))
        change = (
            jnp.maximum(u, 0.0) * (t - west)
            + jnp.minimum(u, 0.0) * (east - t)
            + jnp.maximum(v, 0.0) * (t - south)
            + jnp.minimum(v, 0.0) * (north - t)
        )
        out_ref[k] = t - courant * change


def advect(theta, wind_u, wind_v, west, east, south, north):
    levels = 8
    cells = pl.BlockSpec((levels, CX, CY), lambda i: (i, 0, 0))
    row = pl.BlockSpec((levels, 128), lambda i: (i, 0))
    column = pl.BlockSpec((CX, 128), lambda i: (0, 0))
    return pl.pallas_call(
        functools.partial(advect_kernel, levels),
        grid=(LZ // levels,),
        in_specs=[cells, cells, cells, row, row, column, column],
        out_specs=cells,
        out_shape=jax.ShapeDtypeStruct((LZ, CX, CY), F32),
        name="advect",
        cost_estimate=pl.CostEstimate(flops=14_000_000, bytes_accessed=10_500_000, transcendentals=0),
    )(theta, wind_u, wind_v, west, east, south, north)


def fire_kernel(
    peers, owner_ref, place_ref, winds_ref, level_ref, fuel_ref, base_ref,
    level_out, fuel_out, outbox, surface, edges, wind, count,
):
    step = pl.program_id(0)
    lane = iota(1)
    row = iota(0)

    @pl.when(step == 0)
    def _():
        for c in range(2):
            surface[c, 0:RIM] = jnp.zeros((RIM, 128), F32)
            surface[c, RIM + peers * CX :] = jnp.zeros((RIM, 128), F32)
            edges[c, 0:RIM] = jnp.zeros((RIM, 128), F32)
            edges[c, RIM + peers * CX :] = jnp.zeros((RIM, 128), F32)
        for d in range(peers):
            count[d] = 0
            turned = jnp.transpose(
                jnp.concatenate([winds_ref[d, 2 * CX :], jnp.zeros((120, 128), F32)], axis=0)
            )
            for c in range(2):
                surface[c, RIM + d * CX : RIM + (d + 1) * CX] = winds_ref[d, c * CX : (c + 1) * CX]
                edges[c, RIM + d * CX : RIM + (d + 1) * CX] = turned[c * CX : (c + 1) * CX]
        for d in range(peers * CAP):
            outbox[d] = jnp.where(row < TA, 0.0, -1.0)

    owner = owner_ref[step]
    place = place_ref[step]
    tiles_y = CY // TA
    x_own = place // tiles_y * TA
    y_own = lax.rem(place, tiles_y) * TA
    first = owner * CX + x_own + (RIM - 1)

    low_row = (row + 1) // 2
    low_lane = (lane + R // 2) // R
    part_row = jnp.where(row % 2 == 0, 0.5, 0.0) + 0.5 / R
    part_lane = (lane.astype(F32) + 0.5) / R + 0.5 - low_lane.astype(F32)
    outside = jnp.logical_or(
        jnp.logical_and(lane == 0, y_own == 0), jnp.logical_and(lane == TA + 1, y_own == CY - TA)
    )
    back = lax.rem(CY + 1 - y_own, CY)
    for c in range(2):
        patch = pltpu.roll(surface[c, pl.ds(first, 8), :], back, 1)
        patch = jnp.where(outside, edges[c, pl.ds(first, 8), :], patch)
        left = jnp.take_along_axis(patch, low_lane, axis=1)
        right = jnp.take_along_axis(patch, low_lane + 1, axis=1)
        fine = left + (right - left) * part_lane
        below = jnp.take_along_axis(fine, low_row, axis=0)
        above = jnp.take_along_axis(fine, low_row + 1, axis=0)
        rise = above - below
        begin = below + rise * part_row
        slope = rise * (1.0 / R)
        for k in range(ROWS):
            wind[c, k] = begin + slope * float(k)

    level = [level_ref[0, pl.ds(k, 8, stride=ROWS), :] for k in range(ROWS)]
    fuel = [fuel_ref[0, pl.ds(k, 8, stride=ROWS), :] for k in range(ROWS)]
    heat = sum(fuel[1:], fuel[0])
    rate = [base_ref[0, pl.ds(k, 8, stride=ROWS), :] * (0.5 * time_step) for k in range(ROWS)]
    for _ in range(KSUB):
        before = jnp.where(row == 0, level[0], pltpu.roll(level[-1], 1, 0))
        after = jnp.where(row == 7, level[-1], pltpu.roll(level[0], 7, 0))
        rimmed = [before, *level, after]
        new = []
        for k in range(ROWS):
            cell = rimmed[k + 1]
            west, east = rimmed[k], rimmed[k + 2]
            south = jnp.where(lane == 0, cell, pltpu.roll(cell, 1, 1))
            north = jnp.where(lane == S - 1, cell, pltpu.roll(cell, S - 1, 1))
            dx = east - west
            dy = north - south
            square = dx * dx + dy * dy + 4.0 * regular
            length = square * lax.rsqrt(square)
            move = jnp.maximum(length + (wind[0, k] * dx + wind[1, k] * dy), 0.0)
            around = (east + west) + (north + south)
            cell = cell * (1.0 - 4.0 * diffusion) + around * diffusion - rate[k] * move
            fuel[k] = fuel[k] * ((1.0 - 0.5 * burn_rate) + (0.5 * burn_rate) * jnp.tanh(cell))
            new.append(cell)
        level = new
    for k in range(ROWS):
        level_out[0, pl.ds(k, 8, stride=ROWS), :] = level[k]
        fuel_out[0, pl.ds(k, 8, stride=ROWS), :] = fuel[k]
    heat = (heat - sum(fuel[1:], fuel[0])) * (1.0 / (R * R))
    heat = heat + pltpu.roll(heat, 7, 0)

    message = jnp.where(row < TA, 0.0, (x_own + row - TA).astype(F32))
    rows = jnp.take_along_axis(heat, jnp.minimum(2 * row, 7), axis=0)
    for b in range(TA):
        total = jnp.sum(jnp.where(lane // R == b, rows, 0.0), axis=1, keepdims=True)
        message = jnp.where(jnp.logical_and(row < TA, lane == y_own + b), total, message)
    rank = count[owner]
    count[owner] = rank + 1
    outbox[owner * CAP + rank] = message


def fire(owners, places, winds, level_set, fuel_load, spread_base, peers):
    tile = pl.BlockSpec((1, S, S), lambda i: (i, 0, 0))
    scalars = pl.BlockSpec(memory_space=pltpu.SMEM)
    rows = peers * CX + 2 * RIM
    return pl.pallas_call(
        functools.partial(fire_kernel, peers),
        grid=(TPD,),
        in_specs=[
            scalars,
            scalars,
            pl.BlockSpec((peers, BLOCK, 128), lambda i: (0, 0, 0)),
            tile,
            tile,
            tile,
        ],
        out_specs=[tile, tile, pl.BlockSpec((peers * CAP, 8, 128), lambda i: (0, 0, 0))],
        out_shape=[
            jax.ShapeDtypeStruct((TPD, S, S), F32),
            jax.ShapeDtypeStruct((TPD, S, S), F32),
            jax.ShapeDtypeStruct((peers * CAP, 8, 128), F32),
        ],
        scratch_shapes=[
            pltpu.VMEM((2, rows, 128), F32),
            pltpu.VMEM((2, rows, 128), F32),
            pltpu.VMEM((2, ROWS, 8, 128), F32),
            pltpu.SMEM((peers,), jnp.int32),
        ],
        name="fire",
        compiler_params=pltpu.CompilerParams(vmem_limit_bytes=24 * 1024 * 1024),
        cost_estimate=pl.CostEstimate(
            flops=50_000_000, bytes_accessed=6_500_000, transcendentals=3_200_000
        ),
    )(owners, places, winds, level_set, fuel_load, spread_base)


def final_kernel(levels, inbox_ref, part_ref, out_ref, field):
    step = pl.program_id(0)

    @pl.when(step == 0)
    def _():
        inbox = inbox_ref[...]
        slots = inbox.shape[0]
        position = pltpu.roll(inbox, TA, 1).reshape(slots * 8, 128)
        values = inbox.reshape(slots * 8, 128)
        lane = iota(1, (slots * 8, 128)).astype(F32)
        valid = iota(0, (slots * 8, 128)) % 8 < TA
        hot = jnp.where(jnp.logical_and(valid, lane == position), 1.0, 0.0)
        total = lax.dot_general(
            hot, values, (((0,), (0,)), ((), ())),
            precision=lax.Precision.HIGHEST, preferred_element_type=F32,
        )
        field[...] = total[:CX]

    for k in range(levels):
        z = (jnp.full((8, 128), step * levels + k, jnp.int32)).astype(F32)
        gain = heat_gain * jnp.exp((z + 0.5) * (-4.0 / LZ))
        out_ref[k] = part_ref[k] + field[...] * jnp.concatenate([gain] * (CX // 8), axis=0)


def finish(inbox, part):
    levels = 16
    cells = pl.BlockSpec((levels, CX, CY), lambda i: (i, 0, 0))
    return pl.pallas_call(
        functools.partial(final_kernel, levels),
        grid=(LZ // levels,),
        in_specs=[pl.BlockSpec(inbox.shape, lambda i: (0, 0, 0)), cells],
        out_specs=cells,
        out_shape=jax.ShapeDtypeStruct((LZ, CX, CY), F32),
        scratch_shapes=[pltpu.VMEM((CX, CY), F32)],
        name="finish",
        cost_estimate=pl.CostEstimate(flops=3_000_000, bytes_accessed=5_300_000, transcendentals=0),
    )(inbox, part)


def shifted(cells, axis, up):
    ends = lax.axis_size(axis) - 1
    pairs = [(i, i + 1) if up else (i + 1, i) for i in range(ends)]
    return lax.ppermute(cells, axis, pairs)


def exchange(cells, peers):
    return lax.all_to_all(cells, "gx", split_axis=0, concat_axis=0, tiled=True)


def body(theta, wind_u, wind_v, level_set, fuel_load, spread_base, tile_owner, tile_place):
    peers = lax.axis_size("gx")
    up, down = wind_edges(wind_u, wind_v)
    low = shifted(up, "gy", True)
    high = shifted(down, "gy", False)
    winds = exchange(pack_winds(wind_u, wind_v, low, high, peers), peers)

    first_x, last_x, first_y, last_y = theta_edges(theta)
    west = shifted(last_x, "gx", True)
    east = shifted(first_x, "gx", False)
    south = shifted(last_y, "gy", True)
    north = shifted(first_y, "gy", False)
    part = advect(theta, wind_u, wind_v, west, east, south, north)

    level_out, fuel_out, outbox = fire(
        tile_owner[0, 0], tile_place[0, 0], winds, level_set[0, 0], fuel_load[0, 0], spread_base[0, 0], peers
    )
    inbox = exchange(outbox, peers)
    theta_next = finish(inbox, part)
    return (theta_next, level_out[None, None], fuel_out[None, None])


def solution(mesh):
    in_specs = (
        P(None, "gx", "gy"),
        P(None, "gx", "gy"),
        P(None, "gx", "gy"),
        P("gx", "gy", None, None, None),
        P("gx", "gy", None, None, None),
        P("gx", "gy", None, None, None),
        P("gx", "gy", None),
        P("gx", "gy", None),
    )
    out_specs = (
        P(None, "gx", "gy"),
        P("gx", "gy", None, None, None),
        P("gx", "gy", None, None, None),
    )
    return jax.shard_map(body, mesh=mesh, in_specs=in_specs, out_specs=out_specs, check_vma=False)
```

```python
import functools

import jax
import jax.numpy as jnp
from jax import lax
from jax.experimental import pallas as pl
from jax.experimental.pallas import tpu as pltpu
from jax.sharding import PartitionSpec as P

LZ = 80
TA = 4
R = 32
KSUB = 6
CAP = 2
TPD = 16
S = 128
CX = 64
CY = 128
ROWS = S // 8
BLOCK = 2 * CX + 8
RIM = 8
GROUP = 8
GROUPS = LZ // GROUP

time_step = 0.03
diffusion = 0.15
burn_rate = 0.15
regular = 0.01
courant = 0.4
heat_gain = 2.0

F32 = jnp.float32
LOCAL = pl.BlockSpec(memory_space=pltpu.VMEM)
ANYWHERE = pl.BlockSpec(memory_space=pl.ANY)
SCALARS = pl.BlockSpec(memory_space=pltpu.SMEM)


def iota(dim, shape=(8, 128)):
    return lax.broadcasted_iota(jnp.int32, shape, dim)


def near(cells):
    return pltpu.with_memory_space_constraint(cells, pltpu.VMEM)


def params(mib):
    return pltpu.CompilerParams(vmem_limit_bytes=mib * 1024 * 1024)


def wind_edge_kernel(u_ref, v_ref, block_ref, up_ref, down_ref, sems):
    copies = [
        pltpu.make_async_copy(ref.at[0], block_ref.at[c * CX : (c + 1) * CX], sems.at[c])
        for c, ref in enumerate((u_ref, v_ref))
    ]
    for copy in copies:
        copy.start()
    for copy in copies:
        copy.wait()
    columns = jnp.transpose(block_ref[...])
    row = iota(0)
    last = jnp.broadcast_to(columns[CY - 1 : CY], (8, 128))
    first = jnp.broadcast_to(columns[0:1], (8, 128))
    up_ref[...] = jnp.where(row == 0, last, 0.0)
    down_ref[...] = jnp.where(row == TA + 1, first, 0.0)


def wind_edges(wind_u, wind_v):
    return pl.pallas_call(
        wind_edge_kernel,
        in_specs=[ANYWHERE, ANYWHERE],
        out_specs=[LOCAL, LOCAL, LOCAL],
        out_shape=[pltpu.VMEM((2 * CX, 128), F32), pltpu.VMEM((8, 128), F32), pltpu.VMEM((8, 128), F32)],
        scratch_shapes=[pltpu.SemaphoreType.DMA((2,))],
        name="wind_edges",
        compiler_params=params(4),
    )(wind_u, wind_v)


def pack_kernel(block_ref, low_ref, high_ref, out_ref):
    edge = low_ref[...] + high_ref[...]
    for peer in range(out_ref.shape[0]):
        out_ref[peer, : 2 * CX] = block_ref[...]
        out_ref[peer, 2 * CX :] = edge


def pack_winds(block, low, high, peers):
    return pl.pallas_call(
        pack_kernel,
        in_specs=[LOCAL, LOCAL, LOCAL],
        out_specs=LOCAL,
        out_shape=pltpu.VMEM((peers, BLOCK, 128), F32),
        name="pack_winds",
        compiler_params=params(4),
    )(near(block), near(low), near(high))


def theta_edge_kernel(
    after_ref, theta_ref, u_ref, v_ref,
    theta_out, u_out, v_out, first_x_ref, last_x_ref, first_y_ref, last_y_ref, sems,
):
    def copy(c, g):
        source, target = ((theta_ref, theta_out), (u_ref, u_out), (v_ref, v_out))[c]
        part = pl.ds(g * GROUP, GROUP)
        return pltpu.make_async_copy(source.at[part], target.at[part], sems.at[c, g])

    for g in reversed(range(GROUPS)):
        copy(0, g).start()
    for c in (1, 2):
        for g in range(GROUPS):
            copy(c, g).start()
    lane = iota(1, (CX, 128))

    def one(i, carry):
        first, last = carry
        g = GROUPS - 1 - i
        copy(0, g).wait()
        first = pltpu.roll(first, GROUP, 1)
        last = pltpu.roll(last, GROUP, 1)
        for k in range(GROUP):
            z = g * GROUP + k
            cells = theta_out[z]
            first_x_ref[pl.ds(z, 1)] = cells[0:1]
            last_x_ref[pl.ds(z, 1)] = cells[CX - 1 : CX]
            turned = pltpu.roll(cells, k + 1, 1)
            first = jnp.where(lane == k + 1, turned, first)
            last = jnp.where(lane == k, turned, last)
        return first, last

    zero = jnp.zeros((CX, 128), F32)
    first, last = lax.fori_loop(0, GROUPS, one, (zero, zero))
    first_y_ref[...] = first
    last_y_ref[...] = last
    for c in (1, 2):
        for g in range(GROUPS):
            copy(c, g).wait()


def theta_edges(after, theta, wind_u, wind_v):
    whole = pltpu.VMEM((LZ, CX, CY), F32)
    row = pltpu.VMEM((LZ, 128), F32)
    column = pltpu.VMEM((CX, 128), F32)
    return pl.pallas_call(
        theta_edge_kernel,
        in_specs=[ANYWHERE] * 4,
        out_specs=[LOCAL] * 7,
        out_shape=[whole, whole, whole, row, row, column, column],
        scratch_shapes=[pltpu.SemaphoreType.DMA((3, GROUPS))],
        name="theta_edges",
        compiler_params=params(4),
        cost_estimate=pl.CostEstimate(flops=4_000_000, bytes_accessed=8_000_000, transcendentals=0),
    )(after, theta, wind_u, wind_v)


def advect_kernel(theta_ref, u_ref, v_ref, west_ref, east_ref, south_ref, north_ref, out_ref):
    lane = iota(1, (CX, 128))
    row = iota(0, (CX, 128))

    def one(g, carry):
        south_all, north_all = carry
        for k in range(GROUP):
            z = g * GROUP + k
            t = theta_ref[z]
            u = u_ref[z]
            v = v_ref[z]
            west = jnp.where(row == 0, west_ref[pl.ds(z, 1)], pltpu.roll(t, 1, 0))
            east = jnp.where(row == CX - 1, east_ref[pl.ds(z, 1)], pltpu.roll(t, CX - 1, 0))
            south = pltpu.roll(jnp.where(lane == CY - 1, pltpu.roll(south_all, 127 - k, 1), t), 1, 1)
            north = pltpu.roll(jnp.where(lane == 0, pltpu.roll(north_all, 127 - k, 1), t), CY - 1, 1)
            change = jnp.abs(u) * (t - jnp.where(u > 0, west, east)) + jnp.abs(v) * (
                t - jnp.where(v > 0, south, north)
            )
            out_ref[z] = t - courant * change
        return pltpu.roll(south_all, 128 - GROUP, 1), pltpu.roll(north_all, 128 - GROUP, 1)

    lax.fori_loop(0, GROUPS, one, (south_ref[...], north_ref[...]))


def advect(*args):
    return pl.pallas_call(
        advect_kernel,
        in_specs=[LOCAL] * 7,
        out_specs=LOCAL,
        out_shape=pltpu.VMEM((LZ, CX, CY), F32),
        name="advect",
        compiler_params=params(4),
        cost_estimate=pl.CostEstimate(flops=14_000_000, bytes_accessed=1_000_000, transcendentals=0),
    )(*(near(a) for a in args))


def fire_kernel(
    peers, waits, owner_ref, place_ref, winds_ref, level_ref, fuel_ref, base_ref, *rest
):
    level_out, fuel_out, outbox, surface, edges, wind, level_own, fuel_own, count, sems = rest[waits:]
    lane = iota(1)
    row = iota(0)

    for c in range(2):
        for ref in (surface, edges):
            ref[c, 0:RIM] = jnp.zeros((RIM, 128), F32)
            ref[c, RIM + peers * CX :] = jnp.zeros((RIM, 128), F32)
    for d in range(peers):
        count[d] = 0
        turned = jnp.transpose(
            jnp.concatenate([winds_ref[d, 2 * CX :], jnp.zeros((120, 128), F32)], axis=0)
        )
        for c in range(2):
            surface[c, RIM + d * CX : RIM + (d + 1) * CX] = winds_ref[d, c * CX : (c + 1) * CX]
            edges[c, RIM + d * CX : RIM + (d + 1) * CX] = turned[c * CX : (c + 1) * CX]
    for d in range(peers * CAP):
        outbox[d] = jnp.where(row < TA, 0.0, -1.0)

    tiles_y = CY // TA
    low_row = (row + 1) // 2
    low_lane = (lane + R // 2) // R
    part_row = jnp.where(row % 2 == 0, 0.5, 0.0) + 0.5 / R
    part_lane = (lane.astype(F32) + 0.5) / R + 0.5 - low_lane.astype(F32)

    def results(t):
        return (
            pltpu.make_async_copy(level_own.at[t], level_out.at[t], sems.at[0, t]),
            pltpu.make_async_copy(fuel_own.at[t], fuel_out.at[t], sems.at[1, t]),
        )

    def one(tile, carry):
        owner = owner_ref[tile]
        place = place_ref[tile]
        x_own = place // tiles_y * TA
        y_own = lax.rem(place, tiles_y) * TA
        first = owner * CX + x_own + (RIM - 1)
        outside = jnp.logical_or(
            jnp.logical_and(lane == 0, y_own == 0), jnp.logical_and(lane == TA + 1, y_own == CY - TA)
        )
        back = lax.rem(CY + 1 - y_own, CY)
        for c in range(2):
            patch = pltpu.roll(surface[c, pl.ds(first, 8), :], back, 1)
            patch = jnp.where(outside, edges[c, pl.ds(first, 8), :], patch)
            left = jnp.take_along_axis(patch, low_lane, axis=1)
            right = jnp.take_along_axis(patch, low_lane + 1, axis=1)
            fine = left + (right - left) * part_lane
            below = jnp.take_along_axis(fine, low_row, axis=0)
            above = jnp.take_along_axis(fine, low_row + 1, axis=0)
            rise = above - below
            begin = below + rise * part_row
            slope = rise * (1.0 / R)
            for k in range(ROWS):
                wind[c, k] = begin + slope * float(k)

        level = [level_ref[tile, pl.ds(k, 8, stride=ROWS), :] for k in range(ROWS)]
        fuel = [fuel_ref[tile, pl.ds(k, 8, stride=ROWS), :] for k in range(ROWS)]
        heat = sum(fuel[1:], fuel[0])
        rate = [base_ref[tile, pl.ds(k, 8, stride=ROWS), :] * (0.5 * time_step) for k in range(ROWS)]
        for _ in range(KSUB):
            before = jnp.where(row == 0, level[0], pltpu.roll(level[-1], 1, 0))
            after = jnp.where(row == 7, level[-1], pltpu.roll(level[0], 7, 0))
            rimmed = [before, *level, after]
            new = []
            for k in range(ROWS):
                cell = rimmed[k + 1]
                west, east = rimmed[k], rimmed[k + 2]
                south = jnp.where(lane == 0, cell, pltpu.roll(cell, 1, 1))
                north = jnp.where(lane == S - 1, cell, pltpu.roll(cell, S - 1, 1))
                dx = east - west
                dy = north - south
                square = dx * dx + dy * dy + 4.0 * regular
                length = square * lax.rsqrt(square)
                move = jnp.maximum(length + (wind[0, k] * dx + wind[1, k] * dy), 0.0)
                around = (east + west) + (north + south)
                cell = cell * (1.0 - 4.0 * diffusion) + around * diffusion - rate[k] * move
                fuel[k] = fuel[k] * ((1.0 - 0.5 * burn_rate) + (0.5 * burn_rate) * jnp.tanh(cell))
                new.append(cell)
            level = new
        for k in range(ROWS):
            level_own[tile, pl.ds(k, 8, stride=ROWS), :] = level[k]
            fuel_own[tile, pl.ds(k, 8, stride=ROWS), :] = fuel[k]
        for copy in results(tile):
            copy.start()
        heat = (heat - sum(fuel[1:], fuel[0])) * (1.0 / (R * R))
        heat = heat + pltpu.roll(heat, 7, 0)

        message = jnp.where(row < TA, 0.0, (x_own + row - TA).astype(F32))
        rows = jnp.take_along_axis(heat, jnp.minimum(2 * row, 7), axis=0)
        for b in range(TA):
            total = jnp.sum(jnp.where(lane // R == b, rows, 0.0), axis=1, keepdims=True)
            message = jnp.where(jnp.logical_and(row < TA, lane == y_own + b), total, message)
        rank = count[owner]
        count[owner] = rank + 1
        outbox[owner * CAP + rank] = message
        return carry

    lax.fori_loop(0, TPD, one, 0)
    for t in range(TPD):
        for copy in results(t):
            copy.wait()


def fire(owners, places, winds, level_set, fuel_load, spread_base, peers, waits):
    rows = peers * CX + 2 * RIM
    tiles = (TPD, S, S)
    return pl.pallas_call(
        functools.partial(fire_kernel, peers, len(waits)),
        in_specs=[SCALARS, SCALARS] + [LOCAL] * 4 + [ANYWHERE] * len(waits),
        out_specs=[ANYWHERE, ANYWHERE, LOCAL],
        out_shape=[
            jax.ShapeDtypeStruct(tiles, F32),
            jax.ShapeDtypeStruct(tiles, F32),
            pltpu.VMEM((peers * CAP, 8, 128), F32),
        ],
        scratch_shapes=[
            pltpu.VMEM((2, rows, 128), F32),
            pltpu.VMEM((2, rows, 128), F32),
            pltpu.VMEM((2, ROWS, 8, 128), F32),
            pltpu.VMEM(tiles, F32),
            pltpu.VMEM(tiles, F32),
            pltpu.SMEM((peers,), jnp.int32),
            pltpu.SemaphoreType.DMA((2, TPD)),
        ],
        name="fire",
        compiler_params=params(12),
        cost_estimate=pl.CostEstimate(
            flops=50_000_000, bytes_accessed=6_500_000, transcendentals=3_200_000
        ),
    )(owners, places, *(near(a) for a in (winds, level_set, fuel_load, spread_base)), *waits)


def final_kernel(inbox_ref, part_ref, out_ref, field, result, sems):
    inbox = inbox_ref[...]
    slots = inbox.shape[0]
    position = pltpu.roll(inbox, TA, 1).reshape(slots * 8, 128)
    values = inbox.reshape(slots * 8, 128)
    lane = iota(1, (slots * 8, 128)).astype(F32)
    valid = iota(0, (slots * 8, 128)) % 8 < TA
    hot = jnp.where(jnp.logical_and(valid, lane == position), 1.0, 0.0)
    total = lax.dot_general(
        hot, values, (((0,), (0,)), ((), ())),
        precision=lax.Precision.HIGHEST, preferred_element_type=F32,
    )
    field[...] = total[:CX]

    def copy(g):
        part = pl.ds(g * GROUP, GROUP)
        return pltpu.make_async_copy(result.at[part], out_ref.at[part], sems.at[g])

    def one(g, carry):
        for k in range(GROUP):
            z = g * GROUP + k
            height = jnp.full((8, 128), z, jnp.int32).astype(F32)
            gain = heat_gain * jnp.exp((height + 0.5) * (-4.0 / LZ))
            result[z] = part_ref[z] + field[...] * jnp.concatenate([gain] * (CX // 8), axis=0)
        copy(g).start()
        return carry

    lax.fori_loop(0, GROUPS, one, 0)
    for g in range(GROUPS):
        copy(g).wait()


def finish(inbox, part):
    return pl.pallas_call(
        final_kernel,
        in_specs=[LOCAL, LOCAL],
        out_specs=ANYWHERE,
        out_shape=jax.ShapeDtypeStruct((LZ, CX, CY), F32),
        scratch_shapes=[
            pltpu.VMEM((CX, CY), F32),
            pltpu.VMEM((LZ, CX, CY), F32),
            pltpu.SemaphoreType.DMA((GROUPS,)),
        ],
        name="finish",
        compiler_params=params(8),
        cost_estimate=pl.CostEstimate(flops=3_000_000, bytes_accessed=2_700_000, transcendentals=0),
    )(near(inbox), near(part))


def shifted(cells, axis, up):
    ends = lax.axis_size(axis) - 1
    pairs = [(i, i + 1) if up else (i + 1, i) for i in range(ends)]
    return lax.ppermute(cells, axis, pairs)


def exchange(cells):
    return lax.all_to_all(cells, "gx", split_axis=0, concat_axis=0, tiled=True)


def body(theta, wind_u, wind_v, level_set, fuel_load, spread_base, tile_owner, tile_place):
    peers = lax.axis_size("gx")
    block, up, down = wind_edges(wind_u, wind_v)
    low = shifted(up, "gy", True)
    high = shifted(down, "gy", False)
    packed = pack_winds(block, low, high, peers)
    winds = exchange(packed)

    theta_near, u_near, v_near, first_x, last_x, first_y, last_y = theta_edges(packed, theta, wind_u, wind_v)
    west = shifted(last_x, "gx", True)
    east = shifted(first_x, "gx", False)
    south = shifted(last_y, "gy", True)
    north = shifted(first_y, "gy", False)

    level_out, fuel_out, outbox = fire(
        tile_owner[0, 0], tile_place[0, 0], winds, level_set[0, 0], fuel_load[0, 0], spread_base[0, 0], peers,
        (west, east, south, north),
    )
    part = advect(theta_near, u_near, v_near, west, east, south, north)
    inbox = exchange(outbox)
    theta_next = finish(inbox, part)
    return (theta_next, level_out[None, None], fuel_out[None, None])


def solution(mesh):
    in_specs = (
        P(None, "gx", "gy"),
        P(None, "gx", "gy"),
        P(None, "gx", "gy"),
        P("gx", "gy", None, None, None),
        P("gx", "gy", None, None, None),
        P("gx", "gy", None, None, None),
        P("gx", "gy", None),
        P("gx", "gy", None),
    )
    out_specs = (
        P(None, "gx", "gy"),
        P("gx", "gy", None, None, None),
        P("gx", "gy", None, None, None),
    )
    return jax.shard_map(body, mesh=mesh, in_specs=in_specs, out_specs=out_specs, check_vma=False)
```

```python
import functools

import jax
import jax.numpy as jnp
from jax import lax
from jax.experimental import pallas as pl
from jax.experimental.pallas import tpu as pltpu
from jax.sharding import PartitionSpec as P

LZ = 80
TA = 4
R = 32
KSUB = 6
CAP = 2
TPD = 16
S = 128
CX = 64
CY = 128
ROWS = S // 8
BLOCK = 2 * CX + 8
RIM = 8
GROUP = 8
GROUPS = LZ // GROUP
SIDE = 2
AHEAD = 2

time_step = 0.03
diffusion = 0.15
burn_rate = 0.15
regular = 0.01
courant = 0.4
heat_gain = 2.0

F32 = jnp.float32
LOCAL = pl.BlockSpec(memory_space=pltpu.VMEM)
FAR = pl.BlockSpec(memory_space=pltpu.HBM)
ANYWHERE = pl.BlockSpec(memory_space=pl.ANY)
SCALARS = pl.BlockSpec(memory_space=pltpu.SMEM)


def iota(dim, shape=(8, 128)):
    return lax.broadcasted_iota(jnp.int32, shape, dim)


def near(cells):
    return pltpu.with_memory_space_constraint(cells, pltpu.VMEM)


def far(cells):
    return pltpu.with_memory_space_constraint(cells, pltpu.HBM)


def params(mib):
    return pltpu.CompilerParams(vmem_limit_bytes=mib * 1024 * 1024)


def wind_edge_kernel(u_ref, v_ref, block_ref, up_ref, down_ref, sems):
    copies = [
        pltpu.make_async_copy(ref.at[0], block_ref.at[c * CX : (c + 1) * CX], sems.at[c])
        for c, ref in enumerate((u_ref, v_ref))
    ]
    for copy in copies:
        copy.start()
    for copy in copies:
        copy.wait()
    columns = jnp.transpose(block_ref[...])
    row = iota(0)
    last = jnp.broadcast_to(columns[CY - 1 : CY], (8, 128))
    first = jnp.broadcast_to(columns[0:1], (8, 128))
    up_ref[...] = jnp.where(row == 0, last, 0.0)
    down_ref[...] = jnp.where(row == TA + 1, first, 0.0)


def wind_edges(wind_u, wind_v):
    return pl.pallas_call(
        wind_edge_kernel,
        in_specs=[FAR, FAR],
        out_specs=[LOCAL, LOCAL, LOCAL],
        out_shape=[pltpu.VMEM((2 * CX, 128), F32), pltpu.VMEM((8, 128), F32), pltpu.VMEM((8, 128), F32)],
        scratch_shapes=[pltpu.SemaphoreType.DMA((2,))],
        name="wind_edges",
        compiler_params=params(4),
    )(far(wind_u), far(wind_v))


def pack_kernel(block_ref, low_ref, high_ref, out_ref):
    edge = low_ref[...] + high_ref[...]
    for peer in range(out_ref.shape[0]):
        out_ref[peer, : 2 * CX] = block_ref[...]
        out_ref[peer, 2 * CX :] = edge


def pack_winds(block, low, high, peers):
    return pl.pallas_call(
        pack_kernel,
        in_specs=[LOCAL, LOCAL, LOCAL],
        out_specs=LOCAL,
        out_shape=pltpu.VMEM((peers, BLOCK, 128), F32),
        name="pack_winds",
        compiler_params=params(4),
    )(near(block), near(low), near(high))


def theta_edge_kernel(after_ref, theta_ref, first_x_ref, last_x_ref, first_y_ref, last_y_ref, theta, sems):
    def copy(g):
        part = pl.ds(g * GROUP, GROUP)
        return pltpu.make_async_copy(theta_ref.at[part], theta.at[part], sems.at[g])

    for g in reversed(range(GROUPS)):
        copy(g).start()
    lane = iota(1, (CX, 128))

    def one(i, carry):
        first, last = carry
        g = GROUPS - 1 - i
        copy(g).wait()
        first = pltpu.roll(first, GROUP, 1)
        last = pltpu.roll(last, GROUP, 1)
        for k in range(GROUP):
            z = g * GROUP + k
            cells = theta[z]
            first_x_ref[pl.ds(z, 1)] = cells[0:1]
            last_x_ref[pl.ds(z, 1)] = cells[CX - 1 : CX]
            turned = pltpu.roll(cells, k + 1, 1)
            first = jnp.where(lane == k + 1, turned, first)
            last = jnp.where(lane == k, turned, last)
        return first, last

    zero = jnp.zeros((CX, 128), F32)
    first, last = lax.fori_loop(0, GROUPS, one, (zero, zero))
    first_y_ref[...] = first
    last_y_ref[...] = last


def theta_edges(after, theta):
    row = pltpu.VMEM((LZ, 128), F32)
    column = pltpu.VMEM((CX, 128), F32)
    return pl.pallas_call(
        theta_edge_kernel,
        in_specs=[ANYWHERE, FAR],
        out_specs=[LOCAL] * 4,
        out_shape=[row, row, column, column],
        scratch_shapes=[pltpu.VMEM((LZ, CX, CY), F32), pltpu.SemaphoreType.DMA((GROUPS,))],
        name="theta_edges",
        compiler_params=params(8),
        cost_estimate=pl.CostEstimate(flops=4_000_000, bytes_accessed=2_700_000, transcendentals=0),
    )(after, far(theta))


def advect_kernel(
    theta_ref, u_ref, v_ref, west_ref, east_ref, south_ref, north_ref, out_ref, theta, wind_u, wind_v, sems
):
    def copies(g):
        part = pl.ds(g * GROUP, GROUP)
        pairs = ((theta_ref, theta), (u_ref, wind_u), (v_ref, wind_v))
        return [
            pltpu.make_async_copy(source.at[part], target.at[part], sems.at[c, g])
            for c, (source, target) in enumerate(pairs)
        ]

    for g in range(GROUPS):
        for copy in copies(g):
            copy.start()
    lane = iota(1, (CX, 128))
    row = iota(0, (CX, 128))

    def one(g, carry):
        south_all, north_all = carry
        for copy in copies(g):
            copy.wait()
        def begin(k):
            t = theta[g * GROUP + k]
            rolled = [pltpu.roll(t, 1, 1), pltpu.roll(t, CY - 1, 1)]
            rims = [pltpu.roll(south_all, (128 - k) % 128, 1), pltpu.roll(north_all, 126 - k, 1)]
            return t, rolled, rims

        def end(k, begun):
            z = g * GROUP + k
            t, rolled, rims = begun
            u = wind_u[z]
            v = wind_v[z]
            west = jnp.where(row == 0, west_ref[pl.ds(z, 1)], pltpu.roll(t, 1, 0))
            east = jnp.where(row == CX - 1, east_ref[pl.ds(z, 1)], pltpu.roll(t, CX - 1, 0))
            south = jnp.where(lane == 0, rims[0], rolled[0])
            north = jnp.where(lane == CY - 1, rims[1], rolled[1])
            change = jnp.abs(u) * (t - jnp.where(u > 0, west, east)) + jnp.abs(v) * (
                t - jnp.where(v > 0, south, north)
            )
            out_ref[z] = t - courant * change

        begun = [begin(k) for k in range(AHEAD)]
        for k in range(GROUP):
            if k + AHEAD < GROUP:
                begun.append(begin(k + AHEAD))
            end(k, begun[k])
        return pltpu.roll(south_all, 128 - GROUP, 1), pltpu.roll(north_all, 128 - GROUP, 1)

    lax.fori_loop(0, GROUPS, one, (south_ref[...], north_ref[...]))


def advect(theta, wind_u, wind_v, *rims):
    whole = pltpu.VMEM((LZ, CX, CY), F32)
    return pl.pallas_call(
        advect_kernel,
        in_specs=[FAR] * 3 + [LOCAL] * 4,
        out_specs=LOCAL,
        out_shape=whole,
        scratch_shapes=[whole, whole, whole, pltpu.SemaphoreType.DMA((3, GROUPS))],
        name="advect",
        compiler_params=params(12),
        cost_estimate=pl.CostEstimate(flops=14_000_000, bytes_accessed=8_000_000, transcendentals=0),
    )(far(theta), far(wind_u), far(wind_v), *(near(a) for a in rims))


def fire_kernel(
    peers, waits, owner_ref, place_ref, winds_ref, level_ref, fuel_ref, base_ref, *rest
):
    (
        level_out, fuel_out, outbox, surface, edges, begins, slopes, heats,
        level_own, fuel_own, base_own, count, in_sems, out_sems,
    ) = rest[waits:]
    lane = iota(1)
    row = iota(0)

    def inputs(t):
        pairs = ((level_ref, level_own), (fuel_ref, fuel_own), (base_ref, base_own))
        return [
            pltpu.make_async_copy(source.at[t], target.at[t], in_sems.at[c, t])
            for c, (source, target) in enumerate(pairs)
        ]

    def results(t):
        pairs = ((level_own, level_out), (fuel_own, fuel_out))
        return [
            pltpu.make_async_copy(source.at[t], target.at[t], out_sems.at[c, t])
            for c, (source, target) in enumerate(pairs)
        ]

    for t in range(TPD):
        for copy in inputs(t):
            copy.start()

    for c in range(2):
        for ref in (surface, edges):
            ref[c, 0:RIM] = jnp.zeros((RIM, 128), F32)
            ref[c, RIM + peers * CX :] = jnp.zeros((RIM, 128), F32)
    turned = jnp.transpose(jnp.concatenate([winds_ref[d, 2 * CX :] for d in range(peers)], axis=0))
    for d in range(peers):
        count[d] = 0
        own = pltpu.roll(turned, (128 - 8 * d) % 128, 1)
        for c in range(2):
            surface[c, RIM + d * CX : RIM + (d + 1) * CX] = winds_ref[d, c * CX : (c + 1) * CX]
            edges[c, RIM + d * CX : RIM + (d + 1) * CX] = own[c * CX : (c + 1) * CX]

    tiles_y = CY // TA
    low_row = (row + 1) // 2
    low_lane = (lane + R // 2) // R
    part_row = jnp.where(row % 2 == 0, 0.5, 0.0) + 0.5 / R
    part_lane = (lane.astype(F32) + 0.5) / R + 0.5 - low_lane.astype(F32)

    x_own, y_own, patches = [], [], []
    for t in range(TPD):
        place = place_ref[t]
        x_own.append(place // tiles_y * TA)
        y_own.append(lax.rem(place, tiles_y) * TA)
        first = owner_ref[t] * CX + x_own[t] + (RIM - 1)
        back = lax.rem(CY + 1 - y_own[t], CY)
        outside = jnp.logical_or(
            jnp.logical_and(lane == 0, y_own[t] == 0),
            jnp.logical_and(lane == TA + 1, y_own[t] == CY - TA),
        )
        for c in range(2):
            patch = pltpu.roll(surface[c, pl.ds(first, 8), :], back, 1)
            patches.append(jnp.where(outside, edges[c, pl.ds(first, 8), :], patch))
    left = [jnp.take_along_axis(p, low_lane, axis=1) for p in patches]
    right = [jnp.take_along_axis(p, low_lane + 1, axis=1) for p in patches]
    fine = [p + (q - p) * part_lane for p, q in zip(left, right)]
    below = [jnp.take_along_axis(p, low_row, axis=0) for p in fine]
    above = [jnp.take_along_axis(p, low_row + 1, axis=0) for p in fine]
    for i, (p, q) in enumerate(zip(below, above)):
        begins[i] = p + (q - p) * part_row
        slopes[i] = (q - p) * (1.0 / R)

    def burn(t):
        begin = [begins[2 * t + c] for c in range(2)]
        slope = [slopes[2 * t + c] for c in range(2)]
        level = [level_own[t, pl.ds(k, 8, stride=ROWS), :] for k in range(ROWS)]
        fuel = [fuel_own[t, pl.ds(k, 8, stride=ROWS), :] for k in range(ROWS)]
        heat = sum(fuel[1:], fuel[0])
        rate = [base_own[t, pl.ds(k, 8, stride=ROWS), :] * (0.5 * time_step) for k in range(ROWS)]
        wind = [[begin[c] + slope[c] * float(k) for k in range(ROWS)] for c in range(2)]
        yield
        for _ in range(KSUB):
            before = jnp.where(row == 0, level[0], pltpu.roll(level[-1], 1, 0))
            after = jnp.where(row == 7, level[-1], pltpu.roll(level[0], 7, 0))
            rimmed = [before, *level, after]
            south = [jnp.where(lane == 0, cell, pltpu.roll(cell, 1, 1)) for cell in level]
            north = [jnp.where(lane == S - 1, cell, pltpu.roll(cell, S - 1, 1)) for cell in level]
            yield
            new = []
            for k in range(ROWS):
                cell = rimmed[k + 1]
                west, east = rimmed[k], rimmed[k + 2]
                dx = east - west
                dy = north[k] - south[k]
                square = dx * dx + dy * dy + 4.0 * regular
                length = square * lax.rsqrt(square)
                move = jnp.maximum(length + (wind[0][k] * dx + wind[1][k] * dy), 0.0)
                around = (east + west) + (north[k] + south[k])
                cell = cell * (1.0 - 4.0 * diffusion) + around * diffusion - rate[k] * move
                fuel[k] = fuel[k] * ((1.0 - 0.5 * burn_rate) + (0.5 * burn_rate) * jnp.tanh(cell))
                new.append(cell)
            level = new
        yield
        for k in range(ROWS):
            level_own[t, pl.ds(k, 8, stride=ROWS), :] = level[k]
            fuel_own[t, pl.ds(k, 8, stride=ROWS), :] = fuel[k]
        heats[t] = (heat - sum(fuel[1:], fuel[0])) * (1.0 / (R * R))

    def some(i, carry):
        tiles = [i * SIDE + j for j in range(SIDE)]
        for t in tiles:
            for copy in inputs(t):
                copy.wait()
        works = [burn(t) for t in tiles]
        while works:
            works = [w for w in works if next(w, works) is None]
        for t in tiles:
            for copy in results(t):
                copy.start()
        return carry

    lax.fori_loop(0, TPD // SIDE, some, 0)

    for d in range(peers * CAP):
        outbox[d] = jnp.where(row < TA, 0.0, -1.0)
    pairs = [heats[t] for t in range(TPD)]
    pairs = [h + pltpu.roll(h, 7, 0) for h in pairs]
    pairs = [jnp.take_along_axis(h, jnp.minimum(2 * row, 7), axis=0) for h in pairs]
    sums = [
        [jnp.sum(jnp.where(lane // R == b, h, 0.0), axis=1, keepdims=True) for b in range(TA)] for h in pairs
    ]
    for t in range(TPD):
        message = jnp.where(row < TA, 0.0, (x_own[t] + row - TA).astype(F32))
        for b in range(TA):
            message = jnp.where(jnp.logical_and(row < TA, lane == y_own[t] + b), sums[t][b], message)
        owner = owner_ref[t]
        rank = count[owner]
        count[owner] = rank + 1
        outbox[owner * CAP + rank] = message
    for t in range(TPD):
        for copy in results(t):
            copy.wait()


def fire(owners, places, winds, level_set, fuel_load, spread_base, peers, waits):
    rows = peers * CX + 2 * RIM
    tiles = (TPD, S, S)
    return pl.pallas_call(
        functools.partial(fire_kernel, peers, len(waits)),
        in_specs=[SCALARS, SCALARS, LOCAL] + [FAR] * 3 + [ANYWHERE] * len(waits),
        out_specs=[ANYWHERE, ANYWHERE, LOCAL],
        out_shape=[
            jax.ShapeDtypeStruct(tiles, F32),
            jax.ShapeDtypeStruct(tiles, F32),
            pltpu.VMEM((peers * CAP, 8, 128), F32),
        ],
        scratch_shapes=[
            pltpu.VMEM((2, rows, 128), F32),
            pltpu.VMEM((2, rows, 128), F32),
            pltpu.VMEM((2 * TPD, 8, 128), F32),
            pltpu.VMEM((2 * TPD, 8, 128), F32),
            pltpu.VMEM((TPD, 8, 128), F32),
            pltpu.VMEM(tiles, F32),
            pltpu.VMEM(tiles, F32),
            pltpu.VMEM(tiles, F32),
            pltpu.SMEM((peers,), jnp.int32),
            pltpu.SemaphoreType.DMA((3, TPD)),
            pltpu.SemaphoreType.DMA((2, TPD)),
        ],
        name="fire",
        compiler_params=params(12),
        cost_estimate=pl.CostEstimate(
            flops=50_000_000, bytes_accessed=6_500_000, transcendentals=3_200_000
        ),
    )(owners, places, near(winds), *(far(a) for a in (level_set, fuel_load, spread_base)), *waits)


def final_kernel(inbox_ref, part_ref, out_ref, field, result, sems):
    inbox = inbox_ref[...]
    slots = inbox.shape[0]
    position = pltpu.roll(inbox, TA, 1).reshape(slots * 8, 128)
    values = inbox.reshape(slots * 8, 128)
    lane = iota(1, (slots * 8, 128)).astype(F32)
    valid = iota(0, (slots * 8, 128)) % 8 < TA
    hot = jnp.where(jnp.logical_and(valid, lane == position), 1.0, 0.0)
    total = lax.dot_general(
        hot, values, (((0,), (0,)), ((), ())),
        precision=lax.Precision.HIGHEST, preferred_element_type=F32,
    )
    field[...] = total[:CX]

    def copy(g):
        part = pl.ds(g * GROUP, GROUP)
        return pltpu.make_async_copy(result.at[part], out_ref.at[part], sems.at[g])

    def one(g, carry):
        for k in range(GROUP):
            z = g * GROUP + k
            height = jnp.full((8, 128), z, jnp.int32).astype(F32)
            gain = heat_gain * jnp.exp((height + 0.5) * (-4.0 / LZ))
            result[z] = part_ref[z] + field[...] * jnp.concatenate([gain] * (CX // 8), axis=0)
        copy(g).start()
        return carry

    lax.fori_loop(0, GROUPS, one, 0)
    for g in range(GROUPS):
        copy(g).wait()


def finish(inbox, part):
    return pl.pallas_call(
        final_kernel,
        in_specs=[LOCAL, LOCAL],
        out_specs=ANYWHERE,
        out_shape=jax.ShapeDtypeStruct((LZ, CX, CY), F32),
        scratch_shapes=[
            pltpu.VMEM((CX, CY), F32),
            pltpu.VMEM((LZ, CX, CY), F32),
            pltpu.SemaphoreType.DMA((GROUPS,)),
        ],
        name="finish",
        compiler_params=params(8),
        cost_estimate=pl.CostEstimate(flops=3_000_000, bytes_accessed=2_700_000, transcendentals=0),
    )(near(inbox), near(part))


def shifted(cells, axis, up):
    ends = lax.axis_size(axis) - 1
    pairs = [(i, i + 1) if up else (i + 1, i) for i in range(ends)]
    return lax.ppermute(cells, axis, pairs)


def exchange(cells):
    return lax.all_to_all(cells, "gx", split_axis=0, concat_axis=0, tiled=True)


def body(theta, wind_u, wind_v, level_set, fuel_load, spread_base, tile_owner, tile_place):
    peers = lax.axis_size("gx")
    block, up, down = wind_edges(wind_u, wind_v)
    low = shifted(up, "gy", True)
    high = shifted(down, "gy", False)
    packed = pack_winds(block, low, high, peers)
    winds = exchange(packed)

    first_x, last_x, first_y, last_y = theta_edges(low, theta)
    west = shifted(last_x, "gx", True)
    east = shifted(first_x, "gx", False)
    south = shifted(last_y, "gy", True)
    north = shifted(first_y, "gy", False)

    level_out, fuel_out, outbox = fire(
        tile_owner[0, 0], tile_place[0, 0], winds, level_set[0, 0], fuel_load[0, 0], spread_base[0, 0], peers,
        (west, east, south, north),
    )
    part = advect(theta, wind_u, wind_v, west, east, south, north)
    inbox = exchange(outbox)
    theta_next = finish(inbox, part)
    return (theta_next, level_out[None, None], fuel_out[None, None])


def solution(mesh):
    in_specs = (
        P(None, "gx", "gy"),
        P(None, "gx", "gy"),
        P(None, "gx", "gy"),
        P("gx", "gy", None, None, None),
        P("gx", "gy", None, None, None),
        P("gx", "gy", None, None, None),
        P("gx", "gy", None),
        P("gx", "gy", None),
    )
    out_specs = (
        P(None, "gx", "gy"),
        P("gx", "gy", None, None, None),
        P("gx", "gy", None, None, None),
    )
    return jax.shard_map(body, mesh=mesh, in_specs=in_specs, out_specs=out_specs, check_vma=False)
```

```python
import functools

import jax
import jax.numpy as jnp
from jax import lax
from jax.experimental import pallas as pl
from jax.experimental.pallas import tpu as pltpu
from jax.sharding import PartitionSpec as P

LZ = 80
TA = 4
R = 32
KSUB = 6
CAP = 2
TPD = 16
S = 128
CX = 64
CY = 128
ROWS = S // 8
RIM = 8
SIDES = (0, 1, -1)
WIND = 100
GROUP = 8
GROUPS = LZ // GROUP
SIDE = 2
AHEAD = 2

time_step = 0.03
diffusion = 0.15
burn_rate = 0.15
regular = 0.01
courant = 0.4
heat_gain = 2.0

F32 = jnp.float32
LOCAL = pl.BlockSpec(memory_space=pltpu.VMEM)
FAR = pl.BlockSpec(memory_space=pltpu.HBM)
ANYWHERE = pl.BlockSpec(memory_space=pl.ANY)
SCALARS = pl.BlockSpec(memory_space=pltpu.SMEM)


def iota(dim, shape=(8, 128)):
    return lax.broadcasted_iota(jnp.int32, shape, dim)


def near(cells):
    return pltpu.with_memory_space_constraint(cells, pltpu.VMEM)


def far(cells):
    return pltpu.with_memory_space_constraint(cells, pltpu.HBM)


def params(mib):
    return pltpu.CompilerParams(vmem_limit_bytes=mib * 1024 * 1024)


def ranks_of(owner_ref, count, peers):
    for d in range(peers):
        count[d] = 0
    ranks = []
    for t in range(TPD):
        owner = owner_ref[t]
        ranks.append(count[owner])
        count[owner] = ranks[t] + 1
    return ranks


def request_kernel(owner_ref, place_ref, out_ref, table, count):
    peers = out_ref.shape[0]
    for i in range((peers + 2) * CAP):
        table[i] = -1
    ranks = ranks_of(owner_ref, count, peers)
    for t in range(TPD):
        table[(owner_ref[t] + 1) * CAP + ranks[t]] = place_ref[t]
    lane = iota(1, (1, 128))
    for peer in range(peers):
        line = jnp.full((1, 128), -1, jnp.int32)
        for g, side in enumerate(SIDES):
            for r in range(CAP):
                line = jnp.where(lane == g * CAP + r, table[(peer + 1 + side) * CAP + r], line)
        out_ref[peer] = line


def make_requests(owners, places, peers):
    return pl.pallas_call(
        request_kernel,
        in_specs=[SCALARS, SCALARS],
        out_specs=LOCAL,
        out_shape=pltpu.VMEM((peers, 1, 128), jnp.int32),
        scratch_shapes=[pltpu.SMEM(((peers + 2) * CAP,), jnp.int32), pltpu.SMEM((peers,), jnp.int32)],
        name="make_requests",
        compiler_params=params(4),
    )(owners, places)


def edge_kernel(
    after_ref, theta_ref, u_ref, v_ref,
    block_ref, first_x_ref, last_x_ref, first_y_ref, last_y_ref, theta, sems, wind_sems,
):
    def copy(g):
        part = pl.ds(g * GROUP, GROUP)
        return pltpu.make_async_copy(theta_ref.at[part], theta.at[part], sems.at[g])

    winds = [
        pltpu.make_async_copy(ref.at[0], block_ref.at[c * CX : (c + 1) * CX], wind_sems.at[c])
        for c, ref in enumerate((u_ref, v_ref))
    ]
    for g in reversed(range(GROUPS)):
        copy(g).start()
    for wind in winds:
        wind.start()
    lane = iota(1, (CX, 128))

    def one(i, carry):
        first, last = carry
        g = GROUPS - 1 - i
        copy(g).wait()
        first = pltpu.roll(first, GROUP, 1)
        last = pltpu.roll(last, GROUP, 1)
        for k in range(GROUP):
            z = g * GROUP + k
            cells = theta[z]
            first_x_ref[pl.ds(z, 1)] = cells[0:1]
            last_x_ref[pl.ds(z, 1)] = cells[CX - 1 : CX]
            turned = pltpu.roll(cells, k + 1, 1)
            first = jnp.where(lane == k + 1, turned, first)
            last = jnp.where(lane == k, turned, last)
        return first, last

    zero = jnp.zeros((CX, 128), F32)
    first, last = lax.fori_loop(0, GROUPS, one, (zero, zero))
    for wind in winds:
        wind.wait()
    for c in range(2):
        cells = block_ref[c * CX : (c + 1) * CX]
        first = jnp.where(lane == WIND + c, pltpu.roll(cells, WIND + c, 1), first)
        last = jnp.where(lane == WIND + c, pltpu.roll(cells, WIND + c + 1, 1), last)
    first_y_ref[...] = first
    last_y_ref[...] = last


def make_edges(after, theta, wind_u, wind_v):
    row = pltpu.VMEM((LZ, 128), F32)
    column = pltpu.VMEM((CX, 128), F32)
    return pl.pallas_call(
        edge_kernel,
        in_specs=[ANYWHERE, FAR, FAR, FAR],
        out_specs=[LOCAL] * 5,
        out_shape=[pltpu.VMEM((2 * CX, 128), F32), row, row, column, column],
        scratch_shapes=[
            pltpu.VMEM((LZ, CX, CY), F32),
            pltpu.SemaphoreType.DMA((GROUPS,)),
            pltpu.SemaphoreType.DMA((2,)),
        ],
        name="edges",
        compiler_params=params(8),
        cost_estimate=pl.CostEstimate(flops=4_000_000, bytes_accessed=2_700_000, transcendentals=0),
    )(after, far(theta), far(wind_u), far(wind_v))


def cut_kernel(
    asked_ref, block_ref, south_ref, north_ref, first_x_ref, last_x_ref,
    out_ref, first_x_out, last_x_out, surface, edges,
):
    first_x_out[...] = first_x_ref[...]
    last_x_out[...] = last_x_ref[...]
    wide = iota(1, (CX, 128))
    lane = iota(1)
    blank = jnp.zeros((RIM, 128), F32)
    for c in range(2):
        low = jnp.broadcast_to(south_ref[:, WIND + c : WIND + c + 1], (CX, 128))
        high = jnp.broadcast_to(north_ref[:, WIND + c : WIND + c + 1], (CX, 128))
        surface[c, 0:RIM] = blank
        surface[c, RIM : RIM + CX] = block_ref[c * CX : (c + 1) * CX]
        surface[c, RIM + CX :] = blank
        edges[c, 0:RIM] = blank
        edges[c, RIM : RIM + CX] = jnp.where(wide % 8 == 0, low, high)
        edges[c, RIM + CX :] = blank
    tiles_y = CY // TA
    for source in range(out_ref.shape[0]):
        message = jnp.zeros((8, 128), F32)
        for g, side in enumerate(SIDES):
            for r in range(CAP):
                place = asked_ref[source, 0, g * CAP + r]
                y_own = jnp.bitwise_and(place, tiles_y - 1) * TA
                first = lax.shift_right_arithmetic(place, 5) * TA - 1 + side * CX
                first = jnp.where(place < 0, CX, jnp.clip(first, -RIM, CX)) + RIM
                begin = (g * CAP + r) * 16
                outside = jnp.where(y_own == 0, 0, jnp.where(y_own == CY - TA, TA + 1, 1000))
                for c in range(2):
                    at = begin + 8 * c
                    turn = jnp.bitwise_and(at + 1 - y_own, 127)
                    part = pltpu.roll(surface[c, pl.ds(first, 8), :], turn, 1)
                    part = jnp.where(lane == at + outside, edges[c, pl.ds(first, 8), :], part)
                    message = jnp.where(lane // 8 == at // 8, part, message)
        out_ref[source] = message


def cut_patches(asked, block, south, north, first_x, last_x):
    peers = asked.shape[0]
    row = pltpu.VMEM((LZ, 128), F32)
    rows = CX + 2 * RIM
    return pl.pallas_call(
        cut_kernel,
        in_specs=[SCALARS] + [LOCAL] * 5,
        out_specs=[LOCAL] * 3,
        out_shape=[pltpu.VMEM((peers, 8, 128), F32), row, row],
        scratch_shapes=[pltpu.VMEM((2, rows, 128), F32), pltpu.VMEM((2, rows, 128), F32)],
        name="cut_patches",
        compiler_params=params(4),
    )(asked, *(near(a) for a in (block, south, north, first_x, last_x)))


def advect_kernel(
    theta_ref, u_ref, v_ref, west_ref, east_ref, south_ref, north_ref, out_ref, theta, wind_u, wind_v, sems
):
    def copies(g):
        part = pl.ds(g * GROUP, GROUP)
        pairs = ((theta_ref, theta), (u_ref, wind_u), (v_ref, wind_v))
        return [
            pltpu.make_async_copy(source.at[part], target.at[part], sems.at[c, g])
            for c, (source, target) in enumerate(pairs)
        ]

    for g in range(GROUPS):
        for copy in copies(g):
            copy.start()
    lane = iota(1, (CX, 128))
    row = iota(0, (CX, 128))

    def one(g, carry):
        south_all, north_all = carry
        for copy in copies(g):
            copy.wait()
        def begin(k):
            t = theta[g * GROUP + k]
            rolled = [pltpu.roll(t, 1, 1), pltpu.roll(t, CY - 1, 1)]
            rims = [pltpu.roll(south_all, (128 - k) % 128, 1), pltpu.roll(north_all, 126 - k, 1)]
            return t, rolled, rims

        def end(k, begun):
            z = g * GROUP + k
            t, rolled, rims = begun
            u = wind_u[z]
            v = wind_v[z]
            west = jnp.where(row == 0, west_ref[pl.ds(z, 1)], pltpu.roll(t, 1, 0))
            east = jnp.where(row == CX - 1, east_ref[pl.ds(z, 1)], pltpu.roll(t, CX - 1, 0))
            south = jnp.where(lane == 0, rims[0], rolled[0])
            north = jnp.where(lane == CY - 1, rims[1], rolled[1])
            change = jnp.abs(u) * (t - jnp.where(u > 0, west, east)) + jnp.abs(v) * (
                t - jnp.where(v > 0, south, north)
            )
            out_ref[z] = t - courant * change

        begun = [begin(k) for k in range(AHEAD)]
        for k in range(GROUP):
            if k + AHEAD < GROUP:
                begun.append(begin(k + AHEAD))
            end(k, begun[k])
        return pltpu.roll(south_all, 128 - GROUP, 1), pltpu.roll(north_all, 128 - GROUP, 1)

    lax.fori_loop(0, GROUPS, one, (south_ref[...], north_ref[...]))


def advect(theta, wind_u, wind_v, *rims):
    whole = pltpu.VMEM((LZ, CX, CY), F32)
    return pl.pallas_call(
        advect_kernel,
        in_specs=[FAR] * 3 + [LOCAL] * 4,
        out_specs=LOCAL,
        out_shape=whole,
        scratch_shapes=[whole, whole, whole, pltpu.SemaphoreType.DMA((3, GROUPS))],
        name="advect",
        compiler_params=params(12),
        cost_estimate=pl.CostEstimate(flops=14_000_000, bytes_accessed=8_000_000, transcendentals=0),
    )(far(theta), far(wind_u), far(wind_v), *(near(a) for a in rims))


def fire_kernel(
    peers, waits, owner_ref, place_ref, winds_ref, level_ref, fuel_ref, base_ref, *rest
):
    (
        level_out, fuel_out, outbox, begins, slopes, heats,
        level_own, fuel_own, base_own, count, in_sems, out_sems,
    ) = rest[waits:]
    lane = iota(1)
    row = iota(0)

    def inputs(t):
        pairs = ((level_ref, level_own), (fuel_ref, fuel_own), (base_ref, base_own))
        return [
            pltpu.make_async_copy(source.at[t], target.at[t], in_sems.at[c, t])
            for c, (source, target) in enumerate(pairs)
        ]

    def results(t):
        pairs = ((level_own, level_out), (fuel_own, fuel_out))
        return [
            pltpu.make_async_copy(source.at[t], target.at[t], out_sems.at[c, t])
            for c, (source, target) in enumerate(pairs)
        ]

    for t in range(TPD):
        for copy in inputs(t):
            copy.start()

    tiles_y = CY // TA
    low_row = (row + 1) // 2
    low_lane = (lane + R // 2) // R
    part_row = jnp.where(row % 2 == 0, 0.5, 0.0) + 0.5 / R
    part_lane = (lane.astype(F32) + 0.5) / R + 0.5 - low_lane.astype(F32)

    ranks = ranks_of(owner_ref, count, peers)
    patches = []
    for t in range(TPD):
        owner = owner_ref[t]
        parts = []
        for g, side in enumerate(SIDES):
            begin = (g * CAP + ranks[t]) * 16
            inside = jnp.logical_and(owner >= side, owner - side < peers)
            part = winds_ref[jnp.clip(owner - side, 0, peers - 1)]
            part = jnp.where(inside, part, 0.0)
            parts.append([pltpu.roll(part, jnp.bitwise_and(-begin - 8 * c, 127), 1) for c in range(2)])
        for c in range(2):
            patches.append(parts[0][c] + parts[1][c] + parts[2][c])
    left = [jnp.take_along_axis(p, low_lane, axis=1) for p in patches]
    right = [jnp.take_along_axis(p, low_lane + 1, axis=1) for p in patches]
    fine = [p + (q - p) * part_lane for p, q in zip(left, right)]
    below = [jnp.take_along_axis(p, low_row, axis=0) for p in fine]
    above = [jnp.take_along_axis(p, low_row + 1, axis=0) for p in fine]
    for i, (p, q) in enumerate(zip(below, above)):
        begins[i] = p + (q - p) * part_row
        slopes[i] = (q - p) * (1.0 / R)

    def burn(t):
        begin = [begins[2 * t + c] for c in range(2)]
        slope = [slopes[2 * t + c] for c in range(2)]
        level = [level_own[t, pl.ds(k, 8, stride=ROWS), :] for k in range(ROWS)]
        fuel = [fuel_own[t, pl.ds(k, 8, stride=ROWS), :] for k in range(ROWS)]
        heat = sum(fuel[1:], fuel[0])
        rate = [base_own[t, pl.ds(k, 8, stride=ROWS), :] * (0.5 * time_step) for k in range(ROWS)]
        wind = [[begin[c] + slope[c] * float(k) for k in range(ROWS)] for c in range(2)]
        yield
        for _ in range(KSUB):
            before = jnp.where(row == 0, level[0], pltpu.roll(level[-1], 1, 0))
            after = jnp.where(row == 7, level[-1], pltpu.roll(level[0], 7, 0))
            rimmed = [before, *level, after]
            south = [jnp.where(lane == 0, cell, pltpu.roll(cell, 1, 1)) for cell in level]
            north = [jnp.where(lane == S - 1, cell, pltpu.roll(cell, S - 1, 1)) for cell in level]
            yield
            new = []
            for k in range(ROWS):
                cell = rimmed[k + 1]
                west, east = rimmed[k], rimmed[k + 2]
                dx = east - west
                dy = north[k] - south[k]
                square = dx * dx + dy * dy + 4.0 * regular
                length = square * lax.rsqrt(square)
                move = jnp.maximum(length + (wind[0][k] * dx + wind[1][k] * dy), 0.0)
                around = (east + west) + (north[k] + south[k])
                cell = cell * (1.0 - 4.0 * diffusion) + around * diffusion - rate[k] * move
                fuel[k] = fuel[k] * ((1.0 - 0.5 * burn_rate) + (0.5 * burn_rate) * jnp.tanh(cell))
                new.append(cell)
            level = new
        yield
        for k in range(ROWS):
            level_own[t, pl.ds(k, 8, stride=ROWS), :] = level[k]
            fuel_own[t, pl.ds(k, 8, stride=ROWS), :] = fuel[k]
        heats[t] = (heat - sum(fuel[1:], fuel[0])) * (1.0 / (R * R))

    def some(i, carry):
        tiles = [i * SIDE + j for j in range(SIDE)]
        for t in tiles:
            for copy in inputs(t):
                copy.wait()
        works = [burn(t) for t in tiles]
        while works:
            works = [w for w in works if next(w, works) is None]
        for t in tiles:
            for copy in results(t):
                copy.start()
        return carry

    lax.fori_loop(0, TPD // SIDE, some, 0)

    for d in range(peers * CAP):
        outbox[d] = jnp.where(row < TA, 0.0, -1.0)
    pairs = [heats[t] for t in range(TPD)]
    pairs = [h + pltpu.roll(h, 7, 0) for h in pairs]
    pairs = [jnp.take_along_axis(h, jnp.minimum(2 * row, 7), axis=0) for h in pairs]
    sums = [
        [jnp.sum(jnp.where(lane // R == b, h, 0.0), axis=1, keepdims=True) for b in range(TA)] for h in pairs
    ]
    for t in range(TPD):
        place = place_ref[t]
        x_own = place // tiles_y * TA
        y_own = lax.rem(place, tiles_y) * TA
        message = jnp.where(row < TA, 0.0, (x_own + row - TA).astype(F32))
        for b in range(TA):
            message = jnp.where(jnp.logical_and(row < TA, lane == y_own + b), sums[t][b], message)
        outbox[owner_ref[t] * CAP + ranks[t]] = message
    for t in range(TPD):
        for copy in results(t):
            copy.wait()


def fire(owners, places, winds, level_set, fuel_load, spread_base, peers, waits):
    tiles = (TPD, S, S)
    return pl.pallas_call(
        functools.partial(fire_kernel, peers, len(waits)),
        in_specs=[SCALARS, SCALARS, LOCAL] + [FAR] * 3 + [ANYWHERE] * len(waits),
        out_specs=[ANYWHERE, ANYWHERE, LOCAL],
        out_shape=[
            jax.ShapeDtypeStruct(tiles, F32),
            jax.ShapeDtypeStruct(tiles, F32),
            pltpu.VMEM((peers * CAP, 8, 128), F32),
        ],
        scratch_shapes=[
            pltpu.VMEM((2 * TPD, 8, 128), F32),
            pltpu.VMEM((2 * TPD, 8, 128), F32),
            pltpu.VMEM((TPD, 8, 128), F32),
            pltpu.VMEM(tiles, F32),
            pltpu.VMEM(tiles, F32),
            pltpu.VMEM(tiles, F32),
            pltpu.SMEM((peers,), jnp.int32),
            pltpu.SemaphoreType.DMA((3, TPD)),
            pltpu.SemaphoreType.DMA((2, TPD)),
        ],
        name="fire",
        compiler_params=params(12),
        cost_estimate=pl.CostEstimate(
            flops=50_000_000, bytes_accessed=6_500_000, transcendentals=3_200_000
        ),
    )(owners, places, near(winds), *(far(a) for a in (level_set, fuel_load, spread_base)), *waits)


def final_kernel(inbox_ref, part_ref, out_ref, field, result, sems):
    inbox = inbox_ref[...]
    slots = inbox.shape[0]
    position = pltpu.roll(inbox, TA, 1).reshape(slots * 8, 128)
    values = inbox.reshape(slots * 8, 128)
    lane = iota(1, (slots * 8, 128)).astype(F32)
    valid = iota(0, (slots * 8, 128)) % 8 < TA
    hot = jnp.where(jnp.logical_and(valid, lane == position), 1.0, 0.0)
    total = lax.dot_general(
        hot, values, (((0,), (0,)), ((), ())),
        precision=lax.Precision.HIGHEST, preferred_element_type=F32,
    )
    field[...] = total[:CX]

    def copy(g):
        part = pl.ds(g * GROUP, GROUP)
        return pltpu.make_async_copy(result.at[part], out_ref.at[part], sems.at[g])

    def one(g, carry):
        for k in range(GROUP):
            z = g * GROUP + k
            height = jnp.full((8, 128), z, jnp.int32).astype(F32)
            gain = heat_gain * jnp.exp((height + 0.5) * (-4.0 / LZ))
            result[z] = part_ref[z] + field[...] * jnp.concatenate([gain] * (CX // 8), axis=0)
        copy(g).start()
        return carry

    lax.fori_loop(0, GROUPS, one, 0)
    for g in range(GROUPS):
        copy(g).wait()


def finish(inbox, part):
    return pl.pallas_call(
        final_kernel,
        in_specs=[LOCAL, LOCAL],
        out_specs=ANYWHERE,
        out_shape=jax.ShapeDtypeStruct((LZ, CX, CY), F32),
        scratch_shapes=[
            pltpu.VMEM((CX, CY), F32),
            pltpu.VMEM((LZ, CX, CY), F32),
            pltpu.SemaphoreType.DMA((GROUPS,)),
        ],
        name="finish",
        compiler_params=params(8),
        cost_estimate=pl.CostEstimate(flops=3_000_000, bytes_accessed=2_700_000, transcendentals=0),
    )(near(inbox), near(part))


def shifted(cells, axis, up):
    ends = lax.axis_size(axis) - 1
    pairs = [(i, i + 1) if up else (i + 1, i) for i in range(ends)]
    return lax.ppermute(cells, axis, pairs)


def exchange(cells):
    return lax.all_to_all(cells, "gx", split_axis=0, concat_axis=0, tiled=True)


def body(theta, wind_u, wind_v, level_set, fuel_load, spread_base, tile_owner, tile_place):
    peers = lax.axis_size("gx")
    owners, places = tile_owner[0, 0], tile_place[0, 0]
    requests = make_requests(owners, places, peers)
    asked = exchange(requests)

    block, first_x, last_x, first_y, last_y = make_edges(requests, theta, wind_u, wind_v)
    south = shifted(last_y, "gy", True)
    north = shifted(first_y, "gy", False)

    patches, first_x, last_x = cut_patches(asked, block, south, north, first_x, last_x)
    winds = exchange(patches)
    west = shifted(last_x, "gx", True)
    east = shifted(first_x, "gx", False)

    level_out, fuel_out, outbox = fire(
        owners, places, winds, level_set[0, 0], fuel_load[0, 0], spread_base[0, 0], peers, ()
    )
    part = advect(theta, wind_u, wind_v, west, east, south, north)
    inbox = exchange(outbox)
    theta_next = finish(inbox, part)
    return (theta_next, level_out[None, None], fuel_out[None, None])


def solution(mesh):
    in_specs = (
        P(None, "gx", "gy"),
        P(None, "gx", "gy"),
        P(None, "gx", "gy"),
        P("gx", "gy", None, None, None),
        P("gx", "gy", None, None, None),
        P("gx", "gy", None, None, None),
        P("gx", "gy", None),
        P("gx", "gy", None),
    )
    out_specs = (
        P(None, "gx", "gy"),
        P("gx", "gy", None, None, None),
        P("gx", "gy", None, None, None),
    )
    return jax.shard_map(body, mesh=mesh, in_specs=in_specs, out_specs=out_specs, check_vma=False)
```

```python
import functools

import jax
import jax.numpy as jnp
from jax import lax
from jax.experimental import pallas as pl
from jax.experimental.pallas import tpu as pltpu
from jax.sharding import PartitionSpec as P

LZ = 80
TA = 4
R = 32
KSUB = 6
CAP = 2
TPD = 16
S = 128
CX = 64
CY = 128
ROWS = S // 8
RIM = 8
SIDES = (0, 1, -1)
WIND = 100
GROUP = 8
GROUPS = LZ // GROUP
SIDE = 2
AHEAD = 2

time_step = 0.03
diffusion = 0.15
burn_rate = 0.15
regular = 0.01
courant = 0.4
heat_gain = 2.0

F32 = jnp.float32
LOCAL = pl.BlockSpec(memory_space=pltpu.VMEM)
FAR = pl.BlockSpec(memory_space=pltpu.HBM)
ANYWHERE = pl.BlockSpec(memory_space=pl.ANY)
SCALARS = pl.BlockSpec(memory_space=pltpu.SMEM)


def iota(dim, shape=(8, 128)):
    return lax.broadcasted_iota(jnp.int32, shape, dim)


def near(cells):
    return pltpu.with_memory_space_constraint(cells, pltpu.VMEM)


def far(cells):
    return pltpu.with_memory_space_constraint(cells, pltpu.HBM)


def params(mib):
    return pltpu.CompilerParams(vmem_limit_bytes=mib * 1024 * 1024)


def to_scalars(refs, scalars, sems):
    copies = [pltpu.make_async_copy(ref, own, sems.at[c]) for c, (ref, own) in enumerate(zip(refs, scalars))]
    for copy in copies:
        copy.start()
    for copy in copies:
        copy.wait()


def ranks_of(owner_ref, count, peers):
    for d in range(peers):
        count[d] = 0
    ranks = []
    for t in range(TPD):
        owner = owner_ref[t]
        ranks.append(count[owner])
        count[owner] = ranks[t] + 1
    return ranks


def request_kernel(owner_far, place_far, out_ref, owner_ref, place_ref, table, count, sems):
    to_scalars((owner_far, place_far), (owner_ref, place_ref), sems)
    peers = out_ref.shape[0]
    for i in range((peers + 2) * CAP):
        table[i] = -1
    ranks = ranks_of(owner_ref, count, peers)
    for t in range(TPD):
        table[(owner_ref[t] + 1) * CAP + ranks[t]] = place_ref[t]
    lane = iota(1, (1, 128))
    for peer in range(peers):
        line = jnp.full((1, 128), -1, jnp.int32)
        for g, side in enumerate(SIDES):
            for r in range(CAP):
                line = jnp.where(lane == g * CAP + r, table[(peer + 1 + side) * CAP + r], line)
        out_ref[peer] = jnp.broadcast_to(line, (8, 128))


def make_requests(owners, places, peers):
    return pl.pallas_call(
        request_kernel,
        in_specs=[FAR, FAR],
        out_specs=LOCAL,
        out_shape=pltpu.VMEM((peers, 8, 128), jnp.int32),
        scratch_shapes=[
            pltpu.SMEM((TPD,), jnp.int32),
            pltpu.SMEM((TPD,), jnp.int32),
            pltpu.SMEM(((peers + 2) * CAP,), jnp.int32),
            pltpu.SMEM((peers,), jnp.int32),
            pltpu.SemaphoreType.DMA((2,)),
        ],
        name="make_requests",
        compiler_params=params(4),
    )(far(owners), far(places))


def place_on(axis):
    index = lax.axis_index(axis)
    even = lax.rem(index, 2) == 0
    return even, jnp.logical_or(index == 0, index == lax.axis_size(axis) - 1)


def edge_kernel(
    after_ref, theta_ref, u_ref, v_ref,
    block_ref, one_x_ref, two_x_ref, one_y_ref, two_y_ref, theta, sems, wind_sems,
):
    even_x, wraps_x = place_on("gx")
    even_y, wraps_y = place_on("gy")

    def copy(g):
        part = pl.ds(g * GROUP, GROUP)
        return pltpu.make_async_copy(theta_ref.at[part], theta.at[part], sems.at[g])

    winds = [
        pltpu.make_async_copy(ref.at[0], block_ref.at[c * CX : (c + 1) * CX], wind_sems.at[c])
        for c, ref in enumerate((u_ref, v_ref))
    ]
    for g in reversed(range(GROUPS)):
        copy(g).start()
    for wind in winds:
        wind.start()
    lane = iota(1, (CX, 128))

    def one(i, carry):
        first, last = carry
        g = GROUPS - 1 - i
        copy(g).wait()
        first = pltpu.roll(first, GROUP, 1)
        last = pltpu.roll(last, GROUP, 1)
        for k in range(GROUP):
            z = g * GROUP + k
            cells = theta[z]
            low, high = cells[0:1], cells[CX - 1 : CX]
            one_x_ref[pl.ds(z, 1)] = jnp.where(even_x, high, low)
            two_x_ref[pl.ds(z, 1)] = jnp.where(wraps_x, 0.0, jnp.where(even_x, low, high))
            turned = pltpu.roll(cells, k + 1, 1)
            first = jnp.where(lane == k + 1, turned, first)
            last = jnp.where(lane == k, turned, last)
        return first, last

    zero = jnp.zeros((CX, 128), F32)
    first, last = lax.fori_loop(0, GROUPS, one, (zero, zero))
    for wind in winds:
        wind.wait()
    for c in range(2):
        cells = block_ref[c * CX : (c + 1) * CX]
        first = jnp.where(lane == WIND + c, pltpu.roll(cells, WIND + c, 1), first)
        last = jnp.where(lane == WIND + c, pltpu.roll(cells, WIND + c + 1, 1), last)
    one_y_ref[...] = jnp.where(even_y, last, first)
    two_y_ref[...] = jnp.where(wraps_y, 0.0, jnp.where(even_y, first, last))


def make_edges(after, theta, wind_u, wind_v):
    row = pltpu.VMEM((LZ, 128), F32)
    column = pltpu.VMEM((CX, 128), F32)
    return pl.pallas_call(
        edge_kernel,
        in_specs=[ANYWHERE, FAR, FAR, FAR],
        out_specs=[LOCAL] * 5,
        out_shape=[pltpu.VMEM((2 * CX, 128), F32), row, row, column, column],
        scratch_shapes=[
            pltpu.VMEM((LZ, CX, CY), F32),
            pltpu.SemaphoreType.DMA((GROUPS,)),
            pltpu.SemaphoreType.DMA((2,)),
        ],
        name="edges",
        compiler_params=params(8),
        cost_estimate=pl.CostEstimate(flops=4_000_000, bytes_accessed=2_700_000, transcendentals=0),
    )(after, far(theta), far(wind_u), far(wind_v))


def cut_kernel(
    asked_far, block_ref, one_y_ref, two_y_ref, one_x_ref, two_x_ref,
    out_ref, one_x_out, two_x_out, surface, edges, asked_ref, sem,
):
    copy = pltpu.make_async_copy(asked_far.at[:, 0:1], asked_ref, sem)
    copy.start()
    one_x_out[...] = one_x_ref[...]
    two_x_out[...] = two_x_ref[...]
    even, _ = place_on("gy")
    south = jnp.where(even, two_y_ref[...], one_y_ref[...])
    north = jnp.where(even, one_y_ref[...], two_y_ref[...])
    wide = iota(1, (CX, 128))
    lane = iota(1)
    blank = jnp.zeros((RIM, 128), F32)
    for c in range(2):
        low = jnp.broadcast_to(south[:, WIND + c : WIND + c + 1], (CX, 128))
        high = jnp.broadcast_to(north[:, WIND + c : WIND + c + 1], (CX, 128))
        surface[c, 0:RIM] = blank
        surface[c, RIM : RIM + CX] = block_ref[c * CX : (c + 1) * CX]
        surface[c, RIM + CX :] = blank
        edges[c, 0:RIM] = blank
        edges[c, RIM : RIM + CX] = jnp.where(wide % 8 == 0, low, high)
        edges[c, RIM + CX :] = blank
    copy.wait()
    tiles_y = CY // TA
    for source in range(out_ref.shape[0]):
        message = jnp.zeros((8, 128), F32)
        for g, side in enumerate(SIDES):
            for r in range(CAP):
                place = asked_ref[source, 0, g * CAP + r]
                y_own = jnp.bitwise_and(place, tiles_y - 1) * TA
                first = lax.shift_right_arithmetic(place, 5) * TA - 1 + side * CX
                first = jnp.where(place < 0, CX, jnp.clip(first, -RIM, CX)) + RIM
                begin = (g * CAP + r) * 16
                outside = jnp.where(y_own == 0, 0, jnp.where(y_own == CY - TA, TA + 1, 1000))
                for c in range(2):
                    at = begin + 8 * c
                    turn = jnp.bitwise_and(at + 1 - y_own, 127)
                    part = pltpu.roll(surface[c, pl.ds(first, 8), :], turn, 1)
                    part = jnp.where(lane == at + outside, edges[c, pl.ds(first, 8), :], part)
                    message = jnp.where(lane // 8 == at // 8, part, message)
        out_ref[source] = message


def cut_patches(asked, block, one_y, two_y, one_x, two_x):
    peers = asked.shape[0]
    row = pltpu.VMEM((LZ, 128), F32)
    rows = CX + 2 * RIM
    return pl.pallas_call(
        cut_kernel,
        in_specs=[LOCAL] * 6,
        out_specs=[LOCAL] * 3,
        out_shape=[pltpu.VMEM((peers, 8, 128), F32), row, row],
        scratch_shapes=[
            pltpu.VMEM((2, rows, 128), F32),
            pltpu.VMEM((2, rows, 128), F32),
            pltpu.SMEM((peers, 1, 128), jnp.int32),
            pltpu.SemaphoreType.DMA(()),
        ],
        name="cut_patches",
        compiler_params=params(4),
    )(*(near(a) for a in (asked, block, one_y, two_y, one_x, two_x)))


def advect_kernel(
    theta_ref, u_ref, v_ref, one_x_ref, two_x_ref, one_y_ref, two_y_ref,
    out_ref, theta, wind_u, wind_v, west_ref, east_ref, sems,
):
    def copies(g):
        part = pl.ds(g * GROUP, GROUP)
        pairs = ((theta_ref, theta), (u_ref, wind_u), (v_ref, wind_v))
        return [
            pltpu.make_async_copy(source.at[part], target.at[part], sems.at[c, g])
            for c, (source, target) in enumerate(pairs)
        ]

    for g in range(GROUPS):
        for copy in copies(g):
            copy.start()
    even, _ = place_on("gx")
    west_ref[...] = jnp.where(even, two_x_ref[...], one_x_ref[...])
    east_ref[...] = jnp.where(even, one_x_ref[...], two_x_ref[...])
    even, _ = place_on("gy")
    south = jnp.where(even, two_y_ref[...], one_y_ref[...])
    north = jnp.where(even, one_y_ref[...], two_y_ref[...])
    lane = iota(1, (CX, 128))
    row = iota(0, (CX, 128))

    def one(g, carry):
        south_all, north_all = carry
        for copy in copies(g):
            copy.wait()
        def begin(k):
            t = theta[g * GROUP + k]
            rolled = [pltpu.roll(t, 1, 1), pltpu.roll(t, CY - 1, 1)]
            rims = [pltpu.roll(south_all, (128 - k) % 128, 1), pltpu.roll(north_all, 126 - k, 1)]
            return t, rolled, rims

        def end(k, begun):
            z = g * GROUP + k
            t, rolled, rims = begun
            u = wind_u[z]
            v = wind_v[z]
            west = jnp.where(row == 0, west_ref[pl.ds(z, 1)], pltpu.roll(t, 1, 0))
            east = jnp.where(row == CX - 1, east_ref[pl.ds(z, 1)], pltpu.roll(t, CX - 1, 0))
            south = jnp.where(lane == 0, rims[0], rolled[0])
            north = jnp.where(lane == CY - 1, rims[1], rolled[1])
            change = jnp.abs(u) * (t - jnp.where(u > 0, west, east)) + jnp.abs(v) * (
                t - jnp.where(v > 0, south, north)
            )
            out_ref[z] = t - courant * change

        begun = [begin(k) for k in range(AHEAD)]
        for k in range(GROUP):
            if k + AHEAD < GROUP:
                begun.append(begin(k + AHEAD))
            end(k, begun[k])
        return pltpu.roll(south_all, 128 - GROUP, 1), pltpu.roll(north_all, 128 - GROUP, 1)

    lax.fori_loop(0, GROUPS, one, (south, north))


def advect(theta, wind_u, wind_v, *rims):
    whole = pltpu.VMEM((LZ, CX, CY), F32)
    return pl.pallas_call(
        advect_kernel,
        in_specs=[FAR] * 3 + [LOCAL] * 4,
        out_specs=LOCAL,
        out_shape=whole,
        scratch_shapes=[
            whole,
            whole,
            whole,
            pltpu.VMEM((LZ, 128), F32),
            pltpu.VMEM((LZ, 128), F32),
            pltpu.SemaphoreType.DMA((3, GROUPS)),
        ],
        name="advect",
        compiler_params=params(12),
        cost_estimate=pl.CostEstimate(flops=14_000_000, bytes_accessed=8_000_000, transcendentals=0),
    )(far(theta), far(wind_u), far(wind_v), *(near(a) for a in rims))


def fire_kernel(
    peers, waits, owner_far, place_far, winds_ref, level_ref, fuel_ref, base_ref, *rest
):
    (
        level_out, fuel_out, outbox, begins, slopes, heats,
        level_own, fuel_own, base_own, owner_ref, place_ref, count, scalar_sems, in_sems, out_sems,
    ) = rest[waits:]
    lane = iota(1)
    row = iota(0)

    def inputs(t):
        pairs = ((level_ref, level_own), (fuel_ref, fuel_own), (base_ref, base_own))
        return [
            pltpu.make_async_copy(source.at[t], target.at[t], in_sems.at[c, t])
            for c, (source, target) in enumerate(pairs)
        ]

    def results(t):
        pairs = ((level_own, level_out), (fuel_own, fuel_out))
        return [
            pltpu.make_async_copy(source.at[t], target.at[t], out_sems.at[c, t])
            for c, (source, target) in enumerate(pairs)
        ]

    to_scalars((owner_far, place_far), (owner_ref, place_ref), scalar_sems)
    for t in range(TPD):
        for copy in inputs(t):
            copy.start()

    tiles_y = CY // TA
    low_row = (row + 1) // 2
    low_lane = (lane + R // 2) // R
    part_row = jnp.where(row % 2 == 0, 0.5, 0.0) + 0.5 / R
    part_lane = (lane.astype(F32) + 0.5) / R + 0.5 - low_lane.astype(F32)

    ranks = ranks_of(owner_ref, count, peers)
    patches = []
    for t in range(TPD):
        owner = owner_ref[t]
        parts = []
        for g, side in enumerate(SIDES):
            begin = (g * CAP + ranks[t]) * 16
            inside = jnp.logical_and(owner >= side, owner - side < peers)
            part = winds_ref[jnp.clip(owner - side, 0, peers - 1)]
            part = jnp.where(inside, part, 0.0)
            parts.append([pltpu.roll(part, jnp.bitwise_and(-begin - 8 * c, 127), 1) for c in range(2)])
        for c in range(2):
            patches.append(parts[0][c] + parts[1][c] + parts[2][c])
    left = [jnp.take_along_axis(p, low_lane, axis=1) for p in patches]
    right = [jnp.take_along_axis(p, low_lane + 1, axis=1) for p in patches]
    fine = [p + (q - p) * part_lane for p, q in zip(left, right)]
    below = [jnp.take_along_axis(p, low_row, axis=0) for p in fine]
    above = [jnp.take_along_axis(p, low_row + 1, axis=0) for p in fine]
    for i, (p, q) in enumerate(zip(below, above)):
        begins[i] = p + (q - p) * part_row
        slopes[i] = (q - p) * (1.0 / R)

    def burn(t):
        begin = [begins[2 * t + c] for c in range(2)]
        slope = [slopes[2 * t + c] for c in range(2)]
        level = [level_own[t, pl.ds(k, 8, stride=ROWS), :] for k in range(ROWS)]
        fuel = [fuel_own[t, pl.ds(k, 8, stride=ROWS), :] for k in range(ROWS)]
        heat = sum(fuel[1:], fuel[0])
        rate = [base_own[t, pl.ds(k, 8, stride=ROWS), :] * (0.5 * time_step) for k in range(ROWS)]
        wind = [[begin[c] + slope[c] * float(k) for k in range(ROWS)] for c in range(2)]
        yield
        for _ in range(KSUB):
            before = jnp.where(row == 0, level[0], pltpu.roll(level[-1], 1, 0))
            after = jnp.where(row == 7, level[-1], pltpu.roll(level[0], 7, 0))
            rimmed = [before, *level, after]
            south = [jnp.where(lane == 0, cell, pltpu.roll(cell, 1, 1)) for cell in level]
            north = [jnp.where(lane == S - 1, cell, pltpu.roll(cell, S - 1, 1)) for cell in level]
            yield
            new = []
            for k in range(ROWS):
                cell = rimmed[k + 1]
                west, east = rimmed[k], rimmed[k + 2]
                dx = east - west
                dy = north[k] - south[k]
                square = dx * dx + dy * dy + 4.0 * regular
                length = square * lax.rsqrt(square)
                move = jnp.maximum(length + (wind[0][k] * dx + wind[1][k] * dy), 0.0)
                around = (east + west) + (north[k] + south[k])
                cell = cell * (1.0 - 4.0 * diffusion) + around * diffusion - rate[k] * move
                fuel[k] = fuel[k] * ((1.0 - 0.5 * burn_rate) + (0.5 * burn_rate) * jnp.tanh(cell))
                new.append(cell)
            level = new
        yield
        for k in range(ROWS):
            level_own[t, pl.ds(k, 8, stride=ROWS), :] = level[k]
            fuel_own[t, pl.ds(k, 8, stride=ROWS), :] = fuel[k]
        heats[t] = (heat - sum(fuel[1:], fuel[0])) * (1.0 / (R * R))

    def some(i, carry):
        tiles = [i * SIDE + j for j in range(SIDE)]
        for t in tiles:
            for copy in inputs(t):
                copy.wait()
        works = [burn(t) for t in tiles]
        while works:
            works = [w for w in works if next(w, works) is None]
        for t in tiles:
            for copy in results(t):
                copy.start()
        return carry

    lax.fori_loop(0, TPD // SIDE, some, 0)

    for d in range(peers * CAP):
        outbox[d] = jnp.where(row < TA, 0.0, -1.0)
    pairs = [heats[t] for t in range(TPD)]
    pairs = [h + pltpu.roll(h, 7, 0) for h in pairs]
    pairs = [jnp.take_along_axis(h, jnp.minimum(2 * row, 7), axis=0) for h in pairs]
    sums = [
        [jnp.sum(jnp.where(lane // R == b, h, 0.0), axis=1, keepdims=True) for b in range(TA)] for h in pairs
    ]
    for t in range(TPD):
        place = place_ref[t]
        x_own = place // tiles_y * TA
        y_own = lax.rem(place, tiles_y) * TA
        message = jnp.where(row < TA, 0.0, (x_own + row - TA).astype(F32))
        for b in range(TA):
            message = jnp.where(jnp.logical_and(row < TA, lane == y_own + b), sums[t][b], message)
        outbox[owner_ref[t] * CAP + ranks[t]] = message
    for t in range(TPD):
        for copy in results(t):
            copy.wait()


def fire(owners, places, winds, level_set, fuel_load, spread_base, peers, waits):
    tiles = (TPD, S, S)
    return pl.pallas_call(
        functools.partial(fire_kernel, peers, len(waits)),
        in_specs=[FAR, FAR, LOCAL] + [FAR] * 3 + [ANYWHERE] * len(waits),
        out_specs=[ANYWHERE, ANYWHERE, LOCAL],
        out_shape=[
            jax.ShapeDtypeStruct(tiles, F32),
            jax.ShapeDtypeStruct(tiles, F32),
            pltpu.VMEM((peers * CAP, 8, 128), F32),
        ],
        scratch_shapes=[
            pltpu.VMEM((2 * TPD, 8, 128), F32),
            pltpu.VMEM((2 * TPD, 8, 128), F32),
            pltpu.VMEM((TPD, 8, 128), F32),
            pltpu.VMEM(tiles, F32),
            pltpu.VMEM(tiles, F32),
            pltpu.VMEM(tiles, F32),
            pltpu.SMEM((TPD,), jnp.int32),
            pltpu.SMEM((TPD,), jnp.int32),
            pltpu.SMEM((peers,), jnp.int32),
            pltpu.SemaphoreType.DMA((2,)),
            pltpu.SemaphoreType.DMA((3, TPD)),
            pltpu.SemaphoreType.DMA((2, TPD)),
        ],
        name="fire",
        compiler_params=params(12),
        cost_estimate=pl.CostEstimate(
            flops=50_000_000, bytes_accessed=6_500_000, transcendentals=3_200_000
        ),
    )(far(owners), far(places), near(winds), *(far(a) for a in (level_set, fuel_load, spread_base)), *waits)


def final_kernel(inbox_ref, part_ref, out_ref, field, result, sems):
    inbox = inbox_ref[...]
    slots = inbox.shape[0]
    position = pltpu.roll(inbox, TA, 1).reshape(slots * 8, 128)
    values = inbox.reshape(slots * 8, 128)
    lane = iota(1, (slots * 8, 128)).astype(F32)
    valid = iota(0, (slots * 8, 128)) % 8 < TA
    hot = jnp.where(jnp.logical_and(valid, lane == position), 1.0, 0.0)
    total = lax.dot_general(
        hot, values, (((0,), (0,)), ((), ())),
        precision=lax.Precision.HIGHEST, preferred_element_type=F32,
    )
    field[...] = total[:CX]

    def copy(g):
        part = pl.ds(g * GROUP, GROUP)
        return pltpu.make_async_copy(result.at[part], out_ref.at[part], sems.at[g])

    def one(g, carry):
        for k in range(GROUP):
            z = g * GROUP + k
            height = jnp.full((8, 128), z, jnp.int32).astype(F32)
            gain = heat_gain * jnp.exp((height + 0.5) * (-4.0 / LZ))
            result[z] = part_ref[z] + field[...] * jnp.concatenate([gain] * (CX // 8), axis=0)
        copy(g).start()
        return carry

    lax.fori_loop(0, GROUPS, one, 0)
    for g in range(GROUPS):
        copy(g).wait()


def finish(inbox, part):
    return pl.pallas_call(
        final_kernel,
        in_specs=[LOCAL, LOCAL],
        out_specs=ANYWHERE,
        out_shape=jax.ShapeDtypeStruct((LZ, CX, CY), F32),
        scratch_shapes=[
            pltpu.VMEM((CX, CY), F32),
            pltpu.VMEM((LZ, CX, CY), F32),
            pltpu.SemaphoreType.DMA((GROUPS,)),
        ],
        name="finish",
        compiler_params=params(8),
        cost_estimate=pl.CostEstimate(flops=3_000_000, bytes_accessed=2_700_000, transcendentals=0),
    )(near(inbox), near(part))


def swapped(one, two, axis):
    count = lax.axis_size(axis)
    pairs = [(i, i ^ 1) for i in range(count)]
    others = [((i + 1) % count, ((i ^ 1) + 1) % count) for i in range(count)]
    return lax.ppermute(one, axis, pairs), lax.ppermute(two, axis, others)


def exchange(cells):
    return lax.all_to_all(cells, "gx", split_axis=0, concat_axis=0, tiled=True)


def body(theta, wind_u, wind_v, level_set, fuel_load, spread_base, tile_owner, tile_place):
    peers = lax.axis_size("gx")
    owners, places = tile_owner[0, 0], tile_place[0, 0]
    requests = make_requests(owners, places, peers)
    asked = exchange(requests)

    block, one_x, two_x, one_y, two_y = make_edges(requests, theta, wind_u, wind_v)
    rims_y = swapped(one_y, two_y, "gy")

    patches, one_x, two_x = cut_patches(asked, block, *rims_y, one_x, two_x)
    winds = exchange(patches)
    rims_x = swapped(one_x, two_x, "gx")

    level_out, fuel_out, outbox = fire(
        owners, places, winds, level_set[0, 0], fuel_load[0, 0], spread_base[0, 0], peers, rims_x
    )
    part = advect(theta, wind_u, wind_v, *rims_x, *rims_y)
    inbox = exchange(outbox)
    theta_next = finish(inbox, part)
    return (theta_next, level_out[None, None], fuel_out[None, None])


def solution(mesh):
    in_specs = (
        P(None, "gx", "gy"),
        P(None, "gx", "gy"),
        P(None, "gx", "gy"),
        P("gx", "gy", None, None, None),
        P("gx", "gy", None, None, None),
        P("gx", "gy", None, None, None),
        P("gx", "gy", None),
        P("gx", "gy", None),
    )
    out_specs = (
        P(None, "gx", "gy"),
        P("gx", "gy", None, None, None),
        P("gx", "gy", None, None, None),
    )
    return jax.shard_map(body, mesh=mesh, in_specs=in_specs, out_specs=out_specs, check_vma=False)
```

```python
import functools

import jax
import jax.numpy as jnp
from jax import lax
from jax.experimental import pallas as pl
from jax.experimental.pallas import tpu as pltpu
from jax.sharding import PartitionSpec as P

LZ = 80
TA = 4
R = 32
KSUB = 6
CAP = 2
TPD = 16
S = 128
CX = 64
CY = 128
ROWS = S // 8
RIM = 8
SIDES = (0, 1, -1)
WIND = 100
GROUP = 8
GROUPS = LZ // GROUP
SIDE = 4
AHEAD = 2

time_step = 0.03
diffusion = 0.15
burn_rate = 0.15
regular = 0.01
courant = 0.4
heat_gain = 2.0

F32 = jnp.float32
LOCAL = pl.BlockSpec(memory_space=pltpu.VMEM)
FAR = pl.BlockSpec(memory_space=pltpu.HBM)
ANYWHERE = pl.BlockSpec(memory_space=pl.ANY)
SCALARS = pl.BlockSpec(memory_space=pltpu.SMEM)


def iota(dim, shape=(8, 128)):
    return lax.broadcasted_iota(jnp.int32, shape, dim)


def near(cells):
    return pltpu.with_memory_space_constraint(cells, pltpu.VMEM)


def far(cells):
    return pltpu.with_memory_space_constraint(cells, pltpu.HBM)


def params(mib):
    return pltpu.CompilerParams(vmem_limit_bytes=mib * 1024 * 1024)


def to_scalars(refs, scalars, sems):
    copies = [pltpu.make_async_copy(ref, own, sems.at[c]) for c, (ref, own) in enumerate(zip(refs, scalars))]
    for copy in copies:
        copy.start()
    for copy in copies:
        copy.wait()


def ranks_of(owner_ref, count, peers):
    for d in range(peers):
        count[d] = 0
    ranks = []
    for t in range(TPD):
        owner = owner_ref[t]
        ranks.append(count[owner])
        count[owner] = ranks[t] + 1
    return ranks


def request_kernel(owner_far, place_far, out_ref, owner_ref, place_ref, table, count, sems):
    to_scalars((owner_far, place_far), (owner_ref, place_ref), sems)
    peers = out_ref.shape[0]
    for i in range((peers + 2) * CAP):
        table[i] = -1
    ranks = ranks_of(owner_ref, count, peers)
    for t in range(TPD):
        table[(owner_ref[t] + 1) * CAP + ranks[t]] = place_ref[t]
    lane = iota(1, (1, 128))
    for peer in range(peers):
        line = jnp.full((1, 128), -1, jnp.int32)
        for g, side in enumerate(SIDES):
            for r in range(CAP):
                line = jnp.where(lane == g * CAP + r, table[(peer + 1 + side) * CAP + r], line)
        out_ref[peer] = jnp.broadcast_to(line, (8, 128))


def make_requests(owners, places, peers):
    return pl.pallas_call(
        request_kernel,
        in_specs=[FAR, FAR],
        out_specs=LOCAL,
        out_shape=pltpu.VMEM((peers, 8, 128), jnp.int32),
        scratch_shapes=[
            pltpu.SMEM((TPD,), jnp.int32),
            pltpu.SMEM((TPD,), jnp.int32),
            pltpu.SMEM(((peers + 2) * CAP,), jnp.int32),
            pltpu.SMEM((peers,), jnp.int32),
            pltpu.SemaphoreType.DMA((2,)),
        ],
        name="make_requests",
        compiler_params=params(4),
    )(far(owners), far(places))


def place_on(axis):
    index = lax.axis_index(axis)
    even = lax.rem(index, 2) == 0
    return even, jnp.logical_or(index == 0, index == lax.axis_size(axis) - 1)


def edge_kernel(
    after_ref, theta_ref, u_ref, v_ref,
    block_ref, one_x_ref, two_x_ref, one_y_ref, two_y_ref, theta, sems, wind_sems,
):
    even_x, wraps_x = place_on("gx")
    even_y, wraps_y = place_on("gy")

    def copy(g):
        part = pl.ds(g * GROUP, GROUP)
        return pltpu.make_async_copy(theta_ref.at[part], theta.at[part], sems.at[g])

    winds = [
        pltpu.make_async_copy(ref.at[0], block_ref.at[c * CX : (c + 1) * CX], wind_sems.at[c])
        for c, ref in enumerate((u_ref, v_ref))
    ]
    for g in reversed(range(GROUPS)):
        copy(g).start()
    for wind in winds:
        wind.start()
    lane = iota(1, (CX, 128))

    def one(i, carry):
        first, last = carry
        g = GROUPS - 1 - i
        copy(g).wait()
        first = pltpu.roll(first, GROUP, 1)
        last = pltpu.roll(last, GROUP, 1)
        for k in range(GROUP):
            z = g * GROUP + k
            cells = theta[z]
            low, high = cells[0:1], cells[CX - 1 : CX]
            one_x_ref[pl.ds(z, 1)] = jnp.where(even_x, high, low)
            two_x_ref[pl.ds(z, 1)] = jnp.where(wraps_x, 0.0, jnp.where(even_x, low, high))
            turned = pltpu.roll(cells, k + 1, 1)
            first = jnp.where(lane == k + 1, turned, first)
            last = jnp.where(lane == k, turned, last)
        return first, last

    zero = jnp.zeros((CX, 128), F32)
    first, last = lax.fori_loop(0, GROUPS, one, (zero, zero))
    for wind in winds:
        wind.wait()
    for c in range(2):
        cells = block_ref[c * CX : (c + 1) * CX]
        first = jnp.where(lane == WIND + c, pltpu.roll(cells, WIND + c, 1), first)
        last = jnp.where(lane == WIND + c, pltpu.roll(cells, WIND + c + 1, 1), last)
    one_y_ref[...] = jnp.where(even_y, last, first)
    two_y_ref[...] = jnp.where(wraps_y, 0.0, jnp.where(even_y, first, last))


def make_edges(after, theta, wind_u, wind_v):
    row = pltpu.VMEM((LZ, 128), F32)
    column = pltpu.VMEM((CX, 128), F32)
    return pl.pallas_call(
        edge_kernel,
        in_specs=[ANYWHERE, FAR, FAR, FAR],
        out_specs=[LOCAL] * 5,
        out_shape=[pltpu.VMEM((2 * CX, 128), F32), row, row, column, column],
        scratch_shapes=[
            pltpu.VMEM((LZ, CX, CY), F32),
            pltpu.SemaphoreType.DMA((GROUPS,)),
            pltpu.SemaphoreType.DMA((2,)),
        ],
        name="edges",
        compiler_params=params(8),
        cost_estimate=pl.CostEstimate(flops=4_000_000, bytes_accessed=2_700_000, transcendentals=0),
    )(after, far(theta), far(wind_u), far(wind_v))


def cut_kernel(
    asked_far, block_ref, one_y_ref, two_y_ref, one_x_ref, two_x_ref,
    out_ref, one_x_out, two_x_out, surface, edges, asked_ref, sem,
):
    copy = pltpu.make_async_copy(asked_far.at[:, 0:1], asked_ref, sem)
    copy.start()
    one_x_out[...] = one_x_ref[...]
    two_x_out[...] = two_x_ref[...]
    even, _ = place_on("gy")
    south = jnp.where(even, two_y_ref[...], one_y_ref[...])
    north = jnp.where(even, one_y_ref[...], two_y_ref[...])
    wide = iota(1, (CX, 128))
    lane = iota(1)
    blank = jnp.zeros((RIM, 128), F32)
    for c in range(2):
        low = jnp.broadcast_to(south[:, WIND + c : WIND + c + 1], (CX, 128))
        high = jnp.broadcast_to(north[:, WIND + c : WIND + c + 1], (CX, 128))
        surface[c, 0:RIM] = blank
        surface[c, RIM : RIM + CX] = block_ref[c * CX : (c + 1) * CX]
        surface[c, RIM + CX :] = blank
        edges[c, 0:RIM] = blank
        edges[c, RIM : RIM + CX] = jnp.where(wide % 8 == 0, low, high)
        edges[c, RIM + CX :] = blank
    copy.wait()
    tiles_y = CY // TA
    for source in range(out_ref.shape[0]):
        message = jnp.zeros((8, 128), F32)
        for g, side in enumerate(SIDES):
            for r in range(CAP):
                place = asked_ref[source, 0, g * CAP + r]
                y_own = jnp.bitwise_and(place, tiles_y - 1) * TA
                first = lax.shift_right_arithmetic(place, 5) * TA - 1 + side * CX
                first = jnp.where(place < 0, CX, jnp.clip(first, -RIM, CX)) + RIM
                begin = (g * CAP + r) * 16
                outside = jnp.where(y_own == 0, 0, jnp.where(y_own == CY - TA, TA + 1, 1000))
                for c in range(2):
                    at = begin + 8 * c
                    turn = jnp.bitwise_and(at + 1 - y_own, 127)
                    part = pltpu.roll(surface[c, pl.ds(first, 8), :], turn, 1)
                    part = jnp.where(lane == at + outside, edges[c, pl.ds(first, 8), :], part)
                    message = jnp.where(lane // 8 == at // 8, part, message)
        out_ref[source] = message


def cut_patches(asked, block, one_y, two_y, one_x, two_x):
    peers = asked.shape[0]
    row = pltpu.VMEM((LZ, 128), F32)
    rows = CX + 2 * RIM
    return pl.pallas_call(
        cut_kernel,
        in_specs=[LOCAL] * 6,
        out_specs=[LOCAL] * 3,
        out_shape=[pltpu.VMEM((peers, 8, 128), F32), row, row],
        scratch_shapes=[
            pltpu.VMEM((2, rows, 128), F32),
            pltpu.VMEM((2, rows, 128), F32),
            pltpu.SMEM((peers, 1, 128), jnp.int32),
            pltpu.SemaphoreType.DMA(()),
        ],
        name="cut_patches",
        compiler_params=params(4),
    )(*(near(a) for a in (asked, block, one_y, two_y, one_x, two_x)))


def advect_kernel(
    theta_ref, u_ref, v_ref, one_x_ref, two_x_ref, one_y_ref, two_y_ref,
    out_ref, theta, wind_u, wind_v, west_ref, east_ref, sems,
):
    def copies(g):
        part = pl.ds(g * GROUP, GROUP)
        pairs = ((theta_ref, theta), (u_ref, wind_u), (v_ref, wind_v))
        return [
            pltpu.make_async_copy(source.at[part], target.at[part], sems.at[c, g])
            for c, (source, target) in enumerate(pairs)
        ]

    for g in range(GROUPS):
        for copy in copies(g):
            copy.start()
    even, _ = place_on("gx")
    west_ref[...] = jnp.where(even, two_x_ref[...], one_x_ref[...])
    east_ref[...] = jnp.where(even, one_x_ref[...], two_x_ref[...])
    even, _ = place_on("gy")
    south = jnp.where(even, two_y_ref[...], one_y_ref[...])
    north = jnp.where(even, one_y_ref[...], two_y_ref[...])
    lane = iota(1, (CX, 128))
    row = iota(0, (CX, 128))

    def one(g, carry):
        south_all, north_all = carry
        for copy in copies(g):
            copy.wait()
        def begin(k):
            t = theta[g * GROUP + k]
            rolled = [pltpu.roll(t, 1, 1), pltpu.roll(t, CY - 1, 1)]
            rims = [pltpu.roll(south_all, (128 - k) % 128, 1), pltpu.roll(north_all, 126 - k, 1)]
            return t, rolled, rims

        def end(k, begun):
            z = g * GROUP + k
            t, rolled, rims = begun
            u = wind_u[z]
            v = wind_v[z]
            west = jnp.where(row == 0, west_ref[pl.ds(z, 1)], pltpu.roll(t, 1, 0))
            east = jnp.where(row == CX - 1, east_ref[pl.ds(z, 1)], pltpu.roll(t, CX - 1, 0))
            south = jnp.where(lane == 0, rims[0], rolled[0])
            north = jnp.where(lane == CY - 1, rims[1], rolled[1])
            change = jnp.abs(u) * (t - jnp.where(u > 0, west, east)) + jnp.abs(v) * (
                t - jnp.where(v > 0, south, north)
            )
            out_ref[z] = t - courant * change

        begun = [begin(k) for k in range(AHEAD)]
        for k in range(GROUP):
            if k + AHEAD < GROUP:
                begun.append(begin(k + AHEAD))
            end(k, begun[k])
        return pltpu.roll(south_all, 128 - GROUP, 1), pltpu.roll(north_all, 128 - GROUP, 1)

    lax.fori_loop(0, GROUPS, one, (south, north))


def advect(theta, wind_u, wind_v, *rims):
    whole = pltpu.VMEM((LZ, CX, CY), F32)
    return pl.pallas_call(
        advect_kernel,
        in_specs=[FAR] * 3 + [LOCAL] * 4,
        out_specs=LOCAL,
        out_shape=whole,
        scratch_shapes=[
            whole,
            whole,
            whole,
            pltpu.VMEM((LZ, 128), F32),
            pltpu.VMEM((LZ, 128), F32),
            pltpu.SemaphoreType.DMA((3, GROUPS)),
        ],
        name="advect",
        compiler_params=params(12),
        cost_estimate=pl.CostEstimate(flops=14_000_000, bytes_accessed=8_000_000, transcendentals=0),
    )(far(theta), far(wind_u), far(wind_v), *(near(a) for a in rims))


def fire_kernel(
    peers, waits, owner_far, place_far, winds_ref, level_ref, fuel_ref, base_ref, *rest
):
    (
        level_out, fuel_out, outbox, begins, slopes, heats,
        level_own, fuel_own, base_own, owner_ref, place_ref, count, scalar_sems, in_sems, out_sems,
    ) = rest[waits:]
    lane = iota(1)
    row = iota(0)

    def bases(i):
        some = pl.ds(i * SIDE, SIDE)
        return pltpu.make_async_copy(base_ref.at[some], base_own.at[some], in_sems.at[i])

    def results(i):
        some = pl.ds(i * SIDE, SIDE)
        pairs = ((level_own, level_out), (fuel_own, fuel_out))
        return [
            pltpu.make_async_copy(source.at[some], target.at[some], out_sems.at[c, i])
            for c, (source, target) in enumerate(pairs)
        ]

    for i in range(TPD // SIDE):
        bases(i).start()
    to_scalars((owner_far, place_far), (owner_ref, place_ref), scalar_sems)

    tiles_y = CY // TA
    low_row = (row + 1) // 2
    low_lane = (lane + R // 2) // R
    part_row = jnp.where(row % 2 == 0, 0.5, 0.0) + 0.5 / R
    part_lane = (lane.astype(F32) + 0.5) / R + 0.5 - low_lane.astype(F32)

    ranks = ranks_of(owner_ref, count, peers)
    patches = []
    for t in range(TPD):
        owner = owner_ref[t]
        parts = []
        for g, side in enumerate(SIDES):
            begin = (g * CAP + ranks[t]) * 16
            inside = jnp.logical_and(owner >= side, owner - side < peers)
            part = winds_ref[jnp.clip(owner - side, 0, peers - 1)]
            part = jnp.where(inside, part, 0.0)
            parts.append([pltpu.roll(part, jnp.bitwise_and(-begin - 8 * c, 127), 1) for c in range(2)])
        for c in range(2):
            patches.append(parts[0][c] + parts[1][c] + parts[2][c])
    left = [jnp.take_along_axis(p, low_lane, axis=1) for p in patches]
    right = [jnp.take_along_axis(p, low_lane + 1, axis=1) for p in patches]
    fine = [p + (q - p) * part_lane for p, q in zip(left, right)]
    below = [jnp.take_along_axis(p, low_row, axis=0) for p in fine]
    above = [jnp.take_along_axis(p, low_row + 1, axis=0) for p in fine]
    for i, (p, q) in enumerate(zip(below, above)):
        begins[i] = p + (q - p) * part_row
        slopes[i] = (q - p) * (1.0 / R)

    def burn(t):
        begin = [begins[2 * t + c] for c in range(2)]
        slope = [slopes[2 * t + c] for c in range(2)]
        level = [level_ref[t, pl.ds(k, 8, stride=ROWS), :] for k in range(ROWS)]
        fuel = [fuel_ref[t, pl.ds(k, 8, stride=ROWS), :] for k in range(ROWS)]
        heat = sum(fuel[1:], fuel[0])
        rate = [base_own[t, pl.ds(k, 8, stride=ROWS), :] * (0.5 * time_step) for k in range(ROWS)]
        wind = [[begin[c] + slope[c] * float(k) for k in range(ROWS)] for c in range(2)]
        yield
        for _ in range(KSUB):
            before = jnp.where(row == 0, level[0], pltpu.roll(level[-1], 1, 0))
            after = jnp.where(row == 7, level[-1], pltpu.roll(level[0], 7, 0))
            rimmed = [before, *level, after]
            south = [jnp.where(lane == 0, cell, pltpu.roll(cell, 1, 1)) for cell in level]
            north = [jnp.where(lane == S - 1, cell, pltpu.roll(cell, S - 1, 1)) for cell in level]
            yield
            new = []
            for k in range(ROWS):
                cell = rimmed[k + 1]
                west, east = rimmed[k], rimmed[k + 2]
                dx = east - west
                dy = north[k] - south[k]
                square = dx * dx + dy * dy + 4.0 * regular
                length = square * lax.rsqrt(square)
                move = jnp.maximum(length + (wind[0][k] * dx + wind[1][k] * dy), 0.0)
                around = (east + west) + (north[k] + south[k])
                cell = cell * (1.0 - 4.0 * diffusion) + around * diffusion - rate[k] * move
                fuel[k] = fuel[k] * (jnp.tanh(cell) + (2.0 / burn_rate - 1.0))
                new.append(cell)
            level = new
        fuel = [cell * (0.5 * burn_rate) ** KSUB for cell in fuel]
        yield
        for k in range(ROWS):
            level_own[t, pl.ds(k, 8, stride=ROWS), :] = level[k]
            fuel_own[t, pl.ds(k, 8, stride=ROWS), :] = fuel[k]
        heats[t] = (heat - sum(fuel[1:], fuel[0])) * (1.0 / (R * R))

    def some(i, carry):
        tiles = [i * SIDE + j for j in range(SIDE)]
        bases(i).wait()
        works = [burn(t) for t in tiles]
        while works:
            works = [w for w in works if next(w, works) is None]
        for copy in results(i):
            copy.start()
        return carry

    lax.fori_loop(0, TPD // SIDE, some, 0)

    for d in range(peers * CAP):
        outbox[d] = jnp.where(row < TA, 0.0, -1.0)
    pairs = [heats[t] for t in range(TPD)]
    pairs = [h + pltpu.roll(h, 7, 0) for h in pairs]
    pairs = [jnp.take_along_axis(h, jnp.minimum(2 * row, 7), axis=0) for h in pairs]
    sums = [
        [jnp.sum(jnp.where(lane // R == b, h, 0.0), axis=1, keepdims=True) for b in range(TA)] for h in pairs
    ]
    for t in range(TPD):
        place = place_ref[t]
        x_own = place // tiles_y * TA
        y_own = lax.rem(place, tiles_y) * TA
        message = jnp.where(row < TA, 0.0, (x_own + row - TA).astype(F32))
        for b in range(TA):
            message = jnp.where(jnp.logical_and(row < TA, lane == y_own + b), sums[t][b], message)
        outbox[owner_ref[t] * CAP + ranks[t]] = message
    for i in range(TPD // SIDE):
        for copy in results(i):
            copy.wait()


def fire(owners, places, winds, level_set, fuel_load, spread_base, peers, waits):
    tiles = (TPD, S, S)
    return pl.pallas_call(
        functools.partial(fire_kernel, peers, len(waits)),
        in_specs=[FAR, FAR] + [LOCAL] * 3 + [FAR] + [ANYWHERE] * len(waits),
        out_specs=[ANYWHERE, ANYWHERE, LOCAL],
        out_shape=[
            jax.ShapeDtypeStruct(tiles, F32),
            jax.ShapeDtypeStruct(tiles, F32),
            pltpu.VMEM((peers * CAP, 8, 128), F32),
        ],
        scratch_shapes=[
            pltpu.VMEM((2 * TPD, 8, 128), F32),
            pltpu.VMEM((2 * TPD, 8, 128), F32),
            pltpu.VMEM((TPD, 8, 128), F32),
            pltpu.VMEM(tiles, F32),
            pltpu.VMEM(tiles, F32),
            pltpu.VMEM(tiles, F32),
            pltpu.SMEM((TPD,), jnp.int32),
            pltpu.SMEM((TPD,), jnp.int32),
            pltpu.SMEM((peers,), jnp.int32),
            pltpu.SemaphoreType.DMA((2,)),
            pltpu.SemaphoreType.DMA((TPD // SIDE,)),
            pltpu.SemaphoreType.DMA((2, TPD // SIDE)),
        ],
        name="fire",
        compiler_params=params(12),
        cost_estimate=pl.CostEstimate(
            flops=50_000_000, bytes_accessed=6_500_000, transcendentals=3_200_000
        ),
    )(far(owners), far(places), *(near(a) for a in (winds, level_set, fuel_load)), far(spread_base), *waits)


def final_kernel(inbox_ref, part_ref, out_ref, field, result, sems):
    inbox = inbox_ref[...]
    slots = inbox.shape[0]
    position = pltpu.roll(inbox, TA, 1).reshape(slots * 8, 128)
    values = inbox.reshape(slots * 8, 128)
    lane = iota(1, (slots * 8, 128)).astype(F32)
    valid = iota(0, (slots * 8, 128)) % 8 < TA
    hot = jnp.where(jnp.logical_and(valid, lane == position), 1.0, 0.0)
    total = lax.dot_general(
        hot, values, (((0,), (0,)), ((), ())),
        precision=lax.Precision.HIGHEST, preferred_element_type=F32,
    )
    field[...] = total[:CX]

    def copy(g):
        part = pl.ds(g * GROUP, GROUP)
        return pltpu.make_async_copy(result.at[part], out_ref.at[part], sems.at[g])

    def one(g, carry):
        for k in range(GROUP):
            z = g * GROUP + k
            height = jnp.full((8, 128), z, jnp.int32).astype(F32)
            gain = heat_gain * jnp.exp((height + 0.5) * (-4.0 / LZ))
            result[z] = part_ref[z] + field[...] * jnp.concatenate([gain] * (CX // 8), axis=0)
        copy(g).start()
        return carry

    lax.fori_loop(0, GROUPS, one, 0)
    for g in range(GROUPS):
        copy(g).wait()


def finish(inbox, part):
    return pl.pallas_call(
        final_kernel,
        in_specs=[LOCAL, LOCAL],
        out_specs=ANYWHERE,
        out_shape=jax.ShapeDtypeStruct((LZ, CX, CY), F32),
        scratch_shapes=[
            pltpu.VMEM((CX, CY), F32),
            pltpu.VMEM((LZ, CX, CY), F32),
            pltpu.SemaphoreType.DMA((GROUPS,)),
        ],
        name="finish",
        compiler_params=params(8),
        cost_estimate=pl.CostEstimate(flops=3_000_000, bytes_accessed=2_700_000, transcendentals=0),
    )(near(inbox), near(part))


def swapped(one, two, axis):
    count = lax.axis_size(axis)
    pairs = [(i, i ^ 1) for i in range(count)]
    others = [(i + 1, (i ^ 1) + 1) for i in range(count - 2)] + [(0, 0), (count - 1, count - 1)]
    return lax.ppermute(one, axis, pairs), lax.ppermute(two, axis, others)


def exchange(cells):
    return lax.all_to_all(cells, "gx", split_axis=0, concat_axis=0, tiled=True)


def body(theta, wind_u, wind_v, level_set, fuel_load, spread_base, tile_owner, tile_place):
    peers = lax.axis_size("gx")
    owners, places = tile_owner[0, 0], tile_place[0, 0]
    requests = make_requests(owners, places, peers)
    asked = exchange(requests)

    block, one_x, two_x, one_y, two_y = make_edges(requests, theta, wind_u, wind_v)
    rims_y = swapped(one_y, two_y, "gy")

    patches, one_x, two_x = cut_patches(asked, block, *rims_y, one_x, two_x)
    winds = exchange(patches)
    rims_x = swapped(one_x, two_x, "gx")

    level_out, fuel_out, outbox = fire(
        owners, places, winds, level_set[0, 0], fuel_load[0, 0], spread_base[0, 0], peers, rims_x
    )
    part = advect(theta, wind_u, wind_v, *rims_x, *rims_y)
    inbox = exchange(outbox)
    theta_next = finish(inbox, part)
    return (theta_next, level_out[None, None], fuel_out[None, None])


def solution(mesh):
    in_specs = (
        P(None, "gx", "gy"),
        P(None, "gx", "gy"),
        P(None, "gx", "gy"),
        P("gx", "gy", None, None, None),
        P("gx", "gy", None, None, None),
        P("gx", "gy", None, None, None),
        P("gx", "gy", None),
        P("gx", "gy", None),
    )
    out_specs = (
        P(None, "gx", "gy"),
        P("gx", "gy", None, None, None),
        P("gx", "gy", None, None, None),
    )
    return jax.shard_map(body, mesh=mesh, in_specs=in_specs, out_specs=out_specs, check_vma=False)
```

```python
import functools

import jax
import jax.numpy as jnp
from jax import lax
from jax.experimental import pallas as pl
from jax.experimental.pallas import tpu as pltpu
from jax.sharding import PartitionSpec as P

LZ = 80
TA = 4
R = 32
KSUB = 6
CAP = 2
TPD = 16
S = 128
CX = 64
CY = 128
ROWS = S // 8
RIM = 8
SIDES = (0, 1, -1)
WIND = 100
GROUP = 8
GROUPS = LZ // GROUP
SIDE = 4
AHEAD = 2

time_step = 0.03
diffusion = 0.15
burn_rate = 0.15
regular = 0.01
courant = 0.4
heat_gain = 2.0

F32 = jnp.float32
LOCAL = pl.BlockSpec(memory_space=pltpu.VMEM)
FAR = pl.BlockSpec(memory_space=pltpu.HBM)
ANYWHERE = pl.BlockSpec(memory_space=pl.ANY)
SCALARS = pl.BlockSpec(memory_space=pltpu.SMEM)


def iota(dim, shape=(8, 128)):
    return lax.broadcasted_iota(jnp.int32, shape, dim)


def near(cells):
    return pltpu.with_memory_space_constraint(cells, pltpu.VMEM)


def far(cells):
    return pltpu.with_memory_space_constraint(cells, pltpu.HBM)


def params(mib):
    return pltpu.CompilerParams(vmem_limit_bytes=mib * 1024 * 1024)


def to_scalars(refs, scalars, sems):
    copies = [pltpu.make_async_copy(ref, own, sems.at[c]) for c, (ref, own) in enumerate(zip(refs, scalars))]
    for copy in copies:
        copy.start()
    for copy in copies:
        copy.wait()


def ranks_of(owner_ref, count, peers):
    for d in range(peers):
        count[d] = 0
    ranks = []
    for t in range(TPD):
        owner = owner_ref[t]
        ranks.append(count[owner])
        count[owner] = ranks[t] + 1
    return ranks


def request_kernel(owner_far, place_far, out_ref, owner_ref, place_ref, table, count, sems):
    to_scalars((owner_far, place_far), (owner_ref, place_ref), sems)
    peers = out_ref.shape[0]
    for i in range((peers + 2) * CAP):
        table[i] = -1
    ranks = ranks_of(owner_ref, count, peers)
    for t in range(TPD):
        table[(owner_ref[t] + 1) * CAP + ranks[t]] = place_ref[t]
    lane = iota(1, (1, 128))
    for peer in range(peers):
        line = jnp.full((1, 128), -1, jnp.int32)
        for g, side in enumerate(SIDES):
            for r in range(CAP):
                line = jnp.where(lane == g * CAP + r, table[(peer + 1 + side) * CAP + r], line)
        out_ref[peer] = jnp.broadcast_to(line, (8, 128))


def make_requests(owners, places, peers):
    return pl.pallas_call(
        request_kernel,
        in_specs=[FAR, FAR],
        out_specs=LOCAL,
        out_shape=pltpu.VMEM((peers, 8, 128), jnp.int32),
        scratch_shapes=[
            pltpu.SMEM((TPD,), jnp.int32),
            pltpu.SMEM((TPD,), jnp.int32),
            pltpu.SMEM(((peers + 2) * CAP,), jnp.int32),
            pltpu.SMEM((peers,), jnp.int32),
            pltpu.SemaphoreType.DMA((2,)),
        ],
        name="make_requests",
        compiler_params=params(4),
    )(far(owners), far(places))


def place_on(axis):
    index = lax.axis_index(axis)
    even = lax.rem(index, 2) == 0
    return even, jnp.logical_or(index == 0, index == lax.axis_size(axis) - 1)


def edge_kernel(
    after_ref, theta_ref, u_ref, v_ref,
    block_ref, one_x_ref, two_x_ref, one_y_ref, two_y_ref, theta, sems, wind_sems,
):
    even_x, wraps_x = place_on("gx")
    even_y, wraps_y = place_on("gy")

    def copy(g):
        part = pl.ds(g * GROUP, GROUP)
        return pltpu.make_async_copy(theta_ref.at[part], theta.at[part], sems.at[g])

    winds = [
        pltpu.make_async_copy(ref.at[0], block_ref.at[c * CX : (c + 1) * CX], wind_sems.at[c])
        for c, ref in enumerate((u_ref, v_ref))
    ]
    for g in reversed(range(GROUPS)):
        copy(g).start()
    for wind in winds:
        wind.start()
    lane = iota(1, (CX, 128))

    def one(i, carry):
        first, last = carry
        g = GROUPS - 1 - i
        copy(g).wait()
        first = pltpu.roll(first, GROUP, 1)
        last = pltpu.roll(last, GROUP, 1)
        for k in range(GROUP):
            z = g * GROUP + k
            cells = theta[z]
            low, high = cells[0:1], cells[CX - 1 : CX]
            one_x_ref[pl.ds(z, 1)] = jnp.where(even_x, high, low)
            two_x_ref[pl.ds(z, 1)] = jnp.where(wraps_x, 0.0, jnp.where(even_x, low, high))
            turned = pltpu.roll(cells, k + 1, 1)
            first = jnp.where(lane == k + 1, turned, first)
            last = jnp.where(lane == k, turned, last)
        return first, last

    zero = jnp.zeros((CX, 128), F32)
    first, last = lax.fori_loop(0, GROUPS, one, (zero, zero))
    for wind in winds:
        wind.wait()
    for c in range(2):
        cells = block_ref[c * CX : (c + 1) * CX]
        first = jnp.where(lane == WIND + c, pltpu.roll(cells, WIND + c, 1), first)
        last = jnp.where(lane == WIND + c, pltpu.roll(cells, WIND + c + 1, 1), last)
    one_y_ref[...] = jnp.where(even_y, last, first)
    two_y_ref[...] = jnp.where(wraps_y, 0.0, jnp.where(even_y, first, last))


def make_edges(after, theta, wind_u, wind_v):
    row = pltpu.VMEM((LZ, 128), F32)
    column = pltpu.VMEM((CX, 128), F32)
    return pl.pallas_call(
        edge_kernel,
        in_specs=[ANYWHERE, FAR, FAR, FAR],
        out_specs=[LOCAL] * 5,
        out_shape=[pltpu.VMEM((2 * CX, 128), F32), row, row, column, column],
        scratch_shapes=[
            pltpu.VMEM((LZ, CX, CY), F32),
            pltpu.SemaphoreType.DMA((GROUPS,)),
            pltpu.SemaphoreType.DMA((2,)),
        ],
        name="edges",
        compiler_params=params(8),
        cost_estimate=pl.CostEstimate(flops=4_000_000, bytes_accessed=2_700_000, transcendentals=0),
    )(after, far(theta), far(wind_u), far(wind_v))


def cut_kernel(
    asked_far, block_ref, one_y_ref, two_y_ref, one_x_ref, two_x_ref,
    out_ref, one_x_out, two_x_out, surface, edges, asked_ref, sem,
):
    copy = pltpu.make_async_copy(asked_far.at[:, 0:1], asked_ref, sem)
    copy.start()
    one_x_out[...] = one_x_ref[...]
    two_x_out[...] = two_x_ref[...]
    even, _ = place_on("gy")
    south = jnp.where(even, two_y_ref[...], one_y_ref[...])
    north = jnp.where(even, one_y_ref[...], two_y_ref[...])
    wide = iota(1, (CX, 128))
    lane = iota(1)
    blank = jnp.zeros((RIM, 128), F32)
    for c in range(2):
        low = jnp.broadcast_to(south[:, WIND + c : WIND + c + 1], (CX, 128))
        high = jnp.broadcast_to(north[:, WIND + c : WIND + c + 1], (CX, 128))
        surface[c, 0:RIM] = blank
        surface[c, RIM : RIM + CX] = block_ref[c * CX : (c + 1) * CX]
        surface[c, RIM + CX :] = blank
        edges[c, 0:RIM] = blank
        edges[c, RIM : RIM + CX] = jnp.where(wide % 8 == 0, low, high)
        edges[c, RIM + CX :] = blank
    copy.wait()
    tiles_y = CY // TA
    for source in range(out_ref.shape[0]):
        message = jnp.zeros((8, 128), F32)
        for g, side in enumerate(SIDES):
            for r in range(CAP):
                place = asked_ref[source, 0, g * CAP + r]
                y_own = jnp.bitwise_and(place, tiles_y - 1) * TA
                first = lax.shift_right_arithmetic(place, 5) * TA - 1 + side * CX
                first = jnp.where(place < 0, CX, jnp.clip(first, -RIM, CX)) + RIM
                begin = (g * CAP + r) * 16
                outside = jnp.where(y_own == 0, 0, jnp.where(y_own == CY - TA, TA + 1, 1000))
                for c in range(2):
                    at = begin + 8 * c
                    turn = jnp.bitwise_and(at + 1 - y_own, 127)
                    part = pltpu.roll(surface[c, pl.ds(first, 8), :], turn, 1)
                    part = jnp.where(lane == at + outside, edges[c, pl.ds(first, 8), :], part)
                    message = jnp.where(lane // 8 == at // 8, part, message)
        out_ref[source] = message


def cut_patches(asked, block, one_y, two_y, one_x, two_x):
    peers = asked.shape[0]
    row = pltpu.VMEM((LZ, 128), F32)
    rows = CX + 2 * RIM
    return pl.pallas_call(
        cut_kernel,
        in_specs=[LOCAL] * 6,
        out_specs=[LOCAL] * 3,
        out_shape=[pltpu.VMEM((peers, 8, 128), F32), row, row],
        scratch_shapes=[
            pltpu.VMEM((2, rows, 128), F32),
            pltpu.VMEM((2, rows, 128), F32),
            pltpu.SMEM((peers, 1, 128), jnp.int32),
            pltpu.SemaphoreType.DMA(()),
        ],
        name="cut_patches",
        compiler_params=params(4),
    )(*(near(a) for a in (asked, block, one_y, two_y, one_x, two_x)))


def advect_kernel(
    theta_ref, u_ref, v_ref, west_ref, east_ref, one_y_ref, two_y_ref,
    out_ref, theta, wind_u, wind_v, sems,
):
    def copies(g):
        part = pl.ds(g * GROUP, GROUP)
        pairs = ((theta_ref, theta), (u_ref, wind_u), (v_ref, wind_v))
        return [
            pltpu.make_async_copy(source.at[part], target.at[part], sems.at[c, g])
            for c, (source, target) in enumerate(pairs)
        ]

    for g in range(GROUPS):
        for copy in copies(g):
            copy.start()
    even, _ = place_on("gy")
    south = jnp.where(even, two_y_ref[...], one_y_ref[...])
    north = jnp.where(even, one_y_ref[...], two_y_ref[...])
    lane = iota(1, (CX, 128))
    row = iota(0, (CX, 128))

    def one(g, carry):
        south_all, north_all = carry
        for copy in copies(g):
            copy.wait()
        def begin(k):
            t = theta[g * GROUP + k]
            rolled = [pltpu.roll(t, 1, 1), pltpu.roll(t, CY - 1, 1)]
            rims = [pltpu.roll(south_all, (128 - k) % 128, 1), pltpu.roll(north_all, 126 - k, 1)]
            return t, rolled, rims

        def end(k, begun):
            z = g * GROUP + k
            t, rolled, rims = begun
            u = wind_u[z]
            v = wind_v[z]
            west = jnp.where(row == 0, west_ref[pl.ds(z, 1)], pltpu.roll(t, 1, 0))
            east = jnp.where(row == CX - 1, east_ref[pl.ds(z, 1)], pltpu.roll(t, CX - 1, 0))
            south = jnp.where(lane == 0, rims[0], rolled[0])
            north = jnp.where(lane == CY - 1, rims[1], rolled[1])
            change = jnp.abs(u) * (t - jnp.where(u > 0, west, east)) + jnp.abs(v) * (
                t - jnp.where(v > 0, south, north)
            )
            out_ref[z] = t - courant * change

        begun = [begin(k) for k in range(AHEAD)]
        for k in range(GROUP):
            if k + AHEAD < GROUP:
                begun.append(begin(k + AHEAD))
            end(k, begun[k])
        return pltpu.roll(south_all, 128 - GROUP, 1), pltpu.roll(north_all, 128 - GROUP, 1)

    lax.fori_loop(0, GROUPS, one, (south, north))


def advect(theta, wind_u, wind_v, *rims):
    whole = pltpu.VMEM((LZ, CX, CY), F32)
    return pl.pallas_call(
        advect_kernel,
        in_specs=[FAR] * 3 + [LOCAL] * 4,
        out_specs=LOCAL,
        out_shape=whole,
        scratch_shapes=[
            whole,
            whole,
            whole,
            pltpu.SemaphoreType.DMA((3, GROUPS)),
        ],
        name="advect",
        compiler_params=params(12),
        cost_estimate=pl.CostEstimate(flops=14_000_000, bytes_accessed=8_000_000, transcendentals=0),
    )(far(theta), far(wind_u), far(wind_v), *(near(a) for a in rims))


def fire_kernel(
    peers, waits, owner_far, place_far, winds_ref, level_ref, fuel_ref, base_ref, *rest
):
    (
        level_out, fuel_out, outbox, begins, slopes, heats,
        level_own, fuel_own, base_own, owner_ref, place_ref, count, scalar_sems, in_sems, out_sems,
    ) = rest[waits:]
    lane = iota(1)
    row = iota(0)

    def bases(i):
        some = pl.ds(i * SIDE, SIDE)
        return pltpu.make_async_copy(base_ref.at[some], base_own.at[some], in_sems.at[i])

    def results(i):
        some = pl.ds(i * SIDE, SIDE)
        pairs = ((level_own, level_out), (fuel_own, fuel_out))
        return [
            pltpu.make_async_copy(source.at[some], target.at[some], out_sems.at[c, i])
            for c, (source, target) in enumerate(pairs)
        ]

    for i in range(TPD // SIDE):
        bases(i).start()
    to_scalars((owner_far, place_far), (owner_ref, place_ref), scalar_sems)

    tiles_y = CY // TA
    low_row = (row + 1) // 2
    low_lane = (lane + R // 2) // R
    part_row = jnp.where(row % 2 == 0, 0.5, 0.0) + 0.5 / R
    part_lane = (lane.astype(F32) + 0.5) / R + 0.5 - low_lane.astype(F32)

    ranks = ranks_of(owner_ref, count, peers)
    patches = []
    for t in range(TPD):
        owner = owner_ref[t]
        parts = []
        for g, side in enumerate(SIDES):
            begin = (g * CAP + ranks[t]) * 16
            inside = jnp.logical_and(owner >= side, owner - side < peers)
            part = winds_ref[jnp.clip(owner - side, 0, peers - 1)]
            part = jnp.where(inside, part, 0.0)
            parts.append([pltpu.roll(part, jnp.bitwise_and(-begin - 8 * c, 127), 1) for c in range(2)])
        for c in range(2):
            patches.append(parts[0][c] + parts[1][c] + parts[2][c])
    left = [jnp.take_along_axis(p, low_lane, axis=1) for p in patches]
    right = [jnp.take_along_axis(p, low_lane + 1, axis=1) for p in patches]
    fine = [p + (q - p) * part_lane for p, q in zip(left, right)]
    below = [jnp.take_along_axis(p, low_row, axis=0) for p in fine]
    above = [jnp.take_along_axis(p, low_row + 1, axis=0) for p in fine]
    for i, (p, q) in enumerate(zip(below, above)):
        begins[i] = p + (q - p) * part_row
        slopes[i] = (q - p) * (1.0 / R)

    def burn(t):
        begin = [begins[2 * t + c] for c in range(2)]
        slope = [slopes[2 * t + c] for c in range(2)]
        level = [level_ref[t, pl.ds(k, 8, stride=ROWS), :] for k in range(ROWS)]
        fuel = [fuel_ref[t, pl.ds(k, 8, stride=ROWS), :] for k in range(ROWS)]
        heat = sum(fuel[1:], fuel[0])
        rate = [base_own[t, pl.ds(k, 8, stride=ROWS), :] * (0.5 * time_step) for k in range(ROWS)]
        wind = [[begin[c] + slope[c] * float(k) for k in range(ROWS)] for c in range(2)]
        yield
        for _ in range(KSUB):
            before = jnp.where(row == 0, level[0], pltpu.roll(level[-1], 1, 0))
            after = jnp.where(row == 7, level[-1], pltpu.roll(level[0], 7, 0))
            rimmed = [before, *level, after]
            south = [jnp.where(lane == 0, cell, pltpu.roll(cell, 1, 1)) for cell in level]
            north = [jnp.where(lane == S - 1, cell, pltpu.roll(cell, S - 1, 1)) for cell in level]
            yield
            new = []
            for k in range(ROWS):
                cell = rimmed[k + 1]
                west, east = rimmed[k], rimmed[k + 2]
                dx = east - west
                dy = north[k] - south[k]
                square = dx * dx + dy * dy + 4.0 * regular
                length = square * lax.rsqrt(square)
                move = jnp.maximum(length + (wind[0][k] * dx + wind[1][k] * dy), 0.0)
                around = (east + west) + (north[k] + south[k])
                cell = cell * (1.0 - 4.0 * diffusion) + around * diffusion - rate[k] * move
                fuel[k] = fuel[k] * (jnp.tanh(cell) + (2.0 / burn_rate - 1.0))
                new.append(cell)
            level = new
        fuel = [cell * (0.5 * burn_rate) ** KSUB for cell in fuel]
        yield
        for k in range(ROWS):
            level_own[t, pl.ds(k, 8, stride=ROWS), :] = level[k]
            fuel_own[t, pl.ds(k, 8, stride=ROWS), :] = fuel[k]
        heats[t] = (heat - sum(fuel[1:], fuel[0])) * (1.0 / (R * R))

    def some(i, carry):
        tiles = [i * SIDE + j for j in range(SIDE)]
        bases(i).wait()
        works = [burn(t) for t in tiles]
        while works:
            works = [w for w in works if next(w, works) is None]
        for copy in results(i):
            copy.start()
        return carry

    lax.fori_loop(0, TPD // SIDE, some, 0)

    for d in range(peers):
        outbox[d] = jnp.where(lane < TA, 0.0, -1.0)
    pairs = [heats[t] for t in range(TPD)]
    pairs = [h + pltpu.roll(h, 7, 0) for h in pairs]
    pairs = [jnp.take_along_axis(h, jnp.minimum(2 * row, 7), axis=0) for h in pairs]
    sums = [
        [jnp.sum(jnp.where(lane // R == b, h, 0.0), axis=1, keepdims=True) for b in range(TA)] for h in pairs
    ]
    for t in range(TPD):
        place = place_ref[t]
        x_own = place // tiles_y * TA
        y_own = lax.rem(place, tiles_y) * TA
        message = jnp.where(lane == TA, (x_own + row).astype(F32), y_own.astype(F32))
        for b in range(TA):
            message = jnp.where(lane == b, sums[t][b], message)
        outbox[owner_ref[t], pl.ds(ranks[t] * TA, TA), :] = message[0:TA]
    for i in range(TPD // SIDE):
        for copy in results(i):
            copy.wait()


def fire(owners, places, winds, level_set, fuel_load, spread_base, peers, waits):
    tiles = (TPD, S, S)
    return pl.pallas_call(
        functools.partial(fire_kernel, peers, len(waits)),
        in_specs=[FAR, FAR] + [LOCAL] * 3 + [FAR] + [ANYWHERE] * len(waits),
        out_specs=[ANYWHERE, ANYWHERE, LOCAL],
        out_shape=[
            jax.ShapeDtypeStruct(tiles, F32),
            jax.ShapeDtypeStruct(tiles, F32),
            pltpu.VMEM((peers, 8, 128), F32),
        ],
        scratch_shapes=[
            pltpu.VMEM((2 * TPD, 8, 128), F32),
            pltpu.VMEM((2 * TPD, 8, 128), F32),
            pltpu.VMEM((TPD, 8, 128), F32),
            pltpu.VMEM(tiles, F32),
            pltpu.VMEM(tiles, F32),
            pltpu.VMEM(tiles, F32),
            pltpu.SMEM((TPD,), jnp.int32),
            pltpu.SMEM((TPD,), jnp.int32),
            pltpu.SMEM((peers,), jnp.int32),
            pltpu.SemaphoreType.DMA((2,)),
            pltpu.SemaphoreType.DMA((TPD // SIDE,)),
            pltpu.SemaphoreType.DMA((2, TPD // SIDE)),
        ],
        name="fire",
        compiler_params=params(12),
        cost_estimate=pl.CostEstimate(
            flops=50_000_000, bytes_accessed=6_500_000, transcendentals=3_200_000
        ),
    )(far(owners), far(places), *(near(a) for a in (winds, level_set, fuel_load)), far(spread_base), *waits)


def row_kernel(outbox_ref, one_x_ref, two_x_ref, outbox_out, west_ref, east_ref):
    outbox_out[...] = outbox_ref[...]
    even, _ = place_on("gx")
    west_ref[...] = jnp.where(even, two_x_ref[...], one_x_ref[...])
    east_ref[...] = jnp.where(even, one_x_ref[...], two_x_ref[...])


def sort_rows(outbox, one_x, two_x):
    row = pltpu.VMEM((LZ, 128), F32)
    return pl.pallas_call(
        row_kernel,
        in_specs=[LOCAL] * 3,
        out_specs=[LOCAL] * 3,
        out_shape=[pltpu.VMEM(outbox.shape, F32), row, row],
        name="sort_rows",
        compiler_params=params(4),
    )(near(outbox), near(one_x), near(two_x))


def final_kernel(inbox_ref, part_ref, out_ref, field, result, sems):
    inbox = inbox_ref[...]
    rows = inbox.shape[0] * 8
    values = inbox.reshape(rows, 128)
    lane = iota(1, (rows, 128)).astype(F32)
    hot = jnp.where(lane == values[:, TA : TA + 1], 1.0, 0.0)
    y_own = values[:, TA + 1 : TA + 2]
    spread = jnp.zeros((rows, 128), F32)
    for b in range(TA):
        spread = jnp.where(lane == y_own + float(b), values[:, b : b + 1], spread)
    total = lax.dot_general(
        hot, spread, (((0,), (0,)), ((), ())),
        precision=lax.Precision.HIGHEST, preferred_element_type=F32,
    )
    field[...] = total[:CX]

    def copy(g):
        part = pl.ds(g * GROUP, GROUP)
        return pltpu.make_async_copy(result.at[part], out_ref.at[part], sems.at[g])

    def one(g, carry):
        for k in range(GROUP):
            z = g * GROUP + k
            height = jnp.full((8, 128), z, jnp.int32).astype(F32)
            gain = heat_gain * jnp.exp((height + 0.5) * (-4.0 / LZ))
            result[z] = part_ref[z] + field[...] * jnp.concatenate([gain] * (CX // 8), axis=0)
        copy(g).start()
        return carry

    lax.fori_loop(0, GROUPS, one, 0)
    for g in range(GROUPS):
        copy(g).wait()


def finish(inbox, part):
    return pl.pallas_call(
        final_kernel,
        in_specs=[LOCAL, LOCAL],
        out_specs=ANYWHERE,
        out_shape=jax.ShapeDtypeStruct((LZ, CX, CY), F32),
        scratch_shapes=[
            pltpu.VMEM((CX, CY), F32),
            pltpu.VMEM((LZ, CX, CY), F32),
            pltpu.SemaphoreType.DMA((GROUPS,)),
        ],
        name="finish",
        compiler_params=params(8),
        cost_estimate=pl.CostEstimate(flops=3_000_000, bytes_accessed=2_700_000, transcendentals=0),
    )(near(inbox), near(part))


def swapped(one, two, axis):
    count = lax.axis_size(axis)
    pairs = [(i, i ^ 1) for i in range(count)]
    others = [((i + 1) % count, ((i ^ 1) + 1) % count) for i in range(count)]
    return lax.ppermute(one, axis, pairs), lax.ppermute(two, axis, others)


def exchange(cells):
    return lax.all_to_all(cells, "gx", split_axis=0, concat_axis=0, tiled=True)


def body(theta, wind_u, wind_v, level_set, fuel_load, spread_base, tile_owner, tile_place):
    peers = lax.axis_size("gx")
    owners, places = tile_owner[0, 0], tile_place[0, 0]
    requests = make_requests(owners, places, peers)
    asked = exchange(requests)

    block, one_x, two_x, one_y, two_y = make_edges(requests, theta, wind_u, wind_v)
    rims_y = swapped(one_y, two_y, "gy")

    patches, one_x, two_x = cut_patches(asked, block, *rims_y, one_x, two_x)
    winds = exchange(patches)
    rims_x = swapped(one_x, two_x, "gx")

    level_out, fuel_out, outbox = fire(
        owners, places, winds, level_set[0, 0], fuel_load[0, 0], spread_base[0, 0], peers, ()
    )
    outbox, west, east = sort_rows(outbox, *rims_x)
    part = advect(theta, wind_u, wind_v, west, east, *rims_y)
    inbox = exchange(outbox)
    theta_next = finish(inbox, part)
    return (theta_next, level_out[None, None], fuel_out[None, None])


def solution(mesh):
    in_specs = (
        P(None, "gx", "gy"),
        P(None, "gx", "gy"),
        P(None, "gx", "gy"),
        P("gx", "gy", None, None, None),
        P("gx", "gy", None, None, None),
        P("gx", "gy", None, None, None),
        P("gx", "gy", None),
        P("gx", "gy", None),
    )
    out_specs = (
        P(None, "gx", "gy"),
        P("gx", "gy", None, None, None),
        P("gx", "gy", None, None, None),
    )
    return jax.shard_map(body, mesh=mesh, in_specs=in_specs, out_specs=out_specs, check_vma=False)
```

```python
import functools

import jax
import jax.numpy as jnp
from jax import lax
from jax.experimental import pallas as pl
from jax.experimental.pallas import tpu as pltpu
from jax.sharding import PartitionSpec as P

LZ = 80
TA = 4
R = 32
KSUB = 6
CAP = 2
TPD = 16
S = 128
CX = 64
CY = 128
ROWS = S // 8
RIM = 8
SIDES = (0, 1, -1)
WIND = 100
GROUP = 8
GROUPS = LZ // GROUP
SIDE = 4
AHEAD = 2

time_step = 0.03
diffusion = 0.15
burn_rate = 0.15
regular = 0.01
courant = 0.4
heat_gain = 2.0

F32 = jnp.float32
LOCAL = pl.BlockSpec(memory_space=pltpu.VMEM)
FAR = pl.BlockSpec(memory_space=pltpu.HBM)
ANYWHERE = pl.BlockSpec(memory_space=pl.ANY)
SCALARS = pl.BlockSpec(memory_space=pltpu.SMEM)


def iota(dim, shape=(8, 128)):
    return lax.broadcasted_iota(jnp.int32, shape, dim)


def near(cells):
    return pltpu.with_memory_space_constraint(cells, pltpu.VMEM)


def far(cells):
    return pltpu.with_memory_space_constraint(cells, pltpu.HBM)


def params(mib):
    return pltpu.CompilerParams(vmem_limit_bytes=mib * 1024 * 1024)


def to_scalars(refs, scalars, sems, others=()):
    copies = [pltpu.make_async_copy(ref, own, sems.at[c]) for c, (ref, own) in enumerate(zip(refs, scalars))]
    for copy in [*copies, *others]:
        copy.start()
    for copy in copies:
        copy.wait()


def ranks_of(owner_ref, count, peers):
    for d in range(peers):
        count[d] = 0
    ranks = []
    for t in range(TPD):
        owner = owner_ref[t]
        ranks.append(count[owner])
        count[owner] = ranks[t] + 1
    return ranks


def request_kernel(
    owner_far, place_far, theta_ref, u_ref, v_ref, out_ref, theta_out, block_ref,
    owner_ref, place_ref, table, count, sems, far_sems,
):
    pairs = [(ref.at[0], block_ref.at[c * CX : (c + 1) * CX]) for c, ref in enumerate((u_ref, v_ref))]
    pairs += [(theta_ref.at[pl.ds(g * LZ // 4, LZ // 4)], theta_out.at[pl.ds(g * LZ // 4, LZ // 4)]) for g in range(4)]
    copies = [pltpu.make_async_copy(source, target, far_sems.at[i]) for i, (source, target) in enumerate(pairs)]
    to_scalars((owner_far, place_far), (owner_ref, place_ref), sems, copies)
    peers = out_ref.shape[0]
    for i in range((peers + 2) * CAP):
        table[i] = -1
    ranks = ranks_of(owner_ref, count, peers)
    for t in range(TPD):
        table[(owner_ref[t] + 1) * CAP + ranks[t]] = place_ref[t]
    lane = iota(1, (1, 128))
    for peer in range(peers):
        line = jnp.full((1, 128), -1, jnp.int32)
        for g, side in enumerate(SIDES):
            for r in range(CAP):
                line = jnp.where(lane == g * CAP + r, table[(peer + 1 + side) * CAP + r], line)
        out_ref[peer] = jnp.broadcast_to(line, (8, 128))
    for copy in copies:
        copy.wait()


def make_requests(owners, places, theta, wind_u, wind_v, peers):
    return pl.pallas_call(
        request_kernel,
        in_specs=[FAR] * 5,
        out_specs=[LOCAL] * 3,
        out_shape=[
            pltpu.VMEM((peers, 8, 128), jnp.int32),
            pltpu.VMEM((LZ, CX, CY), F32),
            pltpu.VMEM((2 * CX, 128), F32),
        ],
        scratch_shapes=[
            pltpu.SMEM((TPD,), jnp.int32),
            pltpu.SMEM((TPD,), jnp.int32),
            pltpu.SMEM(((peers + 2) * CAP,), jnp.int32),
            pltpu.SMEM((peers,), jnp.int32),
            pltpu.SemaphoreType.DMA((2,)),
            pltpu.SemaphoreType.DMA((6,)),
        ],
        name="make_requests",
        compiler_params=params(4),
    )(*(far(a) for a in (owners, places, theta, wind_u, wind_v)))


def place_on(axis):
    index = lax.axis_index(axis)
    even = lax.rem(index, 2) == 0
    return even, jnp.logical_or(index == 0, index == lax.axis_size(axis) - 1)


def edge_kernel(theta, block_ref, one_x_ref, two_x_ref, one_y_ref, two_y_ref):
    even_x, wraps_x = place_on("gx")
    even_y, wraps_y = place_on("gy")
    lane = iota(1, (CX, 128))

    def one(i, carry):
        first, last = carry
        g = GROUPS - 1 - i
        first = pltpu.roll(first, GROUP, 1)
        last = pltpu.roll(last, GROUP, 1)
        for k in range(GROUP):
            z = g * GROUP + k
            cells = theta[z]
            low, high = cells[0:1], cells[CX - 1 : CX]
            one_x_ref[pl.ds(z, 1)] = jnp.where(even_x, high, low)
            two_x_ref[pl.ds(z, 1)] = jnp.where(wraps_x, 0.0, jnp.where(even_x, low, high))
            turned = pltpu.roll(cells, k + 1, 1)
            first = jnp.where(lane == k + 1, turned, first)
            last = jnp.where(lane == k, turned, last)
        return first, last

    zero = jnp.zeros((CX, 128), F32)
    first, last = lax.fori_loop(0, GROUPS, one, (zero, zero))
    for c in range(2):
        cells = block_ref[c * CX : (c + 1) * CX]
        first = jnp.where(lane == WIND + c, pltpu.roll(cells, WIND + c, 1), first)
        last = jnp.where(lane == WIND + c, pltpu.roll(cells, WIND + c + 1, 1), last)
    one_y_ref[...] = jnp.where(even_y, last, first)
    two_y_ref[...] = jnp.where(wraps_y, 0.0, jnp.where(even_y, first, last))


def make_edges(theta, block):
    row = pltpu.VMEM((LZ, 128), F32)
    column = pltpu.VMEM((CX, 128), F32)
    return pl.pallas_call(
        edge_kernel,
        in_specs=[LOCAL] * 2,
        out_specs=[LOCAL] * 4,
        out_shape=[row, row, column, column],
        name="edges",
        compiler_params=params(4),
        cost_estimate=pl.CostEstimate(flops=4_000_000, bytes_accessed=2_700_000, transcendentals=0),
    )(near(theta), near(block))


def cut_kernel(
    asked_far, block_ref, one_y_ref, two_y_ref, one_x_ref, two_x_ref,
    out_ref, one_x_out, two_x_out, surface, edges, asked_ref, sem,
):
    copy = pltpu.make_async_copy(asked_far.at[:, 0:1], asked_ref, sem)
    copy.start()
    one_x_out[...] = one_x_ref[...]
    two_x_out[...] = two_x_ref[...]
    even, _ = place_on("gy")
    south = jnp.where(even, two_y_ref[...], one_y_ref[...])
    north = jnp.where(even, one_y_ref[...], two_y_ref[...])
    wide = iota(1, (CX, 128))
    lane = iota(1)
    blank = jnp.zeros((RIM, 128), F32)
    for c in range(2):
        low = jnp.broadcast_to(south[:, WIND + c : WIND + c + 1], (CX, 128))
        high = jnp.broadcast_to(north[:, WIND + c : WIND + c + 1], (CX, 128))
        surface[c, 0:RIM] = blank
        surface[c, RIM : RIM + CX] = block_ref[c * CX : (c + 1) * CX]
        surface[c, RIM + CX :] = blank
        edges[c, 0:RIM] = blank
        edges[c, RIM : RIM + CX] = jnp.where(wide % 8 == 0, low, high)
        edges[c, RIM + CX :] = blank
    copy.wait()
    tiles_y = CY // TA
    for source in range(out_ref.shape[0]):
        message = jnp.zeros((8, 128), F32)
        for g, side in enumerate(SIDES):
            for r in range(CAP):
                place = asked_ref[source, 0, g * CAP + r]
                y_own = jnp.bitwise_and(place, tiles_y - 1) * TA
                first = lax.shift_right_arithmetic(place, 5) * TA - 1 + side * CX
                first = jnp.where(place < 0, CX, jnp.clip(first, -RIM, CX)) + RIM
                begin = (g * CAP + r) * 16
                outside = jnp.where(y_own == 0, 0, jnp.where(y_own == CY - TA, TA + 1, 1000))
                for c in range(2):
                    at = begin + 8 * c
                    turn = jnp.bitwise_and(at + 1 - y_own, 127)
                    part = pltpu.roll(surface[c, pl.ds(first, 8), :], turn, 1)
                    part = jnp.where(lane == at + outside, edges[c, pl.ds(first, 8), :], part)
                    message = jnp.where(lane // 8 == at // 8, part, message)
        out_ref[source] = message


def cut_patches(asked, block, one_y, two_y, one_x, two_x):
    peers = asked.shape[0]
    row = pltpu.VMEM((LZ, 128), F32)
    rows = CX + 2 * RIM
    return pl.pallas_call(
        cut_kernel,
        in_specs=[LOCAL] * 6,
        out_specs=[LOCAL] * 3,
        out_shape=[pltpu.VMEM((peers, 8, 128), F32), row, row],
        scratch_shapes=[
            pltpu.VMEM((2, rows, 128), F32),
            pltpu.VMEM((2, rows, 128), F32),
            pltpu.SMEM((peers, 1, 128), jnp.int32),
            pltpu.SemaphoreType.DMA(()),
        ],
        name="cut_patches",
        compiler_params=params(4),
    )(*(near(a) for a in (asked, block, one_y, two_y, one_x, two_x)))


def advect_kernel(
    theta_ref, u_ref, v_ref, west_ref, east_ref, one_y_ref, two_y_ref,
    out_ref, theta, wind_u, wind_v, sems,
):
    def copies(g):
        part = pl.ds(g * GROUP, GROUP)
        pairs = ((theta_ref, theta), (u_ref, wind_u), (v_ref, wind_v))
        return [
            pltpu.make_async_copy(source.at[part], target.at[part], sems.at[c, g])
            for c, (source, target) in enumerate(pairs)
        ]

    for g in range(GROUPS):
        for copy in copies(g):
            copy.start()
    even, _ = place_on("gy")
    south = jnp.where(even, two_y_ref[...], one_y_ref[...])
    north = jnp.where(even, one_y_ref[...], two_y_ref[...])
    lane = iota(1, (CX, 128))
    row = iota(0, (CX, 128))

    def one(g, carry):
        south_all, north_all = carry
        for copy in copies(g):
            copy.wait()
        def begin(k):
            t = theta[g * GROUP + k]
            rolled = [pltpu.roll(t, 1, 1), pltpu.roll(t, CY - 1, 1)]
            rims = [pltpu.roll(south_all, (128 - k) % 128, 1), pltpu.roll(north_all, 126 - k, 1)]
            return t, rolled, rims

        def end(k, begun):
            z = g * GROUP + k
            t, rolled, rims = begun
            u = wind_u[z]
            v = wind_v[z]
            west = jnp.where(row == 0, west_ref[pl.ds(z, 1)], pltpu.roll(t, 1, 0))
            east = jnp.where(row == CX - 1, east_ref[pl.ds(z, 1)], pltpu.roll(t, CX - 1, 0))
            south = jnp.where(lane == 0, rims[0], rolled[0])
            north = jnp.where(lane == CY - 1, rims[1], rolled[1])
            change = jnp.abs(u) * (t - jnp.where(u > 0, west, east)) + jnp.abs(v) * (
                t - jnp.where(v > 0, south, north)
            )
            out_ref[z] = t - courant * change

        begun = [begin(k) for k in range(AHEAD)]
        for k in range(GROUP):
            if k + AHEAD < GROUP:
                begun.append(begin(k + AHEAD))
            end(k, begun[k])
        return pltpu.roll(south_all, 128 - GROUP, 1), pltpu.roll(north_all, 128 - GROUP, 1)

    lax.fori_loop(0, GROUPS, one, (south, north))


def advect(theta, wind_u, wind_v, *rims):
    whole = pltpu.VMEM((LZ, CX, CY), F32)
    return pl.pallas_call(
        advect_kernel,
        in_specs=[FAR] * 3 + [LOCAL] * 4,
        out_specs=LOCAL,
        out_shape=whole,
        scratch_shapes=[
            whole,
            whole,
            whole,
            pltpu.SemaphoreType.DMA((3, GROUPS)),
        ],
        name="advect",
        compiler_params=params(12),
        cost_estimate=pl.CostEstimate(flops=14_000_000, bytes_accessed=8_000_000, transcendentals=0),
    )(far(theta), far(wind_u), far(wind_v), *(near(a) for a in rims))


def tile_kernel(after_ref, level_ref, fuel_ref, base_ref, out_ref, level, fuel, base, sems):
    def copies(i):
        some = pl.ds(i * SIDE, SIDE)
        pairs = ((level_ref, level), (fuel_ref, fuel), (base_ref, base))
        return [
            pltpu.make_async_copy(source.at[some], target.at[some], sems.at[c, i])
            for c, (source, target) in enumerate(pairs)
        ]

    for i in range(TPD // SIDE):
        for copy in copies(i):
            copy.start()

    def some(i, carry):
        for copy in copies(i):
            copy.wait()
        for j in range(SIDE):
            t = i * SIDE + j
            cells = [fuel[t, pl.ds(k, 8, stride=ROWS), :] for k in range(ROWS)]
            out_ref[t, 3 * ROWS] = sum(cells[1:], cells[0])
            for k in range(ROWS):
                out_ref[t, ROWS + k] = cells[k]
                out_ref[t, k] = level[t, pl.ds(k, 8, stride=ROWS), :]
                out_ref[t, 2 * ROWS + k] = base[t, pl.ds(k, 8, stride=ROWS), :] * (0.5 * time_step)
        return carry

    lax.fori_loop(0, TPD // SIDE, some, 0)


def prepare_tiles(after, level_set, fuel_load, spread_base):
    tiles = pltpu.VMEM((TPD, S, S), F32)
    return pl.pallas_call(
        tile_kernel,
        in_specs=[ANYWHERE, FAR, FAR, FAR],
        out_specs=LOCAL,
        out_shape=pltpu.VMEM((TPD, 3 * ROWS + 1, 8, 128), F32),
        scratch_shapes=[tiles, tiles, tiles, pltpu.SemaphoreType.DMA((3, TPD // SIDE))],
        name="prepare_tiles",
        compiler_params=params(8),
        cost_estimate=pl.CostEstimate(flops=300_000, bytes_accessed=3_200_000, transcendentals=0),
    )(after, *(far(a) for a in (level_set, fuel_load, spread_base)))


def fire_kernel(
    peers, waits, owner_far, place_far, winds_ref, tile_ref, *rest
):
    (
        level_out, fuel_out, outbox, begins, slopes, heats,
        level_own, fuel_own, owner_ref, place_ref, count, scalar_sems, out_sems,
    ) = rest[waits:]
    lane = iota(1)
    row = iota(0)

    def results(i):
        some = pl.ds(i * SIDE, SIDE)
        pairs = ((level_own, level_out), (fuel_own, fuel_out))
        return [
            pltpu.make_async_copy(source.at[some], target.at[some], out_sems.at[c, i])
            for c, (source, target) in enumerate(pairs)
        ]

    to_scalars((owner_far, place_far), (owner_ref, place_ref), scalar_sems)

    tiles_y = CY // TA
    low_row = (row + 1) // 2
    low_lane = (lane + R // 2) // R
    part_row = jnp.where(row % 2 == 0, 0.5, 0.0) + 0.5 / R
    part_lane = (lane.astype(F32) + 0.5) / R + 0.5 - low_lane.astype(F32)

    ranks = ranks_of(owner_ref, count, peers)
    patches = []
    for t in range(TPD):
        owner = owner_ref[t]
        parts = []
        for g, side in enumerate(SIDES):
            begin = (g * CAP + ranks[t]) * 16
            inside = jnp.logical_and(owner >= side, owner - side < peers)
            part = winds_ref[jnp.clip(owner - side, 0, peers - 1)]
            part = jnp.where(inside, part, 0.0)
            parts.append([pltpu.roll(part, jnp.bitwise_and(-begin - 8 * c, 127), 1) for c in range(2)])
        for c in range(2):
            patches.append(parts[0][c] + parts[1][c] + parts[2][c])
    left = [jnp.take_along_axis(p, low_lane, axis=1) for p in patches]
    right = [jnp.take_along_axis(p, low_lane + 1, axis=1) for p in patches]
    fine = [p + (q - p) * part_lane for p, q in zip(left, right)]
    below = [jnp.take_along_axis(p, low_row, axis=0) for p in fine]
    above = [jnp.take_along_axis(p, low_row + 1, axis=0) for p in fine]
    for i, (p, q) in enumerate(zip(below, above)):
        begins[i] = p + (q - p) * part_row
        slopes[i] = (q - p) * (1.0 / R)

    def burn(t):
        begin = [begins[2 * t + c] for c in range(2)]
        slope = [slopes[2 * t + c] for c in range(2)]
        level = [tile_ref[t, k] for k in range(ROWS)]
        fuel = [tile_ref[t, ROWS + k] for k in range(ROWS)]
        rate = [tile_ref[t, 2 * ROWS + k] for k in range(ROWS)]
        wind = [[begin[c] + slope[c] * float(k) for k in range(ROWS)] for c in range(2)]
        yield
        for _ in range(KSUB):
            before = jnp.where(row == 0, level[0], pltpu.roll(level[-1], 1, 0))
            after = jnp.where(row == 7, level[-1], pltpu.roll(level[0], 7, 0))
            rimmed = [before, *level, after]
            south = [jnp.where(lane == 0, cell, pltpu.roll(cell, 1, 1)) for cell in level]
            north = [jnp.where(lane == S - 1, cell, pltpu.roll(cell, S - 1, 1)) for cell in level]
            yield
            new = []
            for k in range(ROWS):
                cell = rimmed[k + 1]
                west, east = rimmed[k], rimmed[k + 2]
                dx = east - west
                dy = north[k] - south[k]
                square = dx * dx + dy * dy + 4.0 * regular
                length = square * lax.rsqrt(square)
                move = jnp.maximum(length + (wind[0][k] * dx + wind[1][k] * dy), 0.0)
                around = (east + west) + (north[k] + south[k])
                cell = cell * (1.0 - 4.0 * diffusion) + around * diffusion - rate[k] * move
                fuel[k] = fuel[k] * (jnp.tanh(cell) + (2.0 / burn_rate - 1.0))
                new.append(cell)
            level = new
        fuel = [cell * (0.5 * burn_rate) ** KSUB for cell in fuel]
        yield
        for k in range(ROWS):
            level_own[t, pl.ds(k, 8, stride=ROWS), :] = level[k]
            fuel_own[t, pl.ds(k, 8, stride=ROWS), :] = fuel[k]
        heats[t] = (tile_ref[t, 3 * ROWS] - sum(fuel[1:], fuel[0])) * (1.0 / (R * R))

    def some(i, carry):
        tiles = [i * SIDE + j for j in range(SIDE)]
        works = [burn(t) for t in tiles]
        while works:
            works = [w for w in works if next(w, works) is None]
        for copy in results(i):
            copy.start()
        return carry

    lax.fori_loop(0, TPD // SIDE, some, 0)

    for d in range(peers):
        outbox[d] = jnp.where(lane < TA, 0.0, -1.0)
    pairs = [heats[t] for t in range(TPD)]
    pairs = [h + pltpu.roll(h, 7, 0) for h in pairs]
    pairs = [jnp.take_along_axis(h, jnp.minimum(2 * row, 7), axis=0) for h in pairs]
    sums = [
        [jnp.sum(jnp.where(lane // R == b, h, 0.0), axis=1, keepdims=True) for b in range(TA)] for h in pairs
    ]
    for t in range(TPD):
        place = place_ref[t]
        x_own = place // tiles_y * TA
        y_own = lax.rem(place, tiles_y) * TA
        message = jnp.where(lane == TA, (x_own + row).astype(F32), y_own.astype(F32))
        for b in range(TA):
            message = jnp.where(lane == b, sums[t][b], message)
        outbox[owner_ref[t], pl.ds(ranks[t] * TA, TA), :] = message[0:TA]
    for i in range(TPD // SIDE):
        for copy in results(i):
            copy.wait()


def fire(owners, places, winds, tiles_near, peers, waits):
    tiles = (TPD, S, S)
    return pl.pallas_call(
        functools.partial(fire_kernel, peers, len(waits)),
        in_specs=[FAR, FAR, LOCAL, LOCAL] + [ANYWHERE] * len(waits),
        out_specs=[ANYWHERE, ANYWHERE, LOCAL],
        out_shape=[
            jax.ShapeDtypeStruct(tiles, F32),
            jax.ShapeDtypeStruct(tiles, F32),
            pltpu.VMEM((peers, 8, 128), F32),
        ],
        scratch_shapes=[
            pltpu.VMEM((2 * TPD, 8, 128), F32),
            pltpu.VMEM((2 * TPD, 8, 128), F32),
            pltpu.VMEM((TPD, 8, 128), F32),
            pltpu.VMEM(tiles, F32),
            pltpu.VMEM(tiles, F32),
            pltpu.SMEM((TPD,), jnp.int32),
            pltpu.SMEM((TPD,), jnp.int32),
            pltpu.SMEM((peers,), jnp.int32),
            pltpu.SemaphoreType.DMA((2,)),
            pltpu.SemaphoreType.DMA((2, TPD // SIDE)),
        ],
        name="fire",
        compiler_params=params(12),
        cost_estimate=pl.CostEstimate(
            flops=50_000_000, bytes_accessed=6_500_000, transcendentals=3_200_000
        ),
    )(far(owners), far(places), near(winds), near(tiles_near), *waits)


def row_kernel(outbox_ref, one_x_ref, two_x_ref, outbox_out, west_ref, east_ref):
    outbox_out[...] = outbox_ref[...]
    even, _ = place_on("gx")
    west_ref[...] = jnp.where(even, two_x_ref[...], one_x_ref[...])
    east_ref[...] = jnp.where(even, one_x_ref[...], two_x_ref[...])


def sort_rows(outbox, one_x, two_x):
    row = pltpu.VMEM((LZ, 128), F32)
    return pl.pallas_call(
        row_kernel,
        in_specs=[LOCAL] * 3,
        out_specs=[LOCAL] * 3,
        out_shape=[pltpu.VMEM(outbox.shape, F32), row, row],
        name="sort_rows",
        compiler_params=params(4),
    )(near(outbox), near(one_x), near(two_x))


def final_kernel(inbox_ref, part_ref, out_ref, field, result, sems):
    inbox = inbox_ref[...]
    rows = inbox.shape[0] * 8
    values = inbox.reshape(rows, 128)
    lane = iota(1, (rows, 128)).astype(F32)
    hot = jnp.where(lane == values[:, TA : TA + 1], 1.0, 0.0)
    y_own = values[:, TA + 1 : TA + 2]
    spread = jnp.zeros((rows, 128), F32)
    for b in range(TA):
        spread = jnp.where(lane == y_own + float(b), values[:, b : b + 1], spread)
    total = lax.dot_general(
        hot, spread, (((0,), (0,)), ((), ())),
        precision=lax.Precision.HIGHEST, preferred_element_type=F32,
    )
    field[...] = total[:CX]

    def copy(g):
        part = pl.ds(g * GROUP, GROUP)
        return pltpu.make_async_copy(result.at[part], out_ref.at[part], sems.at[g])

    def one(g, carry):
        for k in range(GROUP):
            z = g * GROUP + k
            height = jnp.full((8, 128), z, jnp.int32).astype(F32)
            gain = heat_gain * jnp.exp((height + 0.5) * (-4.0 / LZ))
            result[z] = part_ref[z] + field[...] * jnp.concatenate([gain] * (CX // 8), axis=0)
        copy(g).start()
        return carry

    lax.fori_loop(0, GROUPS, one, 0)
    for g in range(GROUPS):
        copy(g).wait()


def finish(inbox, part):
    return pl.pallas_call(
        final_kernel,
        in_specs=[LOCAL, LOCAL],
        out_specs=ANYWHERE,
        out_shape=jax.ShapeDtypeStruct((LZ, CX, CY), F32),
        scratch_shapes=[
            pltpu.VMEM((CX, CY), F32),
            pltpu.VMEM((LZ, CX, CY), F32),
            pltpu.SemaphoreType.DMA((GROUPS,)),
        ],
        name="finish",
        compiler_params=params(8),
        cost_estimate=pl.CostEstimate(flops=3_000_000, bytes_accessed=2_700_000, transcendentals=0),
    )(near(inbox), near(part))


def swapped_y(one, two):
    count = lax.axis_size("gy")
    pairs = [(i, i ^ 1) for i in range(count)]
    others = [((i + 1) % count, ((i ^ 1) + 1) % count) for i in range(count)]
    return lax.ppermute(one, "gy", pairs), lax.ppermute(two, "gy", others)


def swapped_x(one, two):
    count, rows = lax.axis_size("gx"), lax.axis_size("gy")
    pairs = [(i, i ^ 1) for i in range(count)]
    others = []
    for i in range(count):
        for j in range(rows):
            to = (i, j ^ 1) if i in (0, count - 1) else (((i - 1) ^ 1) + 1, j)
            others.append((i * rows + j, to[0] * rows + to[1]))
    return lax.ppermute(one, "gx", pairs), lax.ppermute(two, ("gx", "gy"), others)


def exchange(cells):
    return lax.all_to_all(cells, "gx", split_axis=0, concat_axis=0, tiled=True)


def body(theta, wind_u, wind_v, level_set, fuel_load, spread_base, tile_owner, tile_place):
    peers = lax.axis_size("gx")
    owners, places = tile_owner[0, 0], tile_place[0, 0]
    requests, near_theta, block = make_requests(owners, places, theta, wind_u, wind_v, peers)
    asked = exchange(requests)

    one_x, two_x, one_y, two_y = make_edges(near_theta, block)
    rims_y = swapped_y(one_y, two_y)

    patches, one_x, two_x = cut_patches(asked, block, *rims_y, one_x, two_x)
    winds = exchange(patches)
    rims_x = swapped_x(one_x, two_x)

    tiles_near = prepare_tiles(patches, level_set[0, 0], fuel_load[0, 0], spread_base[0, 0])
    level_out, fuel_out, outbox = fire(owners, places, winds, tiles_near, peers, ())
    outbox, west, east = sort_rows(outbox, *rims_x)
    part = advect(theta, wind_u, wind_v, west, east, *rims_y)
    inbox = exchange(outbox)
    theta_next = finish(inbox, part)
    return (theta_next, level_out[None, None], fuel_out[None, None])


def solution(mesh):
    in_specs = (
        P(None, "gx", "gy"),
        P(None, "gx", "gy"),
        P(None, "gx", "gy"),
        P("gx", "gy", None, None, None),
        P("gx", "gy", None, None, None),
        P("gx", "gy", None, None, None),
        P("gx", "gy", None),
        P("gx", "gy", None),
    )
    out_specs = (
        P(None, "gx", "gy"),
        P("gx", "gy", None, None, None),
        P("gx", "gy", None, None, None),
    )
    return jax.shard_map(body, mesh=mesh, in_specs=in_specs, out_specs=out_specs, check_vma=False)
```

```python
import functools

import jax
import jax.numpy as jnp
from jax import lax
from jax.experimental import pallas as pl
from jax.experimental.pallas import tpu as pltpu
from jax.sharding import PartitionSpec as P

LZ = 80
TA = 4
R = 32
KSUB = 6
CAP = 2
TPD = 16
S = 128
CX = 64
CY = 128
ROWS = S // 8
RIM = 8
SIDES = (0, 1, -1)
WIND = 100
GROUP = 8
GROUPS = LZ // GROUP
SIDE = 4
AHEAD = 2

time_step = 0.03
diffusion = 0.15
burn_rate = 0.15
regular = 0.01
courant = 0.4
heat_gain = 2.0

F32 = jnp.float32
LOCAL = pl.BlockSpec(memory_space=pltpu.VMEM)
FAR = pl.BlockSpec(memory_space=pltpu.HBM)
ANYWHERE = pl.BlockSpec(memory_space=pl.ANY)
SCALARS = pl.BlockSpec(memory_space=pltpu.SMEM)


def iota(dim, shape=(8, 128)):
    return lax.broadcasted_iota(jnp.int32, shape, dim)


def near(cells):
    return pltpu.with_memory_space_constraint(cells, pltpu.VMEM)


def far(cells):
    return pltpu.with_memory_space_constraint(cells, pltpu.HBM)


def params(mib):
    return pltpu.CompilerParams(vmem_limit_bytes=mib * 1024 * 1024)


def to_scalars(refs, scalars, sems, others=()):
    copies = [pltpu.make_async_copy(ref, own, sems.at[c]) for c, (ref, own) in enumerate(zip(refs, scalars))]
    for copy in [*copies, *others]:
        copy.start()
    for copy in copies:
        copy.wait()


def ranks_of(owner_ref, count, peers):
    for d in range(peers):
        count[d] = 0
    ranks = []
    for t in range(TPD):
        owner = owner_ref[t]
        ranks.append(count[owner])
        count[owner] = ranks[t] + 1
    return ranks


def request_kernel(owner_far, place_far, out_ref, owner_ref, place_ref, table, count, sems):
    to_scalars((owner_far, place_far), (owner_ref, place_ref), sems)
    peers = out_ref.shape[0]
    for i in range((peers + 2) * CAP):
        table[i] = -1
    ranks = ranks_of(owner_ref, count, peers)
    for t in range(TPD):
        table[(owner_ref[t] + 1) * CAP + ranks[t]] = place_ref[t]
    lane = iota(1, (1, 128))
    for peer in range(peers):
        line = jnp.full((1, 128), -1, jnp.int32)
        for g, side in enumerate(SIDES):
            for r in range(CAP):
                line = jnp.where(lane % 8 == g * CAP + r, table[(peer + 1 + side) * CAP + r], line)
        out_ref[peer] = jnp.broadcast_to(line, (8, 128))


def make_requests(owners, places, peers):
    return pl.pallas_call(
        request_kernel,
        in_specs=[FAR, FAR],
        out_specs=LOCAL,
        out_shape=pltpu.VMEM((peers, 8, 128), jnp.int32),
        scratch_shapes=[
            pltpu.SMEM((TPD,), jnp.int32),
            pltpu.SMEM((TPD,), jnp.int32),
            pltpu.SMEM(((peers + 2) * CAP,), jnp.int32),
            pltpu.SMEM((peers,), jnp.int32),
            pltpu.SemaphoreType.DMA((2,)),
        ],
        name="make_requests",
        compiler_params=params(4),
    )(far(owners), far(places))


def place_on(axis):
    index = lax.axis_index(axis)
    even = lax.rem(index, 2) == 0
    return even, jnp.logical_or(index == 0, index == lax.axis_size(axis) - 1)


def edge_kernel(
    after_ref, theta_ref, u_ref, v_ref,
    block_ref, one_x_ref, two_x_ref, one_y_ref, two_y_ref, theta, sems, wind_sems,
):
    even_x, wraps_x = place_on("gx")
    even_y, wraps_y = place_on("gy")

    def copy(g):
        part = pl.ds(g * GROUP, GROUP)
        return pltpu.make_async_copy(theta_ref.at[part], theta.at[part], sems.at[g])

    winds = [
        pltpu.make_async_copy(ref.at[0], block_ref.at[c * CX : (c + 1) * CX], wind_sems.at[c])
        for c, ref in enumerate((u_ref, v_ref))
    ]
    for g in range(GROUPS):
        copy(g).start()
    for wind in winds:
        wind.start()
    lane = iota(1, (CX, 128))

    first = last = jnp.zeros((CX, 128), F32)
    for z in range(LZ):
        if z % GROUP == 0:
            copy(z // GROUP).wait()
        cells = theta[z]
        low, high = cells[0:1], cells[CX - 1 : CX]
        one_x_ref[z : z + 1] = jnp.where(even_x, high, low)
        two_x_ref[z : z + 1] = jnp.where(wraps_x, 0.0, jnp.where(even_x, low, high))
        turned = pltpu.roll(cells, z + 1, 1)
        first = jnp.where(lane == z + 1, turned, first)
        last = jnp.where(lane == z, turned, last)
    for wind in winds:
        wind.wait()
    for c in range(2):
        cells = block_ref[c * CX : (c + 1) * CX]
        first = jnp.where(lane == WIND + c, pltpu.roll(cells, WIND + c, 1), first)
        last = jnp.where(lane == WIND + c, pltpu.roll(cells, WIND + c + 1, 1), last)
    one_y_ref[...] = jnp.where(even_y, last, first)
    two_y_ref[...] = jnp.where(wraps_y, 0.0, jnp.where(even_y, first, last))


def make_edges(after, theta, wind_u, wind_v):
    row = pltpu.VMEM((LZ, 128), F32)
    column = pltpu.VMEM((CX, 128), F32)
    return pl.pallas_call(
        edge_kernel,
        in_specs=[ANYWHERE, FAR, FAR, FAR],
        out_specs=[LOCAL] * 5,
        out_shape=[pltpu.VMEM((2 * CX, 128), F32), row, row, column, column],
        scratch_shapes=[
            pltpu.VMEM((LZ, CX, CY), F32),
            pltpu.SemaphoreType.DMA((GROUPS,)),
            pltpu.SemaphoreType.DMA((2,)),
        ],
        name="edges",
        compiler_params=params(8),
        cost_estimate=pl.CostEstimate(flops=4_000_000, bytes_accessed=2_700_000, transcendentals=0),
    )(after, far(theta), far(wind_u), far(wind_v))


def cut_kernel(
    asked_far, block_ref, one_y_ref, two_y_ref, one_x_ref, two_x_ref,
    out_ref, one_x_out, two_x_out, surface, edges, plan, asked_ref, sem,
):
    places = asked_far[...]
    peers = places.shape[0]
    at = iota(2, (peers, 8, 128))
    tiles_y = CY // TA
    y_own = jnp.bitwise_and(places, tiles_y - 1) * TA
    kind = at % 8 // CAP
    first = lax.shift_right_arithmetic(places, 5) * TA - 1
    first = first + jnp.where(kind == 0, SIDES[0], jnp.where(kind == 1, SIDES[1], SIDES[2])) * CX
    first = jnp.where(places < 0, CX, jnp.clip(first, -RIM, CX)) + RIM
    outside = jnp.where(y_own == 0, 0, jnp.where(y_own == CY - TA, TA + 1, 1000))
    plan[...] = jnp.where(at < 8, first, jnp.where(at < 16, jnp.bitwise_and(1 - y_own, 127), outside))
    copy = pltpu.make_async_copy(plan.at[:, 0:1], asked_ref, sem)
    copy.start()
    one_x_out[...] = one_x_ref[...]
    two_x_out[...] = two_x_ref[...]
    even, _ = place_on("gy")
    south = jnp.where(even, two_y_ref[...], one_y_ref[...])
    north = jnp.where(even, one_y_ref[...], two_y_ref[...])
    wide = iota(1, (CX, 128))
    lane = iota(1)
    blank = jnp.zeros((RIM, 128), F32)
    for c in range(2):
        low = jnp.broadcast_to(south[:, WIND + c : WIND + c + 1], (CX, 128))
        high = jnp.broadcast_to(north[:, WIND + c : WIND + c + 1], (CX, 128))
        surface[c, 0:RIM] = blank
        surface[c, RIM : RIM + CX] = block_ref[c * CX : (c + 1) * CX]
        surface[c, RIM + CX :] = blank
        edges[c, 0:RIM] = blank
        edges[c, RIM : RIM + CX] = jnp.where(wide % 8 == 0, low, high)
        edges[c, RIM + CX :] = blank
    copy.wait()
    for source in range(peers):
        message = jnp.zeros((8, 128), F32)
        for g in range(len(SIDES)):
            for r in range(CAP):
                slot = g * CAP + r
                first = asked_ref[source, 0, slot]
                turn = asked_ref[source, 0, 8 + slot]
                outside = asked_ref[source, 0, 16 + slot]
                begin = slot * 16
                for c in range(2):
                    at = begin + 8 * c
                    part = pltpu.roll(surface[c, pl.ds(first, 8), :], jnp.bitwise_and(turn + at, 127), 1)
                    part = jnp.where(lane == at + outside, edges[c, pl.ds(first, 8), :], part)
                    message = jnp.where(lane // 8 == at // 8, part, message)
        out_ref[source] = message


def cut_patches(asked, block, one_y, two_y, one_x, two_x):
    peers = asked.shape[0]
    row = pltpu.VMEM((LZ, 128), F32)
    rows = CX + 2 * RIM
    return pl.pallas_call(
        cut_kernel,
        in_specs=[LOCAL] * 6,
        out_specs=[LOCAL] * 3,
        out_shape=[pltpu.VMEM((peers, 8, 128), F32), row, row],
        scratch_shapes=[
            pltpu.VMEM((2, rows, 128), F32),
            pltpu.VMEM((2, rows, 128), F32),
            pltpu.VMEM((peers, 8, 128), jnp.int32),
            pltpu.SMEM((peers, 1, 128), jnp.int32),
            pltpu.SemaphoreType.DMA(()),
        ],
        name="cut_patches",
        compiler_params=params(4),
    )(*(near(a) for a in (asked, block, one_y, two_y, one_x, two_x)))


def advect_kernel(
    theta_ref, u_ref, v_ref, west_ref, east_ref, one_y_ref, two_y_ref,
    out_ref, theta, wind_u, wind_v, sems,
):
    def copies(g):
        part = pl.ds(g * GROUP, GROUP)
        pairs = ((theta_ref, theta), (u_ref, wind_u), (v_ref, wind_v))
        return [
            pltpu.make_async_copy(source.at[part], target.at[part], sems.at[c, g])
            for c, (source, target) in enumerate(pairs)
        ]

    for g in range(GROUPS):
        for copy in copies(g):
            copy.start()
    even, _ = place_on("gy")
    south = jnp.where(even, two_y_ref[...], one_y_ref[...])
    north = jnp.where(even, one_y_ref[...], two_y_ref[...])
    lane = iota(1, (CX, 128))
    row = iota(0, (CX, 128))

    def one(g, carry):
        south_all, north_all = carry
        for copy in copies(g):
            copy.wait()
        def begin(k):
            t = theta[g * GROUP + k]
            rolled = [pltpu.roll(t, 1, 1), pltpu.roll(t, CY - 1, 1)]
            rims = [pltpu.roll(south_all, (128 - k) % 128, 1), pltpu.roll(north_all, 126 - k, 1)]
            return t, rolled, rims

        def end(k, begun):
            z = g * GROUP + k
            t, rolled, rims = begun
            u = wind_u[z]
            v = wind_v[z]
            west = jnp.where(row == 0, west_ref[pl.ds(z, 1)], pltpu.roll(t, 1, 0))
            east = jnp.where(row == CX - 1, east_ref[pl.ds(z, 1)], pltpu.roll(t, CX - 1, 0))
            south = jnp.where(lane == 0, rims[0], rolled[0])
            north = jnp.where(lane == CY - 1, rims[1], rolled[1])
            change = jnp.abs(u) * (t - jnp.where(u > 0, west, east)) + jnp.abs(v) * (
                t - jnp.where(v > 0, south, north)
            )
            out_ref[z] = t - courant * change

        begun = [begin(k) for k in range(AHEAD)]
        for k in range(GROUP):
            if k + AHEAD < GROUP:
                begun.append(begin(k + AHEAD))
            end(k, begun[k])
        return pltpu.roll(south_all, 128 - GROUP, 1), pltpu.roll(north_all, 128 - GROUP, 1)

    lax.fori_loop(0, GROUPS, one, (south, north))


def advect(theta, wind_u, wind_v, *rims):
    whole = pltpu.VMEM((LZ, CX, CY), F32)
    return pl.pallas_call(
        advect_kernel,
        in_specs=[FAR] * 3 + [LOCAL] * 4,
        out_specs=LOCAL,
        out_shape=whole,
        scratch_shapes=[
            whole,
            whole,
            whole,
            pltpu.SemaphoreType.DMA((3, GROUPS)),
        ],
        name="advect",
        compiler_params=params(12),
        cost_estimate=pl.CostEstimate(flops=14_000_000, bytes_accessed=8_000_000, transcendentals=0),
    )(far(theta), far(wind_u), far(wind_v), *(near(a) for a in rims))


def tile_kernel(after_ref, level_ref, fuel_ref, base_ref, out_ref, level, fuel, base, sems):
    def copies(i):
        some = pl.ds(i * SIDE, SIDE)
        pairs = ((level_ref, level), (fuel_ref, fuel), (base_ref, base))
        return [
            pltpu.make_async_copy(source.at[some], target.at[some], sems.at[c, i])
            for c, (source, target) in enumerate(pairs)
        ]

    for i in range(TPD // SIDE):
        for copy in copies(i):
            copy.start()

    def some(i, carry):
        for copy in copies(i):
            copy.wait()
        for j in range(SIDE):
            t = i * SIDE + j
            cells = [fuel[t, pl.ds(k, 8, stride=ROWS), :] for k in range(ROWS)]
            out_ref[t, 3 * ROWS] = sum(cells[1:], cells[0])
            for k in range(ROWS):
                out_ref[t, ROWS + k] = cells[k]
                out_ref[t, k] = level[t, pl.ds(k, 8, stride=ROWS), :]
                out_ref[t, 2 * ROWS + k] = base[t, pl.ds(k, 8, stride=ROWS), :] * (0.5 * time_step)
        return carry

    lax.fori_loop(0, TPD // SIDE, some, 0)


def prepare_tiles(after, level_set, fuel_load, spread_base):
    tiles = pltpu.VMEM((TPD, S, S), F32)
    return pl.pallas_call(
        tile_kernel,
        in_specs=[ANYWHERE, FAR, FAR, FAR],
        out_specs=LOCAL,
        out_shape=pltpu.VMEM((TPD, 3 * ROWS + 1, 8, 128), F32),
        scratch_shapes=[tiles, tiles, tiles, pltpu.SemaphoreType.DMA((3, TPD // SIDE))],
        name="prepare_tiles",
        compiler_params=params(8),
        cost_estimate=pl.CostEstimate(flops=300_000, bytes_accessed=3_200_000, transcendentals=0),
    )(after, *(far(a) for a in (level_set, fuel_load, spread_base)))


def fire_kernel(
    peers, waits, owner_far, place_far, winds_ref, tile_ref, *rest
):
    (
        level_out, fuel_out, outbox, begins, slopes, heats,
        level_own, fuel_own, owner_ref, place_ref, count, scalar_sems, out_sems,
    ) = rest[waits:]
    lane = iota(1)
    row = iota(0)

    def results(i):
        some = pl.ds(i * SIDE, SIDE)
        pairs = ((level_own, level_out), (fuel_own, fuel_out))
        return [
            pltpu.make_async_copy(source.at[some], target.at[some], out_sems.at[c, i])
            for c, (source, target) in enumerate(pairs)
        ]

    to_scalars((owner_far, place_far), (owner_ref, place_ref), scalar_sems)

    tiles_y = CY // TA
    low_row = (row + 1) // 2
    low_lane = (lane + R // 2) // R
    part_row = jnp.where(row % 2 == 0, 0.5, 0.0) + 0.5 / R
    part_lane = (lane.astype(F32) + 0.5) / R + 0.5 - low_lane.astype(F32)

    ranks = ranks_of(owner_ref, count, peers)
    patches = []
    for t in range(TPD):
        owner = owner_ref[t]
        parts = []
        for g, side in enumerate(SIDES):
            begin = (g * CAP + ranks[t]) * 16
            inside = jnp.logical_and(owner >= side, owner - side < peers)
            part = winds_ref[jnp.clip(owner - side, 0, peers - 1)]
            part = jnp.where(inside, part, 0.0)
            parts.append([pltpu.roll(part, jnp.bitwise_and(-begin - 8 * c, 127), 1) for c in range(2)])
        for c in range(2):
            patches.append(parts[0][c] + parts[1][c] + parts[2][c])
    left = [jnp.take_along_axis(p, low_lane, axis=1) for p in patches]
    right = [jnp.take_along_axis(p, low_lane + 1, axis=1) for p in patches]
    fine = [p + (q - p) * part_lane for p, q in zip(left, right)]
    below = [jnp.take_along_axis(p, low_row, axis=0) for p in fine]
    above = [jnp.take_along_axis(p, low_row + 1, axis=0) for p in fine]
    for i, (p, q) in enumerate(zip(below, above)):
        begins[i] = p + (q - p) * part_row
        slopes[i] = (q - p) * (1.0 / R)

    def burn(t):
        begin = [begins[2 * t + c] for c in range(2)]
        slope = [slopes[2 * t + c] for c in range(2)]
        level = [tile_ref[t, k] for k in range(ROWS)]
        fuel = [tile_ref[t, ROWS + k] for k in range(ROWS)]
        rate = [tile_ref[t, 2 * ROWS + k] for k in range(ROWS)]
        wind = [[begin[c] + slope[c] * float(k) for k in range(ROWS)] for c in range(2)]
        yield
        for _ in range(KSUB):
            before = jnp.where(row == 0, level[0], pltpu.roll(level[-1], 1, 0))
            after = jnp.where(row == 7, level[-1], pltpu.roll(level[0], 7, 0))
            rimmed = [before, *level, after]
            south = [jnp.where(lane == 0, cell, pltpu.roll(cell, 1, 1)) for cell in level]
            north = [jnp.where(lane == S - 1, cell, pltpu.roll(cell, S - 1, 1)) for cell in level]
            yield
            new = []
            for k in range(ROWS):
                cell = rimmed[k + 1]
                west, east = rimmed[k], rimmed[k + 2]
                dx = east - west
                dy = north[k] - south[k]
                square = dx * dx + dy * dy + 4.0 * regular
                length = square * lax.rsqrt(square)
                move = jnp.maximum(length + (wind[0][k] * dx + wind[1][k] * dy), 0.0)
                around = (east + west) + (north[k] + south[k])
                cell = cell * (1.0 - 4.0 * diffusion) + around * diffusion - rate[k] * move
                fuel[k] = fuel[k] * (jnp.tanh(cell) + (2.0 / burn_rate - 1.0))
                new.append(cell)
            level = new
        fuel = [cell * (0.5 * burn_rate) ** KSUB for cell in fuel]
        yield
        for k in range(ROWS):
            level_own[t, pl.ds(k, 8, stride=ROWS), :] = level[k]
            fuel_own[t, pl.ds(k, 8, stride=ROWS), :] = fuel[k]
        heats[t] = (tile_ref[t, 3 * ROWS] - sum(fuel[1:], fuel[0])) * (1.0 / (R * R))

    def some(i, carry):
        tiles = [i * SIDE + j for j in range(SIDE)]
        works = [burn(t) for t in tiles]
        while works:
            works = [w for w in works if next(w, works) is None]
        for copy in results(i):
            copy.start()
        return carry

    lax.fori_loop(0, TPD // SIDE, some, 0)

    for d in range(peers):
        outbox[d] = jnp.where(lane < TA, 0.0, -1.0)
    pairs = [heats[t] for t in range(TPD)]
    pairs = [h + pltpu.roll(h, 7, 0) for h in pairs]
    pairs = [jnp.take_along_axis(h, jnp.minimum(2 * row, 7), axis=0) for h in pairs]
    sums = [
        [jnp.sum(jnp.where(lane // R == b, h, 0.0), axis=1, keepdims=True) for b in range(TA)] for h in pairs
    ]
    for t in range(TPD):
        place = place_ref[t]
        x_own = place // tiles_y * TA
        y_own = lax.rem(place, tiles_y) * TA
        message = jnp.where(lane == TA, (x_own + row).astype(F32), y_own.astype(F32))
        for b in range(TA):
            message = jnp.where(lane == b, sums[t][b], message)
        outbox[owner_ref[t], pl.ds(ranks[t] * TA, TA), :] = message[0:TA]
    for i in range(TPD // SIDE):
        for copy in results(i):
            copy.wait()


def fire(owners, places, winds, tiles_near, peers, waits):
    tiles = (TPD, S, S)
    return pl.pallas_call(
        functools.partial(fire_kernel, peers, len(waits)),
        in_specs=[FAR, FAR, LOCAL, LOCAL] + [ANYWHERE] * len(waits),
        out_specs=[ANYWHERE, ANYWHERE, LOCAL],
        out_shape=[
            jax.ShapeDtypeStruct(tiles, F32),
            jax.ShapeDtypeStruct(tiles, F32),
            pltpu.VMEM((peers, 8, 128), F32),
        ],
        scratch_shapes=[
            pltpu.VMEM((2 * TPD, 8, 128), F32),
            pltpu.VMEM((2 * TPD, 8, 128), F32),
            pltpu.VMEM((TPD, 8, 128), F32),
            pltpu.VMEM(tiles, F32),
            pltpu.VMEM(tiles, F32),
            pltpu.SMEM((TPD,), jnp.int32),
            pltpu.SMEM((TPD,), jnp.int32),
            pltpu.SMEM((peers,), jnp.int32),
            pltpu.SemaphoreType.DMA((2,)),
            pltpu.SemaphoreType.DMA((2, TPD // SIDE)),
        ],
        name="fire",
        compiler_params=params(12),
        cost_estimate=pl.CostEstimate(
            flops=50_000_000, bytes_accessed=6_500_000, transcendentals=3_200_000
        ),
    )(far(owners), far(places), near(winds), near(tiles_near), *waits)


def row_kernel(outbox_ref, one_x_ref, two_x_ref, outbox_out, west_ref, east_ref):
    outbox_out[...] = outbox_ref[...]
    even, _ = place_on("gx")
    west_ref[...] = jnp.where(even, two_x_ref[...], one_x_ref[...])
    east_ref[...] = jnp.where(even, one_x_ref[...], two_x_ref[...])


def sort_rows(outbox, one_x, two_x):
    row = pltpu.VMEM((LZ, 128), F32)
    return pl.pallas_call(
        row_kernel,
        in_specs=[LOCAL] * 3,
        out_specs=[LOCAL] * 3,
        out_shape=[pltpu.VMEM(outbox.shape, F32), row, row],
        name="sort_rows",
        compiler_params=params(4),
    )(near(outbox), near(one_x), near(two_x))


def final_kernel(inbox_ref, part_ref, out_ref, field, result, sems):
    inbox = inbox_ref[...]
    rows = inbox.shape[0] * 8
    values = inbox.reshape(rows, 128)
    lane = iota(1, (rows, 128)).astype(F32)
    hot = jnp.where(lane == values[:, TA : TA + 1], 1.0, 0.0)
    y_own = values[:, TA + 1 : TA + 2]
    spread = jnp.zeros((rows, 128), F32)
    for b in range(TA):
        spread = jnp.where(lane == y_own + float(b), values[:, b : b + 1], spread)
    total = lax.dot_general(
        hot, spread, (((0,), (0,)), ((), ())),
        precision=lax.Precision.HIGHEST, preferred_element_type=F32,
    )
    field[...] = total[:CX]

    def copy(g):
        part = pl.ds(g * GROUP, GROUP)
        return pltpu.make_async_copy(result.at[part], out_ref.at[part], sems.at[g])

    def one(g, carry):
        for k in range(GROUP):
            z = g * GROUP + k
            height = jnp.full((8, 128), z, jnp.int32).astype(F32)
            gain = heat_gain * jnp.exp((height + 0.5) * (-4.0 / LZ))
            result[z] = part_ref[z] + field[...] * jnp.concatenate([gain] * (CX // 8), axis=0)
        copy(g).start()
        return carry

    lax.fori_loop(0, GROUPS, one, 0)
    for g in range(GROUPS):
        copy(g).wait()


def finish(inbox, part):
    return pl.pallas_call(
        final_kernel,
        in_specs=[LOCAL, LOCAL],
        out_specs=ANYWHERE,
        out_shape=jax.ShapeDtypeStruct((LZ, CX, CY), F32),
        scratch_shapes=[
            pltpu.VMEM((CX, CY), F32),
            pltpu.VMEM((LZ, CX, CY), F32),
            pltpu.SemaphoreType.DMA((GROUPS,)),
        ],
        name="finish",
        compiler_params=params(8),
        cost_estimate=pl.CostEstimate(flops=3_000_000, bytes_accessed=2_700_000, transcendentals=0),
    )(near(inbox), near(part))


def swapped_y(one, two):
    count = lax.axis_size("gy")
    pairs = [(i, i ^ 1) for i in range(count)]
    others = [((i + 1) % count, ((i ^ 1) + 1) % count) for i in range(count)]
    return lax.ppermute(one, "gy", pairs), lax.ppermute(two, "gy", others)


def swapped_x(one, two):
    count, rows = lax.axis_size("gx"), lax.axis_size("gy")
    pairs = [(i, i ^ 1) for i in range(count)]
    others = []
    for i in range(count):
        for j in range(rows):
            to = (i, j ^ 1) if i in (0, count - 1) else (((i - 1) ^ 1) + 1, j)
            others.append((i * rows + j, to[0] * rows + to[1]))
    return lax.ppermute(one, "gx", pairs), lax.ppermute(two, ("gx", "gy"), others)


def exchange(cells):
    return lax.all_to_all(cells, "gx", split_axis=0, concat_axis=0, tiled=True)


def body(theta, wind_u, wind_v, level_set, fuel_load, spread_base, tile_owner, tile_place):
    peers = lax.axis_size("gx")
    owners, places = tile_owner[0, 0], tile_place[0, 0]
    requests = make_requests(owners, places, peers)
    asked = exchange(requests)

    block, one_x, two_x, one_y, two_y = make_edges(requests, theta, wind_u, wind_v)
    rims_y = swapped_y(one_y, two_y)

    patches, one_x, two_x = cut_patches(asked, block, *rims_y, one_x, two_x)
    winds = exchange(patches)
    rims_x = swapped_x(one_x, two_x)

    tiles_near = prepare_tiles(patches, level_set[0, 0], fuel_load[0, 0], spread_base[0, 0])
    level_out, fuel_out, outbox = fire(owners, places, winds, tiles_near, peers, ())
    outbox, west, east = sort_rows(outbox, *rims_x)
    part = advect(theta, wind_u, wind_v, west, east, *rims_y)
    inbox = exchange(outbox)
    theta_next = finish(inbox, part)
    return (theta_next, level_out[None, None], fuel_out[None, None])


def solution(mesh):
    in_specs = (
        P(None, "gx", "gy"),
        P(None, "gx", "gy"),
        P(None, "gx", "gy"),
        P("gx", "gy", None, None, None),
        P("gx", "gy", None, None, None),
        P("gx", "gy", None, None, None),
        P("gx", "gy", None),
        P("gx", "gy", None),
    )
    out_specs = (
        P(None, "gx", "gy"),
        P("gx", "gy", None, None, None),
        P("gx", "gy", None, None, None),
    )
    return jax.shard_map(body, mesh=mesh, in_specs=in_specs, out_specs=out_specs, check_vma=False)
```

```python
import functools

import jax
import jax.numpy as jnp
from jax import lax
from jax.experimental import pallas as pl
from jax.experimental.pallas import tpu as pltpu
from jax.sharding import PartitionSpec as P

LZ = 80
TA = 4
R = 32
KSUB = 6
CAP = 2
TPD = 16
S = 128
CX = 64
CY = 128
ROWS = S // 8
RIM = 8
SIDES = (0, 1, -1)
WIND = 100
GROUP = 8
GROUPS = LZ // GROUP
HEAD = 24
SIDE = 4
AHEAD = 2

time_step = 0.03
diffusion = 0.15
burn_rate = 0.15
regular = 0.01
courant = 0.4
heat_gain = 2.0

F32 = jnp.float32
LOCAL = pl.BlockSpec(memory_space=pltpu.VMEM)
FAR = pl.BlockSpec(memory_space=pltpu.HBM)
ANYWHERE = pl.BlockSpec(memory_space=pl.ANY)
SCALARS = pl.BlockSpec(memory_space=pltpu.SMEM)


def iota(dim, shape=(8, 128)):
    return lax.broadcasted_iota(jnp.int32, shape, dim)


def near(cells):
    return pltpu.with_memory_space_constraint(cells, pltpu.VMEM)


def far(cells):
    return pltpu.with_memory_space_constraint(cells, pltpu.HBM)


def params(mib):
    return pltpu.CompilerParams(vmem_limit_bytes=mib * 1024 * 1024)


def to_scalars(refs, scalars, sems, others=()):
    copies = [pltpu.make_async_copy(ref, own, sems.at[c]) for c, (ref, own) in enumerate(zip(refs, scalars))]
    for copy in [*copies, *others]:
        copy.start()
    for copy in copies:
        copy.wait()


def ranks_of(owner_ref, count, peers):
    for d in range(peers):
        count[d] = 0
    ranks = []
    for t in range(TPD):
        owner = owner_ref[t]
        ranks.append(count[owner])
        count[owner] = ranks[t] + 1
    return ranks


def request_kernel(
    owner_far, place_far, theta_ref, u_ref, v_ref, out_ref, head_ref, block_ref,
    owner_ref, place_ref, table, count, sems, far_sems,
):
    pairs = [(ref.at[0], block_ref.at[c * CX : (c + 1) * CX]) for c, ref in enumerate((u_ref, v_ref))]
    pairs.append((theta_ref.at[0:HEAD], head_ref))
    others = [pltpu.make_async_copy(source, target, far_sems.at[i]) for i, (source, target) in enumerate(pairs)]
    to_scalars((owner_far, place_far), (owner_ref, place_ref), sems, others)
    peers = out_ref.shape[0]
    for i in range((peers + 2) * CAP):
        table[i] = -1
    ranks = ranks_of(owner_ref, count, peers)
    for t in range(TPD):
        table[(owner_ref[t] + 1) * CAP + ranks[t]] = place_ref[t]
    lane = iota(1, (1, 128))
    for peer in range(peers):
        line = jnp.full((1, 128), -1, jnp.int32)
        for g, side in enumerate(SIDES):
            for r in range(CAP):
                line = jnp.where(lane % 8 == g * CAP + r, table[(peer + 1 + side) * CAP + r], line)
        out_ref[peer] = jnp.broadcast_to(line, (8, 128))
    for copy in others:
        copy.wait()


def make_requests(owners, places, theta, wind_u, wind_v, peers):
    return pl.pallas_call(
        request_kernel,
        in_specs=[FAR] * 5,
        out_specs=[LOCAL] * 3,
        out_shape=[
            pltpu.VMEM((peers, 8, 128), jnp.int32),
            pltpu.VMEM((HEAD, CX, CY), F32),
            pltpu.VMEM((2 * CX, 128), F32),
        ],
        scratch_shapes=[
            pltpu.SMEM((TPD,), jnp.int32),
            pltpu.SMEM((TPD,), jnp.int32),
            pltpu.SMEM(((peers + 2) * CAP,), jnp.int32),
            pltpu.SMEM((peers,), jnp.int32),
            pltpu.SemaphoreType.DMA((2,)),
            pltpu.SemaphoreType.DMA((3,)),
        ],
        name="make_requests",
        compiler_params=params(4),
    )(*(far(a) for a in (owners, places, theta, wind_u, wind_v)))


def place_on(axis):
    index = lax.axis_index(axis)
    even = lax.rem(index, 2) == 0
    return even, jnp.logical_or(index == 0, index == lax.axis_size(axis) - 1)


def edge_kernel(head_ref, block_ref, theta_ref, one_x_ref, two_x_ref, one_y_ref, two_y_ref, theta, sems):
    even_x, wraps_x = place_on("gx")
    even_y, wraps_y = place_on("gy")

    def copy(z):
        return pltpu.make_async_copy(
            theta_ref.at[z : z + GROUP], theta.at[z - HEAD : z - HEAD + GROUP], sems.at[(z - HEAD) // GROUP]
        )

    for z in range(HEAD, LZ, GROUP):
        copy(z).start()
    lane = iota(1, (CX, 128))

    first = last = jnp.zeros((CX, 128), F32)
    for z in range(LZ):
        if z >= HEAD and z % GROUP == 0:
            copy(z).wait()
        cells = head_ref[z] if z < HEAD else theta[z - HEAD]
        low, high = cells[0:1], cells[CX - 1 : CX]
        one_x_ref[z : z + 1] = jnp.where(even_x, high, low)
        two_x_ref[z : z + 1] = jnp.where(wraps_x, 0.0, jnp.where(even_x, low, high))
        turned = pltpu.roll(cells, z + 1, 1)
        first = jnp.where(lane == z + 1, turned, first)
        last = jnp.where(lane == z, turned, last)
    for c in range(2):
        cells = block_ref[c * CX : (c + 1) * CX]
        first = jnp.where(lane == WIND + c, pltpu.roll(cells, WIND + c, 1), first)
        last = jnp.where(lane == WIND + c, pltpu.roll(cells, WIND + c + 1, 1), last)
    one_y_ref[...] = jnp.where(even_y, last, first)
    two_y_ref[...] = jnp.where(wraps_y, 0.0, jnp.where(even_y, first, last))


def make_edges(head, block, theta):
    row = pltpu.VMEM((LZ, 128), F32)
    column = pltpu.VMEM((CX, 128), F32)
    return pl.pallas_call(
        edge_kernel,
        in_specs=[LOCAL, LOCAL, FAR],
        out_specs=[LOCAL] * 4,
        out_shape=[row, row, column, column],
        scratch_shapes=[
            pltpu.VMEM((LZ - HEAD, CX, CY), F32),
            pltpu.SemaphoreType.DMA(((LZ - HEAD) // GROUP,)),
        ],
        name="edges",
        compiler_params=params(8),
        cost_estimate=pl.CostEstimate(flops=4_000_000, bytes_accessed=2_700_000, transcendentals=0),
    )(near(head), near(block), far(theta))


def cut_kernel(
    asked_far, block_ref, one_y_ref, two_y_ref, one_x_ref, two_x_ref,
    out_ref, one_x_out, two_x_out, surface, edges, plan, asked_ref, sem,
):
    places = asked_far[...]
    peers = places.shape[0]
    at = iota(2, (peers, 8, 128))
    tiles_y = CY // TA
    y_own = jnp.bitwise_and(places, tiles_y - 1) * TA
    kind = at % 8 // CAP
    first = lax.shift_right_arithmetic(places, 5) * TA - 1
    first = first + jnp.where(kind == 0, SIDES[0], jnp.where(kind == 1, SIDES[1], SIDES[2])) * CX
    first = jnp.where(places < 0, CX, jnp.clip(first, -RIM, CX)) + RIM
    outside = jnp.where(y_own == 0, 0, jnp.where(y_own == CY - TA, TA + 1, 1000))
    plan[...] = jnp.where(at < 8, first, jnp.where(at < 16, jnp.bitwise_and(1 - y_own, 127), outside))
    copy = pltpu.make_async_copy(plan.at[:, 0:1], asked_ref, sem)
    copy.start()
    one_x_out[...] = one_x_ref[...]
    two_x_out[...] = two_x_ref[...]
    even, _ = place_on("gy")
    south = jnp.where(even, two_y_ref[...], one_y_ref[...])
    north = jnp.where(even, one_y_ref[...], two_y_ref[...])
    wide = iota(1, (CX, 128))
    lane = iota(1)
    blank = jnp.zeros((RIM, 128), F32)
    for c in range(2):
        low = jnp.broadcast_to(south[:, WIND + c : WIND + c + 1], (CX, 128))
        high = jnp.broadcast_to(north[:, WIND + c : WIND + c + 1], (CX, 128))
        surface[c, 0:RIM] = blank
        surface[c, RIM : RIM + CX] = block_ref[c * CX : (c + 1) * CX]
        surface[c, RIM + CX :] = blank
        edges[c, 0:RIM] = blank
        edges[c, RIM : RIM + CX] = jnp.where(wide % 8 == 0, low, high)
        edges[c, RIM + CX :] = blank
    copy.wait()
    for source in range(peers):
        message = jnp.zeros((8, 128), F32)
        for g in range(len(SIDES)):
            for r in range(CAP):
                slot = g * CAP + r
                first = asked_ref[source, 0, slot]
                turn = asked_ref[source, 0, 8 + slot]
                outside = asked_ref[source, 0, 16 + slot]
                begin = slot * 16
                for c in range(2):
                    at = begin + 8 * c
                    part = pltpu.roll(surface[c, pl.ds(first, 8), :], jnp.bitwise_and(turn + at, 127), 1)
                    part = jnp.where(lane == at + outside, edges[c, pl.ds(first, 8), :], part)
                    message = jnp.where(lane // 8 == at // 8, part, message)
        out_ref[source] = message


def cut_patches(asked, block, one_y, two_y, one_x, two_x):
    peers = asked.shape[0]
    row = pltpu.VMEM((LZ, 128), F32)
    rows = CX + 2 * RIM
    return pl.pallas_call(
        cut_kernel,
        in_specs=[LOCAL] * 6,
        out_specs=[LOCAL] * 3,
        out_shape=[pltpu.VMEM((peers, 8, 128), F32), row, row],
        scratch_shapes=[
            pltpu.VMEM((2, rows, 128), F32),
            pltpu.VMEM((2, rows, 128), F32),
            pltpu.VMEM((peers, 8, 128), jnp.int32),
            pltpu.SMEM((peers, 1, 128), jnp.int32),
            pltpu.SemaphoreType.DMA(()),
        ],
        name="cut_patches",
        compiler_params=params(4),
    )(*(near(a) for a in (asked, block, one_y, two_y, one_x, two_x)))


def advect_kernel(
    theta_ref, u_ref, v_ref, west_ref, east_ref, one_y_ref, two_y_ref,
    out_ref, theta, wind_u, wind_v, sems,
):
    def copies(g):
        part = pl.ds(g * GROUP, GROUP)
        pairs = ((theta_ref, theta), (u_ref, wind_u), (v_ref, wind_v))
        return [
            pltpu.make_async_copy(source.at[part], target.at[part], sems.at[c, g])
            for c, (source, target) in enumerate(pairs)
        ]

    for g in range(GROUPS):
        for copy in copies(g):
            copy.start()
    even, _ = place_on("gy")
    south = jnp.where(even, two_y_ref[...], one_y_ref[...])
    north = jnp.where(even, one_y_ref[...], two_y_ref[...])
    lane = iota(1, (CX, 128))
    row = iota(0, (CX, 128))

    def one(g, carry):
        south_all, north_all = carry
        for copy in copies(g):
            copy.wait()
        def begin(k):
            t = theta[g * GROUP + k]
            rolled = [pltpu.roll(t, 1, 1), pltpu.roll(t, CY - 1, 1)]
            rims = [pltpu.roll(south_all, (128 - k) % 128, 1), pltpu.roll(north_all, 126 - k, 1)]
            return t, rolled, rims

        def end(k, begun):
            z = g * GROUP + k
            t, rolled, rims = begun
            u = wind_u[z]
            v = wind_v[z]
            west = jnp.where(row == 0, west_ref[pl.ds(z, 1)], pltpu.roll(t, 1, 0))
            east = jnp.where(row == CX - 1, east_ref[pl.ds(z, 1)], pltpu.roll(t, CX - 1, 0))
            south = jnp.where(lane == 0, rims[0], rolled[0])
            north = jnp.where(lane == CY - 1, rims[1], rolled[1])
            change = jnp.abs(u) * (t - jnp.where(u > 0, west, east)) + jnp.abs(v) * (
                t - jnp.where(v > 0, south, north)
            )
            out_ref[z] = t - courant * change

        begun = [begin(k) for k in range(AHEAD)]
        for k in range(GROUP):
            if k + AHEAD < GROUP:
                begun.append(begin(k + AHEAD))
            end(k, begun[k])
        return pltpu.roll(south_all, 128 - GROUP, 1), pltpu.roll(north_all, 128 - GROUP, 1)

    lax.fori_loop(0, GROUPS, one, (south, north))


def advect(theta, wind_u, wind_v, *rims):
    whole = pltpu.VMEM((LZ, CX, CY), F32)
    return pl.pallas_call(
        advect_kernel,
        in_specs=[FAR] * 3 + [LOCAL] * 4,
        out_specs=LOCAL,
        out_shape=whole,
        scratch_shapes=[
            whole,
            whole,
            whole,
            pltpu.SemaphoreType.DMA((3, GROUPS)),
        ],
        name="advect",
        compiler_params=params(12),
        cost_estimate=pl.CostEstimate(flops=14_000_000, bytes_accessed=8_000_000, transcendentals=0),
    )(far(theta), far(wind_u), far(wind_v), *(near(a) for a in rims))


def tile_kernel(after_ref, level_ref, fuel_ref, base_ref, out_ref, level, fuel, base, sems):
    def copies(i):
        some = pl.ds(i * SIDE, SIDE)
        pairs = ((level_ref, level), (fuel_ref, fuel), (base_ref, base))
        return [
            pltpu.make_async_copy(source.at[some], target.at[some], sems.at[c, i])
            for c, (source, target) in enumerate(pairs)
        ]

    for i in range(TPD // SIDE):
        for copy in copies(i):
            copy.start()

    def some(i, carry):
        for copy in copies(i):
            copy.wait()
        for j in range(SIDE):
            t = i * SIDE + j
            cells = [fuel[t, pl.ds(k, 8, stride=ROWS), :] for k in range(ROWS)]
            out_ref[t, 3 * ROWS] = sum(cells[1:], cells[0])
            for k in range(ROWS):
                out_ref[t, ROWS + k] = cells[k]
                out_ref[t, k] = level[t, pl.ds(k, 8, stride=ROWS), :]
                out_ref[t, 2 * ROWS + k] = base[t, pl.ds(k, 8, stride=ROWS), :] * (0.5 * time_step)
        return carry

    lax.fori_loop(0, TPD // SIDE, some, 0)


def prepare_tiles(after, level_set, fuel_load, spread_base):
    tiles = pltpu.VMEM((TPD, S, S), F32)
    return pl.pallas_call(
        tile_kernel,
        in_specs=[ANYWHERE, FAR, FAR, FAR],
        out_specs=LOCAL,
        out_shape=pltpu.VMEM((TPD, 3 * ROWS + 1, 8, 128), F32),
        scratch_shapes=[tiles, tiles, tiles, pltpu.SemaphoreType.DMA((3, TPD // SIDE))],
        name="prepare_tiles",
        compiler_params=params(8),
        cost_estimate=pl.CostEstimate(flops=300_000, bytes_accessed=3_200_000, transcendentals=0),
    )(after, *(far(a) for a in (level_set, fuel_load, spread_base)))


def fire_kernel(
    peers, waits, owner_far, place_far, winds_ref, tile_ref, *rest
):
    (
        level_out, fuel_out, outbox, begins, slopes, heats,
        level_own, fuel_own, owner_ref, place_ref, count, scalar_sems, out_sems,
    ) = rest[waits:]
    lane = iota(1)
    row = iota(0)

    def results(i):
        some = pl.ds(i * SIDE, SIDE)
        pairs = ((level_own, level_out), (fuel_own, fuel_out))
        return [
            pltpu.make_async_copy(source.at[some], target.at[some], out_sems.at[c, i])
            for c, (source, target) in enumerate(pairs)
        ]

    to_scalars((owner_far, place_far), (owner_ref, place_ref), scalar_sems)

    tiles_y = CY // TA
    low_row = (row + 1) // 2
    low_lane = (lane + R // 2) // R
    part_row = jnp.where(row % 2 == 0, 0.5, 0.0) + 0.5 / R
    part_lane = (lane.astype(F32) + 0.5) / R + 0.5 - low_lane.astype(F32)

    ranks = ranks_of(owner_ref, count, peers)
    patches = []
    for t in range(TPD):
        owner = owner_ref[t]
        parts = []
        for g, side in enumerate(SIDES):
            begin = (g * CAP + ranks[t]) * 16
            inside = jnp.logical_and(owner >= side, owner - side < peers)
            part = winds_ref[jnp.clip(owner - side, 0, peers - 1)]
            part = jnp.where(inside, part, 0.0)
            parts.append([pltpu.roll(part, jnp.bitwise_and(-begin - 8 * c, 127), 1) for c in range(2)])
        for c in range(2):
            patches.append(parts[0][c] + parts[1][c] + parts[2][c])
    left = [jnp.take_along_axis(p, low_lane, axis=1) for p in patches]
    right = [jnp.take_along_axis(p, low_lane + 1, axis=1) for p in patches]
    fine = [p + (q - p) * part_lane for p, q in zip(left, right)]
    below = [jnp.take_along_axis(p, low_row, axis=0) for p in fine]
    above = [jnp.take_along_axis(p, low_row + 1, axis=0) for p in fine]
    for i, (p, q) in enumerate(zip(below, above)):
        begins[i] = p + (q - p) * part_row
        slopes[i] = (q - p) * (1.0 / R)

    def burn(t):
        begin = [begins[2 * t + c] for c in range(2)]
        slope = [slopes[2 * t + c] for c in range(2)]
        level = [tile_ref[t, k] for k in range(ROWS)]
        fuel = [tile_ref[t, ROWS + k] for k in range(ROWS)]
        rate = [tile_ref[t, 2 * ROWS + k] for k in range(ROWS)]
        wind = [[begin[c] + slope[c] * float(k) for k in range(ROWS)] for c in range(2)]
        yield
        for _ in range(KSUB):
            before = jnp.where(row == 0, level[0], pltpu.roll(level[-1], 1, 0))
            after = jnp.where(row == 7, level[-1], pltpu.roll(level[0], 7, 0))
            rimmed = [before, *level, after]
            south = [jnp.where(lane == 0, cell, pltpu.roll(cell, 1, 1)) for cell in level]
            north = [jnp.where(lane == S - 1, cell, pltpu.roll(cell, S - 1, 1)) for cell in level]
            yield
            new = []
            for k in range(ROWS):
                cell = rimmed[k + 1]
                west, east = rimmed[k], rimmed[k + 2]
                dx = east - west
                dy = north[k] - south[k]
                square = dx * dx + dy * dy + 4.0 * regular
                length = square * lax.rsqrt(square)
                move = jnp.maximum(length + (wind[0][k] * dx + wind[1][k] * dy), 0.0)
                around = (east + west) + (north[k] + south[k])
                cell = cell * (1.0 - 4.0 * diffusion) + around * diffusion - rate[k] * move
                fuel[k] = fuel[k] * (jnp.tanh(cell) + (2.0 / burn_rate - 1.0))
                new.append(cell)
            level = new
        fuel = [cell * (0.5 * burn_rate) ** KSUB for cell in fuel]
        yield
        for k in range(ROWS):
            level_own[t, pl.ds(k, 8, stride=ROWS), :] = level[k]
            fuel_own[t, pl.ds(k, 8, stride=ROWS), :] = fuel[k]
        heats[t] = (tile_ref[t, 3 * ROWS] - sum(fuel[1:], fuel[0])) * (1.0 / (R * R))

    def some(i, carry):
        tiles = [i * SIDE + j for j in range(SIDE)]
        works = [burn(t) for t in tiles]
        while works:
            works = [w for w in works if next(w, works) is None]
        for copy in results(i):
            copy.start()
        return carry

    lax.fori_loop(0, TPD // SIDE, some, 0)

    for d in range(peers):
        outbox[d] = jnp.where(lane < TA, 0.0, -1.0)
    pairs = [heats[t] for t in range(TPD)]
    pairs = [h + pltpu.roll(h, 7, 0) for h in pairs]
    pairs = [jnp.take_along_axis(h, jnp.minimum(2 * row, 7), axis=0) for h in pairs]
    sums = [
        [jnp.sum(jnp.where(lane // R == b, h, 0.0), axis=1, keepdims=True) for b in range(TA)] for h in pairs
    ]
    for t in range(TPD):
        place = place_ref[t]
        x_own = place // tiles_y * TA
        y_own = lax.rem(place, tiles_y) * TA
        message = jnp.where(lane == TA, (x_own + row).astype(F32), y_own.astype(F32))
        for b in range(TA):
            message = jnp.where(lane == b, sums[t][b], message)
        outbox[owner_ref[t], pl.ds(ranks[t] * TA, TA), :] = message[0:TA]
    for i in range(TPD // SIDE):
        for copy in results(i):
            copy.wait()


def fire(owners, places, winds, tiles_near, peers, waits):
    tiles = (TPD, S, S)
    return pl.pallas_call(
        functools.partial(fire_kernel, peers, len(waits)),
        in_specs=[FAR, FAR, LOCAL, LOCAL] + [ANYWHERE] * len(waits),
        out_specs=[ANYWHERE, ANYWHERE, LOCAL],
        out_shape=[
            jax.ShapeDtypeStruct(tiles, F32),
            jax.ShapeDtypeStruct(tiles, F32),
            pltpu.VMEM((peers, 8, 128), F32),
        ],
        scratch_shapes=[
            pltpu.VMEM((2 * TPD, 8, 128), F32),
            pltpu.VMEM((2 * TPD, 8, 128), F32),
            pltpu.VMEM((TPD, 8, 128), F32),
            pltpu.VMEM(tiles, F32),
            pltpu.VMEM(tiles, F32),
            pltpu.SMEM((TPD,), jnp.int32),
            pltpu.SMEM((TPD,), jnp.int32),
            pltpu.SMEM((peers,), jnp.int32),
            pltpu.SemaphoreType.DMA((2,)),
            pltpu.SemaphoreType.DMA((2, TPD // SIDE)),
        ],
        name="fire",
        compiler_params=params(12),
        cost_estimate=pl.CostEstimate(
            flops=50_000_000, bytes_accessed=6_500_000, transcendentals=3_200_000
        ),
    )(far(owners), far(places), near(winds), near(tiles_near), *waits)


def row_kernel(outbox_ref, one_x_ref, two_x_ref, outbox_out, west_ref, east_ref):
    outbox_out[...] = outbox_ref[...]
    even, _ = place_on("gx")
    west_ref[...] = jnp.where(even, two_x_ref[...], one_x_ref[...])
    east_ref[...] = jnp.where(even, one_x_ref[...], two_x_ref[...])


def sort_rows(outbox, one_x, two_x):
    row = pltpu.VMEM((LZ, 128), F32)
    return pl.pallas_call(
        row_kernel,
        in_specs=[LOCAL] * 3,
        out_specs=[LOCAL] * 3,
        out_shape=[pltpu.VMEM(outbox.shape, F32), row, row],
        name="sort_rows",
        compiler_params=params(4),
    )(near(outbox), near(one_x), near(two_x))


def final_kernel(inbox_ref, part_ref, out_ref, field, result, sems):
    inbox = inbox_ref[...]
    rows = inbox.shape[0] * 8
    values = inbox.reshape(rows, 128)
    lane = iota(1, (rows, 128)).astype(F32)
    hot = jnp.where(lane == values[:, TA : TA + 1], 1.0, 0.0)
    y_own = values[:, TA + 1 : TA + 2]
    spread = jnp.zeros((rows, 128), F32)
    for b in range(TA):
        spread = jnp.where(lane == y_own + float(b), values[:, b : b + 1], spread)
    total = lax.dot_general(
        hot, spread, (((0,), (0,)), ((), ())),
        precision=lax.Precision.HIGHEST, preferred_element_type=F32,
    )
    field[...] = total[:CX]

    def copy(g):
        part = pl.ds(g * GROUP, GROUP)
        return pltpu.make_async_copy(result.at[part], out_ref.at[part], sems.at[g])

    def one(g, carry):
        for k in range(GROUP):
            z = g * GROUP + k
            height = jnp.full((8, 128), z, jnp.int32).astype(F32)
            gain = heat_gain * jnp.exp((height + 0.5) * (-4.0 / LZ))
            result[z] = part_ref[z] + field[...] * jnp.concatenate([gain] * (CX // 8), axis=0)
        copy(g).start()
        return carry

    lax.fori_loop(0, GROUPS, one, 0)
    for g in range(GROUPS):
        copy(g).wait()


def finish(inbox, part):
    return pl.pallas_call(
        final_kernel,
        in_specs=[LOCAL, LOCAL],
        out_specs=ANYWHERE,
        out_shape=jax.ShapeDtypeStruct((LZ, CX, CY), F32),
        scratch_shapes=[
            pltpu.VMEM((CX, CY), F32),
            pltpu.VMEM((LZ, CX, CY), F32),
            pltpu.SemaphoreType.DMA((GROUPS,)),
        ],
        name="finish",
        compiler_params=params(8),
        cost_estimate=pl.CostEstimate(flops=3_000_000, bytes_accessed=2_700_000, transcendentals=0),
    )(near(inbox), near(part))


def swapped_y(one, two):
    count = lax.axis_size("gy")
    pairs = [(i, i ^ 1) for i in range(count)]
    others = [((i + 1) % count, ((i ^ 1) + 1) % count) for i in range(count)]
    return lax.ppermute(one, "gy", pairs), lax.ppermute(two, "gy", others)


def swapped_x(one, two):
    count, rows = lax.axis_size("gx"), lax.axis_size("gy")
    pairs = [(i, i ^ 1) for i in range(count)]
    others = []
    for i in range(count):
        for j in range(rows):
            to = (i, j ^ 1) if i in (0, count - 1) else (((i - 1) ^ 1) + 1, j)
            others.append((i * rows + j, to[0] * rows + to[1]))
    return lax.ppermute(one, "gx", pairs), lax.ppermute(two, ("gx", "gy"), others)


def exchange(cells):
    return lax.all_to_all(cells, "gx", split_axis=0, concat_axis=0, tiled=True)


def body(theta, wind_u, wind_v, level_set, fuel_load, spread_base, tile_owner, tile_place):
    peers = lax.axis_size("gx")
    owners, places = tile_owner[0, 0], tile_place[0, 0]
    requests, head, block = make_requests(owners, places, theta, wind_u, wind_v, peers)
    asked = exchange(requests)

    one_x, two_x, one_y, two_y = make_edges(head, block, theta)
    rims_y = swapped_y(one_y, two_y)

    patches, one_x, two_x = cut_patches(asked, block, *rims_y, one_x, two_x)
    winds = exchange(patches)
    rims_x = swapped_x(one_x, two_x)

    tiles_near = prepare_tiles(patches, level_set[0, 0], fuel_load[0, 0], spread_base[0, 0])
    level_out, fuel_out, outbox = fire(owners, places, winds, tiles_near, peers, ())
    outbox, west, east = sort_rows(outbox, *rims_x)
    part = advect(theta, wind_u, wind_v, west, east, *rims_y)
    inbox = exchange(outbox)
    theta_next = finish(inbox, part)
    return (theta_next, level_out[None, None], fuel_out[None, None])


def solution(mesh):
    in_specs = (
        P(None, "gx", "gy"),
        P(None, "gx", "gy"),
        P(None, "gx", "gy"),
        P("gx", "gy", None, None, None),
        P("gx", "gy", None, None, None),
        P("gx", "gy", None, None, None),
        P("gx", "gy", None),
        P("gx", "gy", None),
    )
    out_specs = (
        P(None, "gx", "gy"),
        P("gx", "gy", None, None, None),
        P("gx", "gy", None, None, None),
    )
    return jax.shard_map(body, mesh=mesh, in_specs=in_specs, out_specs=out_specs, check_vma=False)
```

```python
import functools

import jax
import jax.numpy as jnp
from jax import lax
from jax.experimental import pallas as pl
from jax.experimental.pallas import tpu as pltpu
from jax.sharding import PartitionSpec as P

LZ = 80
TA = 4
R = 32
KSUB = 6
CAP = 2
TPD = 16
S = 128
CX = 64
CY = 128
ROWS = S // 8
RIM = 8
SIDES = (0, 1, -1)
WIND = 100
GROUP = 8
GROUPS = LZ // GROUP
HEAD = 24
SIDE = 4
AHEAD = 2

time_step = 0.03
diffusion = 0.15
burn_rate = 0.15
regular = 0.01
courant = 0.4
heat_gain = 2.0

F32 = jnp.float32
LOCAL = pl.BlockSpec(memory_space=pltpu.VMEM)
FAR = pl.BlockSpec(memory_space=pltpu.HBM)
ANYWHERE = pl.BlockSpec(memory_space=pl.ANY)
SCALARS = pl.BlockSpec(memory_space=pltpu.SMEM)


def iota(dim, shape=(8, 128)):
    return lax.broadcasted_iota(jnp.int32, shape, dim)


def near(cells):
    return pltpu.with_memory_space_constraint(cells, pltpu.VMEM)


def far(cells):
    return pltpu.with_memory_space_constraint(cells, pltpu.HBM)


def params(mib):
    return pltpu.CompilerParams(vmem_limit_bytes=mib * 1024 * 1024)


def to_scalars(refs, scalars, sems, others=()):
    copies = [pltpu.make_async_copy(ref, own, sems.at[c]) for c, (ref, own) in enumerate(zip(refs, scalars))]
    for copy in [*copies, *others]:
        copy.start()
    for copy in copies:
        copy.wait()


def ranks_of(owners):
    return [sum((jnp.where(owners[s] == owners[t], 1, 0) for s in range(t)), jnp.int32(0)) for t in range(TPD)]


def request_kernel(
    owner_far, place_far, theta_ref, u_ref, v_ref, out_ref, head_ref, block_ref,
    owner_ref, place_ref, table, sems, far_sems,
):
    pairs = [(ref.at[0], block_ref.at[c * CX : (c + 1) * CX]) for c, ref in enumerate((u_ref, v_ref))]
    pairs.append((theta_ref.at[0:HEAD], head_ref))
    others = [pltpu.make_async_copy(source, target, far_sems.at[i]) for i, (source, target) in enumerate(pairs)]
    to_scalars((owner_far, place_far), (owner_ref, place_ref), sems, others)
    peers = out_ref.shape[0]
    for i in range((peers + 2) * CAP):
        table[i] = -1
    ranks = ranks_of([owner_ref[t] for t in range(TPD)])
    for t in range(TPD):
        table[(owner_ref[t] + 1) * CAP + ranks[t]] = place_ref[t]
    lane = iota(1, (1, 128))
    for peer in range(peers):
        line = jnp.full((1, 128), -1, jnp.int32)
        for g, side in enumerate(SIDES):
            for r in range(CAP):
                line = jnp.where(lane % 8 == g * CAP + r, table[(peer + 1 + side) * CAP + r], line)
        out_ref[peer] = jnp.broadcast_to(line, (8, 128))
    for copy in others:
        copy.wait()


def make_requests(owners, places, theta, wind_u, wind_v, peers):
    return pl.pallas_call(
        request_kernel,
        in_specs=[FAR] * 5,
        out_specs=[LOCAL] * 3,
        out_shape=[
            pltpu.VMEM((peers, 8, 128), jnp.int32),
            pltpu.VMEM((HEAD, CX, CY), F32),
            pltpu.VMEM((2 * CX, 128), F32),
        ],
        scratch_shapes=[
            pltpu.SMEM((TPD,), jnp.int32),
            pltpu.SMEM((TPD,), jnp.int32),
            pltpu.SMEM(((peers + 2) * CAP,), jnp.int32),
            pltpu.SemaphoreType.DMA((2,)),
            pltpu.SemaphoreType.DMA((3,)),
        ],
        name="make_requests",
        compiler_params=params(4),
    )(*(far(a) for a in (owners, places, theta, wind_u, wind_v)))


def place_on(axis):
    index = lax.axis_index(axis)
    even = lax.rem(index, 2) == 0
    return even, jnp.logical_or(index == 0, index == lax.axis_size(axis) - 1)


def edge_kernel(head_ref, block_ref, theta_ref, one_x_ref, two_x_ref, one_y_ref, two_y_ref, theta, sems):
    even_x, wraps_x = place_on("gx")
    even_y, wraps_y = place_on("gy")

    def copy(z):
        return pltpu.make_async_copy(
            theta_ref.at[z : z + GROUP], theta.at[z - HEAD : z - HEAD + GROUP], sems.at[(z - HEAD) // GROUP]
        )

    for z in range(HEAD, LZ, GROUP):
        copy(z).start()
    lane = iota(1, (CX, 128))

    first = last = jnp.zeros((CX, 128), F32)
    for z in range(LZ):
        if z >= HEAD and z % GROUP == 0:
            copy(z).wait()
        cells = head_ref[z] if z < HEAD else theta[z - HEAD]
        low, high = cells[0:1], cells[CX - 1 : CX]
        one_x_ref[z : z + 1] = jnp.where(even_x, high, low)
        two_x_ref[z : z + 1] = jnp.where(wraps_x, 0.0, jnp.where(even_x, low, high))
        turned = pltpu.roll(cells, z + 1, 1)
        first = jnp.where(lane == z + 1, turned, first)
        last = jnp.where(lane == z, turned, last)
    for c in range(2):
        cells = block_ref[c * CX : (c + 1) * CX]
        first = jnp.where(lane == WIND + c, pltpu.roll(cells, WIND + c, 1), first)
        last = jnp.where(lane == WIND + c, pltpu.roll(cells, WIND + c + 1, 1), last)
    one_y_ref[...] = jnp.where(even_y, last, first)
    two_y_ref[...] = jnp.where(wraps_y, 0.0, jnp.where(even_y, first, last))


def make_edges(head, block, theta):
    row = pltpu.VMEM((LZ, 128), F32)
    column = pltpu.VMEM((CX, 128), F32)
    return pl.pallas_call(
        edge_kernel,
        in_specs=[LOCAL, LOCAL, FAR],
        out_specs=[LOCAL] * 4,
        out_shape=[row, row, column, column],
        scratch_shapes=[
            pltpu.VMEM((LZ - HEAD, CX, CY), F32),
            pltpu.SemaphoreType.DMA(((LZ - HEAD) // GROUP,)),
        ],
        name="edges",
        compiler_params=params(8),
        cost_estimate=pl.CostEstimate(flops=4_000_000, bytes_accessed=2_700_000, transcendentals=0),
    )(near(head), near(block), far(theta))


def cut_kernel(
    asked_far, block_ref, one_y_ref, two_y_ref, one_x_ref, two_x_ref,
    out_ref, one_x_out, two_x_out, surface, edges, plan, asked_ref, sem,
):
    places = asked_far[...]
    peers = places.shape[0]
    at = iota(2, (peers, 8, 128))
    tiles_y = CY // TA
    y_own = jnp.bitwise_and(places, tiles_y - 1) * TA
    kind = at % 8 // CAP
    first = lax.shift_right_arithmetic(places, 5) * TA - 1
    first = first + jnp.where(kind == 0, SIDES[0], jnp.where(kind == 1, SIDES[1], SIDES[2])) * CX
    first = jnp.where(places < 0, CX, jnp.clip(first, -RIM, CX)) + RIM
    outside = jnp.where(y_own == 0, 0, jnp.where(y_own == CY - TA, TA + 1, 1000))
    plan[...] = jnp.where(at < 8, first, jnp.where(at < 16, jnp.bitwise_and(1 - y_own, 127), outside))
    copy = pltpu.make_async_copy(plan.at[:, 0:1], asked_ref, sem)
    copy.start()
    one_x_out[...] = one_x_ref[...]
    two_x_out[...] = two_x_ref[...]
    even, _ = place_on("gy")
    south = jnp.where(even, two_y_ref[...], one_y_ref[...])
    north = jnp.where(even, one_y_ref[...], two_y_ref[...])
    wide = iota(1, (CX, 128))
    lane = iota(1)
    blank = jnp.zeros((RIM, 128), F32)
    for c in range(2):
        low = jnp.broadcast_to(south[:, WIND + c : WIND + c + 1], (CX, 128))
        high = jnp.broadcast_to(north[:, WIND + c : WIND + c + 1], (CX, 128))
        surface[c, 0:RIM] = blank
        surface[c, RIM : RIM + CX] = block_ref[c * CX : (c + 1) * CX]
        surface[c, RIM + CX :] = blank
        edges[c, 0:RIM] = blank
        edges[c, RIM : RIM + CX] = jnp.where(wide % 8 == 0, low, high)
        edges[c, RIM + CX :] = blank
    copy.wait()
    for source in range(peers):
        message = jnp.zeros((8, 128), F32)
        for g in range(len(SIDES)):
            for r in range(CAP):
                slot = g * CAP + r
                first = asked_ref[source, 0, slot]
                turn = asked_ref[source, 0, 8 + slot]
                outside = asked_ref[source, 0, 16 + slot]
                begin = slot * 16
                for c in range(2):
                    at = begin + 8 * c
                    part = pltpu.roll(surface[c, pl.ds(first, 8), :], jnp.bitwise_and(turn + at, 127), 1)
                    part = jnp.where(lane == at + outside, edges[c, pl.ds(first, 8), :], part)
                    message = jnp.where(lane // 8 == at // 8, part, message)
        out_ref[source] = message


def cut_patches(asked, block, one_y, two_y, one_x, two_x):
    peers = asked.shape[0]
    row = pltpu.VMEM((LZ, 128), F32)
    rows = CX + 2 * RIM
    return pl.pallas_call(
        cut_kernel,
        in_specs=[LOCAL] * 6,
        out_specs=[LOCAL] * 3,
        out_shape=[pltpu.VMEM((peers, 8, 128), F32), row, row],
        scratch_shapes=[
            pltpu.VMEM((2, rows, 128), F32),
            pltpu.VMEM((2, rows, 128), F32),
            pltpu.VMEM((peers, 8, 128), jnp.int32),
            pltpu.SMEM((peers, 1, 128), jnp.int32),
            pltpu.SemaphoreType.DMA(()),
        ],
        name="cut_patches",
        compiler_params=params(4),
    )(*(near(a) for a in (asked, block, one_y, two_y, one_x, two_x)))


def advect_kernel(
    theta_ref, u_ref, v_ref, west_ref, east_ref, one_y_ref, two_y_ref,
    out_ref, theta, wind_u, wind_v, sems,
):
    def copies(g):
        part = pl.ds(g * GROUP, GROUP)
        pairs = ((theta_ref, theta), (u_ref, wind_u), (v_ref, wind_v))
        return [
            pltpu.make_async_copy(source.at[part], target.at[part], sems.at[c, g])
            for c, (source, target) in enumerate(pairs)
        ]

    for g in range(GROUPS):
        for copy in copies(g):
            copy.start()
    even, _ = place_on("gy")
    south = jnp.where(even, two_y_ref[...], one_y_ref[...])
    north = jnp.where(even, one_y_ref[...], two_y_ref[...])
    lane = iota(1, (CX, 128))
    row = iota(0, (CX, 128))

    def one(g, carry):
        south_all, north_all = carry
        for copy in copies(g):
            copy.wait()
        def begin(k):
            t = theta[g * GROUP + k]
            rolled = [pltpu.roll(t, 1, 1), pltpu.roll(t, CY - 1, 1)]
            rims = [pltpu.roll(south_all, (128 - k) % 128, 1), pltpu.roll(north_all, 126 - k, 1)]
            return t, rolled, rims

        def end(k, begun):
            z = g * GROUP + k
            t, rolled, rims = begun
            u = wind_u[z]
            v = wind_v[z]
            west = jnp.where(row == 0, west_ref[pl.ds(z, 1)], pltpu.roll(t, 1, 0))
            east = jnp.where(row == CX - 1, east_ref[pl.ds(z, 1)], pltpu.roll(t, CX - 1, 0))
            south = jnp.where(lane == 0, rims[0], rolled[0])
            north = jnp.where(lane == CY - 1, rims[1], rolled[1])
            change = jnp.abs(u) * (t - jnp.where(u > 0, west, east)) + jnp.abs(v) * (
                t - jnp.where(v > 0, south, north)
            )
            out_ref[z] = t - courant * change

        begun = [begin(k) for k in range(AHEAD)]
        for k in range(GROUP):
            if k + AHEAD < GROUP:
                begun.append(begin(k + AHEAD))
            end(k, begun[k])
        return pltpu.roll(south_all, 128 - GROUP, 1), pltpu.roll(north_all, 128 - GROUP, 1)

    lax.fori_loop(0, GROUPS, one, (south, north))


def advect(theta, wind_u, wind_v, *rims):
    whole = pltpu.VMEM((LZ, CX, CY), F32)
    return pl.pallas_call(
        advect_kernel,
        in_specs=[FAR] * 3 + [LOCAL] * 4,
        out_specs=LOCAL,
        out_shape=whole,
        scratch_shapes=[
            whole,
            whole,
            whole,
            pltpu.SemaphoreType.DMA((3, GROUPS)),
        ],
        name="advect",
        compiler_params=params(12),
        cost_estimate=pl.CostEstimate(flops=14_000_000, bytes_accessed=8_000_000, transcendentals=0),
    )(far(theta), far(wind_u), far(wind_v), *(near(a) for a in rims))


def tile_kernel(after_ref, level_ref, fuel_ref, base_ref, out_ref, level, fuel, base, sems):
    def copies(i):
        some = pl.ds(i * SIDE, SIDE)
        pairs = ((level_ref, level), (fuel_ref, fuel), (base_ref, base))
        return [
            pltpu.make_async_copy(source.at[some], target.at[some], sems.at[c, i])
            for c, (source, target) in enumerate(pairs)
        ]

    for i in range(TPD // SIDE):
        for copy in copies(i):
            copy.start()

    def some(i, carry):
        for copy in copies(i):
            copy.wait()
        for j in range(SIDE):
            t = i * SIDE + j
            cells = [fuel[t, pl.ds(k, 8, stride=ROWS), :] for k in range(ROWS)]
            out_ref[t, 3 * ROWS] = sum(cells[1:], cells[0])
            for k in range(ROWS):
                out_ref[t, ROWS + k] = cells[k]
                out_ref[t, k] = level[t, pl.ds(k, 8, stride=ROWS), :]
                out_ref[t, 2 * ROWS + k] = base[t, pl.ds(k, 8, stride=ROWS), :] * (0.5 * time_step)
        return carry

    lax.fori_loop(0, TPD // SIDE, some, 0)


def prepare_tiles(after, level_set, fuel_load, spread_base):
    tiles = pltpu.VMEM((TPD, S, S), F32)
    return pl.pallas_call(
        tile_kernel,
        in_specs=[ANYWHERE, FAR, FAR, FAR],
        out_specs=LOCAL,
        out_shape=pltpu.VMEM((TPD, 3 * ROWS + 1, 8, 128), F32),
        scratch_shapes=[tiles, tiles, tiles, pltpu.SemaphoreType.DMA((3, TPD // SIDE))],
        name="prepare_tiles",
        compiler_params=params(8),
        cost_estimate=pl.CostEstimate(flops=300_000, bytes_accessed=3_200_000, transcendentals=0),
    )(after, *(far(a) for a in (level_set, fuel_load, spread_base)))


def fire_kernel(
    peers, waits, owner_vec, place_vec, winds_ref, tile_ref, *rest
):
    (
        level_out, fuel_out, outbox, begins, slopes, heats,
        level_own, fuel_own, out_sems,
    ) = rest[waits:]
    lane = iota(1)
    row = iota(0)

    def results(i):
        some = pl.ds(i * SIDE, SIDE)
        pairs = ((level_own, level_out), (fuel_own, fuel_out))
        return [
            pltpu.make_async_copy(source.at[some], target.at[some], out_sems.at[c, i])
            for c, (source, target) in enumerate(pairs)
        ]

    owner_all, place_all = owner_vec[...], place_vec[...]
    owners = [owner_all[t] for t in range(TPD)]
    places = [place_all[t] for t in range(TPD)]

    tiles_y = CY // TA
    low_row = (row + 1) // 2
    low_lane = (lane + R // 2) // R
    part_row = jnp.where(row % 2 == 0, 0.5, 0.0) + 0.5 / R
    part_lane = (lane.astype(F32) + 0.5) / R + 0.5 - low_lane.astype(F32)

    ranks = ranks_of(owners)
    patches = []
    for t in range(TPD):
        owner = owners[t]
        parts = []
        for g, side in enumerate(SIDES):
            begin = (g * CAP + ranks[t]) * 16
            inside = jnp.logical_and(owner >= side, owner - side < peers)
            part = winds_ref[jnp.clip(owner - side, 0, peers - 1)]
            part = jnp.where(inside, part, 0.0)
            parts.append([pltpu.roll(part, jnp.bitwise_and(-begin - 8 * c, 127), 1) for c in range(2)])
        for c in range(2):
            patches.append(parts[0][c] + parts[1][c] + parts[2][c])
    left = [jnp.take_along_axis(p, low_lane, axis=1) for p in patches]
    right = [jnp.take_along_axis(p, low_lane + 1, axis=1) for p in patches]
    fine = [p + (q - p) * part_lane for p, q in zip(left, right)]
    below = [jnp.take_along_axis(p, low_row, axis=0) for p in fine]
    above = [jnp.take_along_axis(p, low_row + 1, axis=0) for p in fine]
    for i, (p, q) in enumerate(zip(below, above)):
        begins[i] = p + (q - p) * part_row
        slopes[i] = (q - p) * (1.0 / R)

    def burn(t):
        begin = [begins[2 * t + c] for c in range(2)]
        slope = [slopes[2 * t + c] for c in range(2)]
        level = [tile_ref[t, k] for k in range(ROWS)]
        fuel = [tile_ref[t, ROWS + k] for k in range(ROWS)]
        rate = [tile_ref[t, 2 * ROWS + k] for k in range(ROWS)]
        wind = [[begin[c] + slope[c] * float(k) for k in range(ROWS)] for c in range(2)]
        yield
        for _ in range(KSUB):
            before = jnp.where(row == 0, level[0], pltpu.roll(level[-1], 1, 0))
            after = jnp.where(row == 7, level[-1], pltpu.roll(level[0], 7, 0))
            rimmed = [before, *level, after]
            south = [jnp.where(lane == 0, cell, pltpu.roll(cell, 1, 1)) for cell in level]
            north = [jnp.where(lane == S - 1, cell, pltpu.roll(cell, S - 1, 1)) for cell in level]
            yield
            new = []
            for k in range(ROWS):
                cell = rimmed[k + 1]
                west, east = rimmed[k], rimmed[k + 2]
                dx = east - west
                dy = north[k] - south[k]
                square = dx * dx + dy * dy + 4.0 * regular
                length = square * lax.rsqrt(square)
                move = jnp.maximum(length + (wind[0][k] * dx + wind[1][k] * dy), 0.0)
                around = (east + west) + (north[k] + south[k])
                cell = cell * (1.0 - 4.0 * diffusion) + around * diffusion - rate[k] * move
                fuel[k] = fuel[k] * (jnp.tanh(cell) + (2.0 / burn_rate - 1.0))
                new.append(cell)
            level = new
        fuel = [cell * (0.5 * burn_rate) ** KSUB for cell in fuel]
        yield
        for k in range(ROWS):
            level_own[t, pl.ds(k, 8, stride=ROWS), :] = level[k]
            fuel_own[t, pl.ds(k, 8, stride=ROWS), :] = fuel[k]
        heats[t] = (tile_ref[t, 3 * ROWS] - sum(fuel[1:], fuel[0])) * (1.0 / (R * R))

    def some(i, carry):
        tiles = [i * SIDE + j for j in range(SIDE)]
        works = [burn(t) for t in tiles]
        while works:
            works = [w for w in works if next(w, works) is None]
        for copy in results(i):
            copy.start()
        return carry

    lax.fori_loop(0, TPD // SIDE, some, 0)

    for d in range(peers):
        outbox[d] = jnp.where(lane < TA, 0.0, -1.0)
    pairs = [heats[t] for t in range(TPD)]
    pairs = [h + pltpu.roll(h, 7, 0) for h in pairs]
    pairs = [jnp.take_along_axis(h, jnp.minimum(2 * row, 7), axis=0) for h in pairs]
    sums = [
        [jnp.sum(jnp.where(lane // R == b, h, 0.0), axis=1, keepdims=True) for b in range(TA)] for h in pairs
    ]
    for t in range(TPD):
        place = places[t]
        x_own = place // tiles_y * TA
        y_own = lax.rem(place, tiles_y) * TA
        message = jnp.where(lane == TA, (x_own + row).astype(F32), y_own.astype(F32))
        for b in range(TA):
            message = jnp.where(lane == b, sums[t][b], message)
        outbox[owners[t], pl.ds(ranks[t] * TA, TA), :] = message[0:TA]
    for i in range(TPD // SIDE):
        for copy in results(i):
            copy.wait()


def fire(owners, places, winds, tiles_near, peers, waits):
    tiles = (TPD, S, S)
    return pl.pallas_call(
        functools.partial(fire_kernel, peers, len(waits)),
        in_specs=[LOCAL] * 4 + [ANYWHERE] * len(waits),
        out_specs=[ANYWHERE, ANYWHERE, LOCAL],
        out_shape=[
            jax.ShapeDtypeStruct(tiles, F32),
            jax.ShapeDtypeStruct(tiles, F32),
            pltpu.VMEM((peers, 8, 128), F32),
        ],
        scratch_shapes=[
            pltpu.VMEM((2 * TPD, 8, 128), F32),
            pltpu.VMEM((2 * TPD, 8, 128), F32),
            pltpu.VMEM((TPD, 8, 128), F32),
            pltpu.VMEM(tiles, F32),
            pltpu.VMEM(tiles, F32),
            pltpu.SemaphoreType.DMA((2, TPD // SIDE)),
        ],
        name="fire",
        compiler_params=params(12),
        cost_estimate=pl.CostEstimate(
            flops=50_000_000, bytes_accessed=6_500_000, transcendentals=3_200_000
        ),
    )(*(near(a) for a in (owners, places, winds, tiles_near)), *waits)


def row_kernel(outbox_ref, one_x_ref, two_x_ref, outbox_out, west_ref, east_ref):
    outbox_out[...] = outbox_ref[...]
    even, _ = place_on("gx")
    west_ref[...] = jnp.where(even, two_x_ref[...], one_x_ref[...])
    east_ref[...] = jnp.where(even, one_x_ref[...], two_x_ref[...])


def sort_rows(outbox, one_x, two_x):
    row = pltpu.VMEM((LZ, 128), F32)
    return pl.pallas_call(
        row_kernel,
        in_specs=[LOCAL] * 3,
        out_specs=[LOCAL] * 3,
        out_shape=[pltpu.VMEM(outbox.shape, F32), row, row],
        name="sort_rows",
        compiler_params=params(4),
    )(near(outbox), near(one_x), near(two_x))


def final_kernel(inbox_ref, part_ref, out_ref, field, result, sems):
    inbox = inbox_ref[...]
    rows = inbox.shape[0] * 8
    values = inbox.reshape(rows, 128)
    lane = iota(1, (rows, 128)).astype(F32)
    hot = jnp.where(lane == values[:, TA : TA + 1], 1.0, 0.0)
    y_own = values[:, TA + 1 : TA + 2]
    spread = jnp.zeros((rows, 128), F32)
    for b in range(TA):
        spread = jnp.where(lane == y_own + float(b), values[:, b : b + 1], spread)
    total = lax.dot_general(
        hot, spread, (((0,), (0,)), ((), ())),
        precision=lax.Precision.HIGHEST, preferred_element_type=F32,
    )
    field[...] = total[:CX]

    def copy(g):
        part = pl.ds(g * GROUP, GROUP)
        return pltpu.make_async_copy(result.at[part], out_ref.at[part], sems.at[g])

    def one(g, carry):
        for k in range(GROUP):
            z = g * GROUP + k
            height = jnp.full((8, 128), z, jnp.int32).astype(F32)
            gain = heat_gain * jnp.exp((height + 0.5) * (-4.0 / LZ))
            result[z] = part_ref[z] + field[...] * jnp.concatenate([gain] * (CX // 8), axis=0)
        copy(g).start()
        return carry

    lax.fori_loop(0, GROUPS, one, 0)
    for g in range(GROUPS):
        copy(g).wait()


def finish(inbox, part):
    return pl.pallas_call(
        final_kernel,
        in_specs=[LOCAL, LOCAL],
        out_specs=ANYWHERE,
        out_shape=jax.ShapeDtypeStruct((LZ, CX, CY), F32),
        scratch_shapes=[
            pltpu.VMEM((CX, CY), F32),
            pltpu.VMEM((LZ, CX, CY), F32),
            pltpu.SemaphoreType.DMA((GROUPS,)),
        ],
        name="finish",
        compiler_params=params(8),
        cost_estimate=pl.CostEstimate(flops=3_000_000, bytes_accessed=2_700_000, transcendentals=0),
    )(near(inbox), near(part))


def swapped_y(one, two):
    count = lax.axis_size("gy")
    pairs = [(i, i ^ 1) for i in range(count)]
    others = [((i + 1) % count, ((i ^ 1) + 1) % count) for i in range(count)]
    return lax.ppermute(one, "gy", pairs), lax.ppermute(two, "gy", others)


def swapped_x(one, two):
    count, rows = lax.axis_size("gx"), lax.axis_size("gy")
    pairs = [(i, i ^ 1) for i in range(count)]
    others = []
    for i in range(count):
        for j in range(rows):
            to = (i, j ^ 1) if i in (0, count - 1) else (((i - 1) ^ 1) + 1, j)
            others.append((i * rows + j, to[0] * rows + to[1]))
    return lax.ppermute(one, "gx", pairs), lax.ppermute(two, ("gx", "gy"), others)


def exchange(cells):
    return lax.all_to_all(cells, "gx", split_axis=0, concat_axis=0, tiled=True)


def body(theta, wind_u, wind_v, level_set, fuel_load, spread_base, tile_owner, tile_place):
    peers = lax.axis_size("gx")
    owners, places = tile_owner[0, 0], tile_place[0, 0]
    requests, head, block = make_requests(owners, places, theta, wind_u, wind_v, peers)
    asked = exchange(requests)

    one_x, two_x, one_y, two_y = make_edges(head, block, theta)
    rims_y = swapped_y(one_y, two_y)

    patches, one_x, two_x = cut_patches(asked, block, *rims_y, one_x, two_x)
    winds = exchange(patches)
    rims_x = swapped_x(one_x, two_x)

    tiles_near = prepare_tiles(patches, level_set[0, 0], fuel_load[0, 0], spread_base[0, 0])
    level_out, fuel_out, outbox = fire(owners, places, winds, tiles_near, peers, ())
    outbox, west, east = sort_rows(outbox, *rims_x)
    part = advect(theta, wind_u, wind_v, west, east, *rims_y)
    inbox = exchange(outbox)
    theta_next = finish(inbox, part)
    return (theta_next, level_out[None, None], fuel_out[None, None])


def solution(mesh):
    in_specs = (
        P(None, "gx", "gy"),
        P(None, "gx", "gy"),
        P(None, "gx", "gy"),
        P("gx", "gy", None, None, None),
        P("gx", "gy", None, None, None),
        P("gx", "gy", None, None, None),
        P("gx", "gy", None),
        P("gx", "gy", None),
    )
    out_specs = (
        P(None, "gx", "gy"),
        P("gx", "gy", None, None, None),
        P("gx", "gy", None, None, None),
    )
    return jax.shard_map(body, mesh=mesh, in_specs=in_specs, out_specs=out_specs, check_vma=False)
```

```python
import functools

import jax
import jax.numpy as jnp
from jax import lax
from jax.experimental import pallas as pl
from jax.experimental.pallas import tpu as pltpu
from jax.sharding import PartitionSpec as P

LZ = 80
TA = 4
R = 32
KSUB = 6
CAP = 2
TPD = 16
S = 128
CX = 64
CY = 128
ROWS = S // 8
RIM = 8
SIDES = (0, 1, -1)
WIND = 100
GROUP = 8
GROUPS = LZ // GROUP
HEAD = 24
SIDE = 4
AHEAD = 2

time_step = 0.03
diffusion = 0.15
burn_rate = 0.15
regular = 0.01
courant = 0.4
heat_gain = 2.0

F32 = jnp.float32
LOCAL = pl.BlockSpec(memory_space=pltpu.VMEM)
FAR = pl.BlockSpec(memory_space=pltpu.HBM)
ANYWHERE = pl.BlockSpec(memory_space=pl.ANY)
SCALARS = pl.BlockSpec(memory_space=pltpu.SMEM)


def iota(dim, shape=(8, 128)):
    return lax.broadcasted_iota(jnp.int32, shape, dim)


def near(cells):
    return pltpu.with_memory_space_constraint(cells, pltpu.VMEM)


def far(cells):
    return pltpu.with_memory_space_constraint(cells, pltpu.HBM)


def params(mib):
    return pltpu.CompilerParams(vmem_limit_bytes=mib * 1024 * 1024)


def to_scalars(refs, scalars, sems, others=()):
    copies = [pltpu.make_async_copy(ref, own, sems.at[c]) for c, (ref, own) in enumerate(zip(refs, scalars))]
    for copy in [*copies, *others]:
        copy.start()
    for copy in copies:
        copy.wait()


def ranks_of(owners):
    return [sum((jnp.where(owners[s] == owners[t], 1, 0) for s in range(t)), jnp.int32(0)) for t in range(TPD)]


def request_kernel(
    owner_far, place_far, theta_ref, u_ref, v_ref, out_ref, head_ref, block_ref,
    owner_ref, place_ref, table, sems, far_sems,
):
    pairs = [(ref.at[0], block_ref.at[c * CX : (c + 1) * CX]) for c, ref in enumerate((u_ref, v_ref))]
    pairs.append((theta_ref.at[0:HEAD], head_ref))
    others = [pltpu.make_async_copy(source, target, far_sems.at[i]) for i, (source, target) in enumerate(pairs)]
    to_scalars((owner_far, place_far), (owner_ref, place_ref), sems, others)
    peers = out_ref.shape[0]
    for i in range((peers + 2) * CAP):
        table[i] = -1
    ranks = ranks_of([owner_ref[t] for t in range(TPD)])
    for t in range(TPD):
        table[(owner_ref[t] + 1) * CAP + ranks[t]] = place_ref[t]
    lane = iota(1, (1, 128))
    for peer in range(peers):
        line = jnp.full((1, 128), -1, jnp.int32)
        for g, side in enumerate(SIDES):
            for r in range(CAP):
                line = jnp.where(lane % 8 == g * CAP + r, table[(peer + 1 + side) * CAP + r], line)
        out_ref[peer] = jnp.broadcast_to(line, (8, 128))
    for copy in others:
        copy.wait()


def make_requests(owners, places, theta, wind_u, wind_v, peers):
    return pl.pallas_call(
        request_kernel,
        in_specs=[FAR] * 5,
        out_specs=[LOCAL] * 3,
        out_shape=[
            pltpu.VMEM((peers, 8, 128), jnp.int32),
            pltpu.VMEM((HEAD, CX, CY), F32),
            pltpu.VMEM((2 * CX, 128), F32),
        ],
        scratch_shapes=[
            pltpu.SMEM((TPD,), jnp.int32),
            pltpu.SMEM((TPD,), jnp.int32),
            pltpu.SMEM(((peers + 2) * CAP,), jnp.int32),
            pltpu.SemaphoreType.DMA((2,)),
            pltpu.SemaphoreType.DMA((3,)),
        ],
        name="make_requests",
        compiler_params=params(4),
    )(*(far(a) for a in (owners, places, theta, wind_u, wind_v)))


def place_on(axis):
    index = lax.axis_index(axis)
    even = lax.rem(index, 2) == 0
    return even, jnp.logical_or(index == 0, index == lax.axis_size(axis) - 1)


def edge_kernel(head_ref, block_ref, theta_ref, one_x_ref, two_x_ref, one_y_ref, two_y_ref, theta, sems):
    even_x, wraps_x = place_on("gx")
    even_y, wraps_y = place_on("gy")

    def copy(z):
        return pltpu.make_async_copy(
            theta_ref.at[z : z + GROUP], theta.at[z - HEAD : z - HEAD + GROUP], sems.at[(z - HEAD) // GROUP]
        )

    for z in range(HEAD, LZ, GROUP):
        copy(z).start()
    lane = iota(1, (CX, 128))

    first = last = jnp.zeros((CX, 128), F32)
    for z in range(LZ):
        if z >= HEAD and z % GROUP == 0:
            copy(z).wait()
        cells = head_ref[z] if z < HEAD else theta[z - HEAD]
        low, high = cells[0:1], cells[CX - 1 : CX]
        one_x_ref[z : z + 1] = jnp.where(even_x, high, low)
        two_x_ref[z : z + 1] = jnp.where(wraps_x, 0.0, jnp.where(even_x, low, high))
        turned = pltpu.roll(cells, z + 1, 1)
        first = jnp.where(lane == z + 1, turned, first)
        last = jnp.where(lane == z, turned, last)
    for c in range(2):
        cells = block_ref[c * CX : (c + 1) * CX]
        first = jnp.where(lane == WIND + c, pltpu.roll(cells, WIND + c, 1), first)
        last = jnp.where(lane == WIND + c, pltpu.roll(cells, WIND + c + 1, 1), last)
    one_y_ref[...] = jnp.where(even_y, last, first)
    two_y_ref[...] = jnp.where(wraps_y, 0.0, jnp.where(even_y, first, last))


def make_edges(head, block, theta):
    row = pltpu.VMEM((LZ, 128), F32)
    column = pltpu.VMEM((CX, 128), F32)
    return pl.pallas_call(
        edge_kernel,
        in_specs=[LOCAL, LOCAL, FAR],
        out_specs=[LOCAL] * 4,
        out_shape=[row, row, column, column],
        scratch_shapes=[
            pltpu.VMEM((LZ - HEAD, CX, CY), F32),
            pltpu.SemaphoreType.DMA(((LZ - HEAD) // GROUP,)),
        ],
        name="edges",
        compiler_params=params(8),
        cost_estimate=pl.CostEstimate(flops=4_000_000, bytes_accessed=2_700_000, transcendentals=0),
    )(near(head), near(block), far(theta))


def cut_kernel(
    asked_far, block_ref, one_y_ref, two_y_ref, one_x_ref, two_x_ref,
    out_ref, one_x_out, two_x_out, surface, edges, plan, asked_ref, sem,
):
    places = asked_far[...]
    peers = places.shape[0]
    at = iota(2, (peers, 8, 128))
    tiles_y = CY // TA
    y_own = jnp.bitwise_and(places, tiles_y - 1) * TA
    kind = at % 8 // CAP
    first = lax.shift_right_arithmetic(places, 5) * TA - 1
    first = first + jnp.where(kind == 0, SIDES[0], jnp.where(kind == 1, SIDES[1], SIDES[2])) * CX
    first = jnp.where(places < 0, CX, jnp.clip(first, -RIM, CX)) + RIM
    outside = jnp.where(y_own == 0, 0, jnp.where(y_own == CY - TA, TA + 1, 1000))
    plan[...] = jnp.where(at < 8, first, jnp.where(at < 16, jnp.bitwise_and(1 - y_own, 127), outside))
    copy = pltpu.make_async_copy(plan.at[:, 0:1], asked_ref, sem)
    copy.start()
    one_x_out[...] = one_x_ref[...]
    two_x_out[...] = two_x_ref[...]
    even, _ = place_on("gy")
    south = jnp.where(even, two_y_ref[...], one_y_ref[...])
    north = jnp.where(even, one_y_ref[...], two_y_ref[...])
    wide = iota(1, (CX, 128))
    lane = iota(1)
    blank = jnp.zeros((RIM, 128), F32)
    for c in range(2):
        low = jnp.broadcast_to(south[:, WIND + c : WIND + c + 1], (CX, 128))
        high = jnp.broadcast_to(north[:, WIND + c : WIND + c + 1], (CX, 128))
        surface[c, 0:RIM] = blank
        surface[c, RIM : RIM + CX] = block_ref[c * CX : (c + 1) * CX]
        surface[c, RIM + CX :] = blank
        edges[c, 0:RIM] = blank
        edges[c, RIM : RIM + CX] = jnp.where(wide % 8 == 0, low, high)
        edges[c, RIM + CX :] = blank
    copy.wait()
    for source in range(peers):
        message = jnp.zeros((8, 128), F32)
        for g in range(len(SIDES)):
            for r in range(CAP):
                slot = g * CAP + r
                first = asked_ref[source, 0, slot]
                turn = asked_ref[source, 0, 8 + slot]
                outside = asked_ref[source, 0, 16 + slot]
                begin = slot * 16
                for c in range(2):
                    at = begin + 8 * c
                    part = pltpu.roll(surface[c, pl.ds(first, 8), :], jnp.bitwise_and(turn + at, 127), 1)
                    part = jnp.where(lane == at + outside, edges[c, pl.ds(first, 8), :], part)
                    message = jnp.where(lane // 8 == at // 8, part, message)
        out_ref[source] = message


def cut_patches(asked, block, one_y, two_y, one_x, two_x):
    peers = asked.shape[0]
    row = pltpu.VMEM((LZ, 128), F32)
    rows = CX + 2 * RIM
    return pl.pallas_call(
        cut_kernel,
        in_specs=[LOCAL] * 6,
        out_specs=[LOCAL] * 3,
        out_shape=[pltpu.VMEM((peers, 8, 128), F32), row, row],
        scratch_shapes=[
            pltpu.VMEM((2, rows, 128), F32),
            pltpu.VMEM((2, rows, 128), F32),
            pltpu.VMEM((peers, 8, 128), jnp.int32),
            pltpu.SMEM((peers, 1, 128), jnp.int32),
            pltpu.SemaphoreType.DMA(()),
        ],
        name="cut_patches",
        compiler_params=params(4),
    )(*(near(a) for a in (asked, block, one_y, two_y, one_x, two_x)))


def advect_kernel(
    theta_ref, u_ref, v_ref, one_x_ref, two_x_ref, one_y_ref, two_y_ref,
    out_ref, theta, wind_u, wind_v, west_ref, east_ref, sems,
):
    def copies(g):
        part = pl.ds(g * GROUP, GROUP)
        pairs = ((theta_ref, theta), (u_ref, wind_u), (v_ref, wind_v))
        return [
            pltpu.make_async_copy(source.at[part], target.at[part], sems.at[c, g])
            for c, (source, target) in enumerate(pairs)
        ]

    for g in range(GROUPS):
        for copy in copies(g):
            copy.start()
    even, _ = place_on("gx")
    west_ref[...] = jnp.where(even, two_x_ref[...], one_x_ref[...])
    east_ref[...] = jnp.where(even, one_x_ref[...], two_x_ref[...])
    even, _ = place_on("gy")
    south = jnp.where(even, two_y_ref[...], one_y_ref[...])
    north = jnp.where(even, one_y_ref[...], two_y_ref[...])
    lane = iota(1, (CX, 128))
    row = iota(0, (CX, 128))

    def one(g, carry):
        south_all, north_all = carry
        for copy in copies(g):
            copy.wait()
        def begin(k):
            t = theta[g * GROUP + k]
            rolled = [pltpu.roll(t, 1, 1), pltpu.roll(t, CY - 1, 1)]
            rims = [pltpu.roll(south_all, (128 - k) % 128, 1), pltpu.roll(north_all, 126 - k, 1)]
            return t, rolled, rims

        def end(k, begun):
            z = g * GROUP + k
            t, rolled, rims = begun
            u = wind_u[z]
            v = wind_v[z]
            west = jnp.where(row == 0, west_ref[pl.ds(z, 1)], pltpu.roll(t, 1, 0))
            east = jnp.where(row == CX - 1, east_ref[pl.ds(z, 1)], pltpu.roll(t, CX - 1, 0))
            south = jnp.where(lane == 0, rims[0], rolled[0])
            north = jnp.where(lane == CY - 1, rims[1], rolled[1])
            change = jnp.abs(u) * (t - jnp.where(u > 0, west, east)) + jnp.abs(v) * (
                t - jnp.where(v > 0, south, north)
            )
            out_ref[z] = t - courant * change

        begun = [begin(k) for k in range(AHEAD)]
        for k in range(GROUP):
            if k + AHEAD < GROUP:
                begun.append(begin(k + AHEAD))
            end(k, begun[k])
        return pltpu.roll(south_all, 128 - GROUP, 1), pltpu.roll(north_all, 128 - GROUP, 1)

    lax.fori_loop(0, GROUPS, one, (south, north))


def advect(theta, wind_u, wind_v, *rims):
    whole = pltpu.VMEM((LZ, CX, CY), F32)
    return pl.pallas_call(
        advect_kernel,
        in_specs=[FAR] * 3 + [LOCAL] * 4,
        out_specs=LOCAL,
        out_shape=whole,
        scratch_shapes=[
            whole,
            whole,
            whole,
            pltpu.VMEM((LZ, 128), F32),
            pltpu.VMEM((LZ, 128), F32),
            pltpu.SemaphoreType.DMA((3, GROUPS)),
        ],
        name="advect",
        compiler_params=params(12),
        cost_estimate=pl.CostEstimate(flops=14_000_000, bytes_accessed=8_000_000, transcendentals=0),
    )(far(theta), far(wind_u), far(wind_v), *(near(a) for a in rims))


def tile_kernel(after_ref, level_ref, fuel_ref, base_ref, out_ref, level, fuel, base, sems):
    def copies(i):
        some = pl.ds(i * SIDE, SIDE)
        pairs = ((level_ref, level), (fuel_ref, fuel), (base_ref, base))
        return [
            pltpu.make_async_copy(source.at[some], target.at[some], sems.at[c, i])
            for c, (source, target) in enumerate(pairs)
        ]

    for i in range(TPD // SIDE):
        for copy in copies(i):
            copy.start()

    def some(i, carry):
        for copy in copies(i):
            copy.wait()
        for j in range(SIDE):
            t = i * SIDE + j
            cells = [fuel[t, pl.ds(k, 8, stride=ROWS), :] for k in range(ROWS)]
            out_ref[t, 3 * ROWS] = sum(cells[1:], cells[0])
            for k in range(ROWS):
                out_ref[t, ROWS + k] = cells[k]
                out_ref[t, k] = level[t, pl.ds(k, 8, stride=ROWS), :]
                out_ref[t, 2 * ROWS + k] = base[t, pl.ds(k, 8, stride=ROWS), :] * (0.5 * time_step)
        return carry

    lax.fori_loop(0, TPD // SIDE, some, 0)


def prepare_tiles(after, level_set, fuel_load, spread_base):
    tiles = pltpu.VMEM((TPD, S, S), F32)
    return pl.pallas_call(
        tile_kernel,
        in_specs=[ANYWHERE, FAR, FAR, FAR],
        out_specs=LOCAL,
        out_shape=pltpu.VMEM((TPD, 3 * ROWS + 1, 8, 128), F32),
        scratch_shapes=[tiles, tiles, tiles, pltpu.SemaphoreType.DMA((3, TPD // SIDE))],
        name="prepare_tiles",
        compiler_params=params(8),
        cost_estimate=pl.CostEstimate(flops=300_000, bytes_accessed=3_200_000, transcendentals=0),
    )(after, *(far(a) for a in (level_set, fuel_load, spread_base)))


def fire_kernel(
    peers, waits, owner_vec, place_vec, winds_ref, tile_ref, *rest
):
    (
        level_out, fuel_out, outbox, begins, slopes, heats,
        level_own, fuel_own, out_sems,
    ) = rest[waits:]
    lane = iota(1)
    row = iota(0)

    def results(i):
        some = pl.ds(i * SIDE, SIDE)
        pairs = ((level_own, level_out), (fuel_own, fuel_out))
        return [
            pltpu.make_async_copy(source.at[some], target.at[some], out_sems.at[c, i])
            for c, (source, target) in enumerate(pairs)
        ]

    owner_all, place_all = owner_vec[...], place_vec[...]
    owners = [owner_all[t] for t in range(TPD)]
    places = [place_all[t] for t in range(TPD)]

    tiles_y = CY // TA
    low_row = (row + 1) // 2
    low_lane = (lane + R // 2) // R
    part_row = jnp.where(row % 2 == 0, 0.5, 0.0) + 0.5 / R
    part_lane = (lane.astype(F32) + 0.5) / R + 0.5 - low_lane.astype(F32)

    ranks = ranks_of(owners)
    patches = []
    for t in range(TPD):
        owner = owners[t]
        parts = []
        for g, side in enumerate(SIDES):
            begin = (g * CAP + ranks[t]) * 16
            inside = jnp.logical_and(owner >= side, owner - side < peers)
            part = winds_ref[jnp.clip(owner - side, 0, peers - 1)]
            part = jnp.where(inside, part, 0.0)
            parts.append([pltpu.roll(part, jnp.bitwise_and(-begin - 8 * c, 127), 1) for c in range(2)])
        for c in range(2):
            patches.append(parts[0][c] + parts[1][c] + parts[2][c])
    left = [jnp.take_along_axis(p, low_lane, axis=1) for p in patches]
    right = [jnp.take_along_axis(p, low_lane + 1, axis=1) for p in patches]
    fine = [p + (q - p) * part_lane for p, q in zip(left, right)]
    below = [jnp.take_along_axis(p, low_row, axis=0) for p in fine]
    above = [jnp.take_along_axis(p, low_row + 1, axis=0) for p in fine]
    for i, (p, q) in enumerate(zip(below, above)):
        begins[i] = p + (q - p) * part_row
        slopes[i] = (q - p) * (1.0 / R)

    def burn(t):
        begin = [begins[2 * t + c] for c in range(2)]
        slope = [slopes[2 * t + c] for c in range(2)]
        level = [tile_ref[t, k] for k in range(ROWS)]
        fuel = [tile_ref[t, ROWS + k] for k in range(ROWS)]
        rate = [tile_ref[t, 2 * ROWS + k] for k in range(ROWS)]
        wind = [[begin[c] + slope[c] * float(k) for k in range(ROWS)] for c in range(2)]
        yield
        for _ in range(KSUB):
            before = jnp.where(row == 0, level[0], pltpu.roll(level[-1], 1, 0))
            after = jnp.where(row == 7, level[-1], pltpu.roll(level[0], 7, 0))
            rimmed = [before, *level, after]
            south = [jnp.where(lane == 0, cell, pltpu.roll(cell, 1, 1)) for cell in level]
            north = [jnp.where(lane == S - 1, cell, pltpu.roll(cell, S - 1, 1)) for cell in level]
            yield
            new = []
            for k in range(ROWS):
                cell = rimmed[k + 1]
                west, east = rimmed[k], rimmed[k + 2]
                dx = east - west
                dy = north[k] - south[k]
                square = dx * dx + dy * dy + 4.0 * regular
                length = square * lax.rsqrt(square)
                move = jnp.maximum(length + (wind[0][k] * dx + wind[1][k] * dy), 0.0)
                around = (east + west) + (north[k] + south[k])
                cell = cell * (1.0 - 4.0 * diffusion) + around * diffusion - rate[k] * move
                fuel[k] = fuel[k] * (jnp.tanh(cell) + (2.0 / burn_rate - 1.0))
                new.append(cell)
            level = new
        fuel = [cell * (0.5 * burn_rate) ** KSUB for cell in fuel]
        yield
        for k in range(ROWS):
            level_own[t, pl.ds(k, 8, stride=ROWS), :] = level[k]
            fuel_own[t, pl.ds(k, 8, stride=ROWS), :] = fuel[k]
        heats[t] = (tile_ref[t, 3 * ROWS] - sum(fuel[1:], fuel[0])) * (1.0 / (R * R))

    def some(i, carry):
        tiles = [i * SIDE + j for j in range(SIDE)]
        works = [burn(t) for t in tiles]
        while works:
            works = [w for w in works if next(w, works) is None]
        for copy in results(i):
            copy.start()
        return carry

    lax.fori_loop(0, TPD // SIDE, some, 0)

    for d in range(peers):
        outbox[d] = jnp.where(lane < TA, 0.0, -1.0)
    pairs = [heats[t] for t in range(TPD)]
    pairs = [h + pltpu.roll(h, 7, 0) for h in pairs]
    pairs = [jnp.take_along_axis(h, jnp.minimum(2 * row, 7), axis=0) for h in pairs]
    sums = [
        [jnp.sum(jnp.where(lane // R == b, h, 0.0), axis=1, keepdims=True) for b in range(TA)] for h in pairs
    ]
    for t in range(TPD):
        place = places[t]
        x_own = place // tiles_y * TA
        y_own = lax.rem(place, tiles_y) * TA
        message = jnp.where(lane == TA, (x_own + row).astype(F32), y_own.astype(F32))
        for b in range(TA):
            message = jnp.where(lane == b, sums[t][b], message)
        outbox[owners[t], pl.ds(ranks[t] * TA, TA), :] = message[0:TA]
    for i in range(TPD // SIDE):
        for copy in results(i):
            copy.wait()


def fire(owners, places, winds, tiles_near, peers, waits):
    tiles = (TPD, S, S)
    return pl.pallas_call(
        functools.partial(fire_kernel, peers, len(waits)),
        in_specs=[LOCAL] * 4 + [ANYWHERE] * len(waits),
        out_specs=[ANYWHERE, ANYWHERE, LOCAL],
        out_shape=[
            jax.ShapeDtypeStruct(tiles, F32),
            jax.ShapeDtypeStruct(tiles, F32),
            pltpu.VMEM((peers, 8, 128), F32),
        ],
        scratch_shapes=[
            pltpu.VMEM((2 * TPD, 8, 128), F32),
            pltpu.VMEM((2 * TPD, 8, 128), F32),
            pltpu.VMEM((TPD, 8, 128), F32),
            pltpu.VMEM(tiles, F32),
            pltpu.VMEM(tiles, F32),
            pltpu.SemaphoreType.DMA((2, TPD // SIDE)),
        ],
        name="fire",
        compiler_params=params(12),
        cost_estimate=pl.CostEstimate(
            flops=50_000_000, bytes_accessed=6_500_000, transcendentals=3_200_000
        ),
    )(*(near(a) for a in (owners, places, winds, tiles_near)), *waits)


def pass_kernel(outbox_ref, one_x_ref, two_x_ref, outbox_out):
    outbox_out[...] = outbox_ref[...]


def pass_on(outbox, one_x, two_x):
    return pl.pallas_call(
        pass_kernel,
        in_specs=[LOCAL, ANYWHERE, ANYWHERE],
        out_specs=LOCAL,
        out_shape=pltpu.VMEM(outbox.shape, F32),
        name="pass_on",
        compiler_params=params(4),
    )(near(outbox), one_x, two_x)


def final_kernel(inbox_ref, part_ref, out_ref, field, result, sems):
    inbox = inbox_ref[...]
    rows = inbox.shape[0] * 8
    values = inbox.reshape(rows, 128)
    lane = iota(1, (rows, 128)).astype(F32)
    hot = jnp.where(lane == values[:, TA : TA + 1], 1.0, 0.0)
    y_own = values[:, TA + 1 : TA + 2]
    spread = jnp.zeros((rows, 128), F32)
    for b in range(TA):
        spread = jnp.where(lane == y_own + float(b), values[:, b : b + 1], spread)
    total = lax.dot_general(
        hot, spread, (((0,), (0,)), ((), ())),
        precision=lax.Precision.HIGHEST, preferred_element_type=F32,
    )
    field[...] = total[:CX]

    def copy(g):
        part = pl.ds(g * GROUP, GROUP)
        return pltpu.make_async_copy(result.at[part], out_ref.at[part], sems.at[g])

    for g in range(GROUPS):
        for k in range(GROUP):
            z = g * GROUP + k
            height = jnp.full((8, 128), z, jnp.int32).astype(F32)
            gain = heat_gain * jnp.exp((height + 0.5) * (-4.0 / LZ))
            result[z] = part_ref[z] + field[...] * jnp.concatenate([gain] * (CX // 8), axis=0)
        copy(g).start()
    for g in range(GROUPS):
        copy(g).wait()


def finish(inbox, part):
    return pl.pallas_call(
        final_kernel,
        in_specs=[LOCAL, LOCAL],
        out_specs=ANYWHERE,
        out_shape=jax.ShapeDtypeStruct((LZ, CX, CY), F32),
        scratch_shapes=[
            pltpu.VMEM((CX, CY), F32),
            pltpu.VMEM((LZ, CX, CY), F32),
            pltpu.SemaphoreType.DMA((GROUPS,)),
        ],
        name="finish",
        compiler_params=params(8),
        cost_estimate=pl.CostEstimate(flops=3_000_000, bytes_accessed=2_700_000, transcendentals=0),
    )(near(inbox), near(part))


def swapped_y(one, two):
    count = lax.axis_size("gy")
    pairs = [(i, i ^ 1) for i in range(count)]
    others = [((i + 1) % count, ((i ^ 1) + 1) % count) for i in range(count)]
    return lax.ppermute(one, "gy", pairs), lax.ppermute(two, "gy", others)


def swapped_x(one, two):
    count, rows = lax.axis_size("gx"), lax.axis_size("gy")
    pairs = [(i, i ^ 1) for i in range(count)]
    others = []
    for i in range(count):
        for j in range(rows):
            to = (i, j ^ 1) if i in (0, count - 1) else (((i - 1) ^ 1) + 1, j)
            others.append((i * rows + j, to[0] * rows + to[1]))
    return lax.ppermute(one, "gx", pairs), lax.ppermute(two, ("gx", "gy"), others)


def exchange(cells):
    return lax.all_to_all(cells, "gx", split_axis=0, concat_axis=0, tiled=True)


def body(theta, wind_u, wind_v, level_set, fuel_load, spread_base, tile_owner, tile_place):
    peers = lax.axis_size("gx")
    owners, places = tile_owner[0, 0], tile_place[0, 0]
    requests, head, block = make_requests(owners, places, theta, wind_u, wind_v, peers)
    asked = exchange(requests)

    one_x, two_x, one_y, two_y = make_edges(head, block, theta)
    rims_y = swapped_y(one_y, two_y)

    patches, one_x, two_x = cut_patches(asked, block, *rims_y, one_x, two_x)
    winds = exchange(patches)
    rims_x = swapped_x(one_x, two_x)

    tiles_near = prepare_tiles(patches, level_set[0, 0], fuel_load[0, 0], spread_base[0, 0])
    level_out, fuel_out, outbox = fire(owners, places, winds, tiles_near, peers, ())
    outbox = pass_on(outbox, *rims_x)
    part = advect(theta, wind_u, wind_v, *rims_x, *rims_y)
    inbox = exchange(outbox)
    theta_next = finish(inbox, part)
    return (theta_next, level_out[None, None], fuel_out[None, None])


def solution(mesh):
    in_specs = (
        P(None, "gx", "gy"),
        P(None, "gx", "gy"),
        P(None, "gx", "gy"),
        P("gx", "gy", None, None, None),
        P("gx", "gy", None, None, None),
        P("gx", "gy", None, None, None),
        P("gx", "gy", None),
        P("gx", "gy", None),
    )
    out_specs = (
        P(None, "gx", "gy"),
        P("gx", "gy", None, None, None),
        P("gx", "gy", None, None, None),
    )
    return jax.shard_map(body, mesh=mesh, in_specs=in_specs, out_specs=out_specs, check_vma=False)
```
